32 devices in a mesh: ctx: 16 (over z, y, core), head: 2 (over x).
Axes of the slice: x: 2, y: 2, z: 4, core: 2. Of those that a mesh axis runs over, the one named last changes fastest.
Arguments:
- queries: bfloat16 [8192, 2048], P('ctx', 'head'), may hold values from -13 to 13, as said below
- keys: bfloat16 [8192, 512], P('ctx', 'head'), may hold values from -13 to 13
- values: bfloat16 [8192, 512], P('ctx', 'head'), may hold values from -24 to 24
- positions: int32 [8192], P('ctx'), may hold values from 0 to 4095, as said below
- out_weight: bfloat16 [2048, 4096], P(None, 'head'), may hold values from -0.125 to 0.125
Outputs:
- mixed: bfloat16 [8192, 4096], P('ctx', 'head')
The draws below stay inside these ranges and needn't reach their ends.
Inputs may be any that keep to these rules, and one draw needn't show every extreme that they name: queries, keys: every entry lies in the stated range. positions[r] is 0 where the token at sequence position g(r) begins a document and one more than the position of the token at g(r) - 1 otherwise; documents begin at sequence positions 0 and 4096 and possibly elsewhere in the first half; the second half is one document.
All inputs are finite; a program needn't handle non-finite values.
Results may differ from the reference program's by a relative error of at most 0.012.
The reference program's roundings to bfloat16 on the way count: a program that leaves them out, or rounds other values in their place, can miss the bound.
Values may be sent and summed in bfloat16 or wider, within the bound.
No kernel may reach another device: no remote copies, remote signals or barrier semaphores. Data moves between devices by JAX's collectives and lax.ppermute only.
A program may use at most 128 MiB of HBM per device.

```python
import math
import jax
import jax.numpy as jnp
import numpy as np
from jax import lax

D = 4096
QUERY_HEADS = 16
KEY_VALUE_HEADS = 4
HEAD_SIZE = 128
STEPS = 4
BLOCK_TOKENS = 512
SPAN = 256
RANKS = 16
PROMPT_TOKENS = 8192


def draw_queries(key, part):
    tensor_shape = (PROMPT_TOKENS, QUERY_HEADS * HEAD_SIZE)
    base_offset = 1.5 * jax.random.normal(jax.random.fold_in(key, 1), tensor_shape, jnp.float32)
    return jnp.clip(base_offset, -9.0, 9.0).astype(jnp.bfloat16)


def draw_keys(key, part):
    tensor_shape = (PROMPT_TOKENS, KEY_VALUE_HEADS * HEAD_SIZE)
    base_offset = jax.random.normal(jax.random.fold_in(key, 2), tensor_shape, jnp.float32)
    return jnp.clip(base_offset, -6.0, 6.0).astype(jnp.bfloat16)


def draw_positions(key, part):
    order = jnp.arange(PROMPT_TOKENS, dtype=jnp.int32)
    halfway = PROMPT_TOKENS // 2
    flags = jax.random.randint(jax.random.fold_in(key, 3), (PROMPT_TOKENS,), 0, max(PROMPT_TOKENS // 3, 2)) == 0
    flags = flags & (order < halfway) | (order == 0) | (order == halfway)
    begins = lax.cummax(jnp.where(flags, order, 0).astype(jnp.int32), axis=0)
    natural = (order - begins).astype(jnp.int32)
    block_of = order // BLOCK_TOKENS
    offset = order % BLOCK_TOKENS
    sequence_at = jnp.where(offset < SPAN, block_of * SPAN + offset, (2 * RANKS - 1 - block_of) * SPAN + offset - SPAN).astype(jnp.int32)
    return jnp.take(natural, sequence_at, axis=0).astype(jnp.int32)


def steps_of(own_key, extent, pieces, low, top_value):
    loudness = 1.0
    for axis_at, parts in pieces:
        steps = jax.random.uniform(jax.random.fold_in(jax.random.fold_in(own_key, 6), axis_at), (parts,), jnp.float32, low / len(pieces), top_value / len(pieces))
        loudness = loudness * jnp.repeat(jnp.exp(steps), extent[axis_at] // parts).reshape((-1,) + (1,) * (len(extent) - 1 - axis_at))
    return loudness


def gaussian(key, shape, scale, bound, pieces=(), kind=jnp.bfloat16):
    loudness = steps_of(key, shape, pieces, -0.22, 0.18) if pieces else 1.0
    entries = jax.random.normal(key, shape, jnp.float32) * scale * loudness
    return jnp.minimum(jnp.maximum(entries, -bound), bound).astype(kind)


def setup_inputs(seed: int = 0) -> dict:
    key_list = jax.random.split(jax.random.key(seed), 6)
    return {
        "queries": draw_queries(jax.random.fold_in(key_list[5], 71), 0),
        "keys": draw_keys(jax.random.fold_in(key_list[5], 71), 0),
        "values": gaussian(key_list[2], (PROMPT_TOKENS, KEY_VALUE_HEADS * HEAD_SIZE), 4.0, 24.0, ((0, 16), (1, 2))),
        "positions": draw_positions(jax.random.fold_in(key_list[5], 71), 0),
        "out_weight": gaussian(key_list[4], (QUERY_HEADS * HEAD_SIZE, D), (QUERY_HEADS * HEAD_SIZE) ** -0.5, 0.125, ((1, 2),)),
    }


neg_large = -1e+30

def rotate(block, positions, width):
    halfway = width // 2
    table = np.power(500000.0, -2.0 * np.arange(halfway) / width).astype(np.float32)
    angle = positions.astype(jnp.float32)[:, None] * jnp.asarray(table, dtype=jnp.float32)[None, :]
    cosine = jnp.cos(angle)[:, None, :]
    sinus = jnp.sin(angle)[:, None, :]
    number = block.shape[0]
    groups = block.shape[1] // width
    split_up = block.astype(jnp.float32).reshape(number, groups, width)
    leading = split_up[:, :, :halfway]
    trailing = split_up[:, :, halfway:]
    turned = jnp.concatenate([leading * cosine - trailing * sinus, trailing * cosine + leading * sinus], axis=2)
    return turned.reshape(number, groups * width).astype(jnp.bfloat16)

def reference(queries, keys, values, positions, out_weight):
    within = jnp.arange(PROMPT_TOKENS, dtype=jnp.int32)
    block_of = within // BLOCK_TOKENS
    offset = within % BLOCK_TOKENS
    index_of = jnp.where(offset < SPAN, block_of * SPAN + offset, (2 * RANKS - 1 - block_of) * SPAN + offset - SPAN).astype(jnp.int32)
    doc_start = (index_of - positions).astype(jnp.int32)
    q_rot = rotate(queries, positions, HEAD_SIZE)
    rotary_keys = rotate(keys, positions, HEAD_SIZE)
    query_group = QUERY_HEADS // KEY_VALUE_HEADS
    scale = 1.0 / math.sqrt(HEAD_SIZE)

    def one_block(number):
        first_row = (number * BLOCK_TOKENS).astype(jnp.int32)
        query_row_slice = lax.dynamic_slice_in_dim(q_rot, first_row, BLOCK_TOKENS, 0)
        query_index = lax.dynamic_slice_in_dim(index_of, first_row, BLOCK_TOKENS, 0)
        query_start = lax.dynamic_slice_in_dim(doc_start, first_row, BLOCK_TOKENS, 0)
        sources = ((number - jnp.arange(STEPS, dtype=jnp.int32)) % RANKS).astype(jnp.int32)
        key_row_slice = (sources[:, None] * BLOCK_TOKENS + jnp.arange(BLOCK_TOKENS, dtype=jnp.int32)[None, :]).reshape(-1)
        key_tile_block = jnp.take(rotary_keys, key_row_slice, axis=0).astype(jnp.float32).reshape(-1, KEY_VALUE_HEADS, HEAD_SIZE)
        value_tile_block = jnp.take(values, key_row_slice, axis=0).astype(jnp.float32).reshape(-1, KEY_VALUE_HEADS, HEAD_SIZE)
        key_index = jnp.take(index_of, key_row_slice, axis=0)
        query_float_rows = query_row_slice.astype(jnp.float32).reshape(BLOCK_TOKENS, KEY_VALUE_HEADS, query_group, HEAD_SIZE)
        scores = jnp.einsum('qhgd,khd->hgqk', query_float_rows, key_tile_block, precision=lax.Precision.HIGHEST) * scale
        allowed = (key_index[None, :] <= query_index[:, None]) & (key_index[None, :] >= query_start[:, None])
        scores = jnp.where(allowed, scores, neg_large)
        highest = lax.optimization_barrier(jnp.max(scores, axis=3, keepdims=True))
        weights = jnp.where(allowed, jnp.exp(scores - highest), 0.0)
        total = lax.optimization_barrier(jnp.sum(weights, axis=3))
        rounded = lax.optimization_barrier(weights.astype(jnp.bfloat16)).astype(jnp.float32)
        summed = jnp.einsum('hgqk,khd->qhgd', rounded, value_tile_block, precision=lax.Precision.HIGHEST)
        result = summed / jnp.transpose(total, (2, 0, 1))[..., None]
        return result.reshape(BLOCK_TOKENS, QUERY_HEADS * HEAD_SIZE).astype(jnp.bfloat16)
    attended = lax.map(one_block, jnp.arange(RANKS, dtype=jnp.int32)).reshape(PROMPT_TOKENS, QUERY_HEADS * HEAD_SIZE)
    return jnp.dot(attended, out_weight, preferred_element_type=jnp.float32).astype(jnp.bfloat16)
```

```python
import functools
import math

import jax
import jax.numpy as jnp
import numpy as np
from jax import lax
from jax.experimental import pallas as pl
from jax.experimental.pallas import tpu as pltpu
from jax.sharding import PartitionSpec as P

HEAD_SIZE = 128
LOWEST = -1e30
FAR = 1 << 16
MIB = 1 << 20
SCORE_SCALE = math.log2(math.e) / math.sqrt(HEAD_SIZE)
BF16, F32 = jnp.bfloat16, jnp.float32


def distance(rank, step, count):
    return jnp.where(rank >= step, step, count - step)


def waits_for_keys(rank):
    return (rank == 1) | (rank == 2)


def first_begin(rank, half):
    return pl.multiple_of(jnp.where(rank < 2, 0, half), half)


def half_positions(p_ref, rank, first):
    half = p_ref.shape[1] // 2
    early = (rank < 2) if first else (rank >= 2)
    return jnp.where(early, p_ref[:, :half], p_ref[:, half:])


def column(row, width):
    return jnp.broadcast_to(row, (width, row.shape[1])).T


def tile_biases(position_row, kinds):
    number = position_row.shape[1]
    position = column(position_row, number)
    query = lax.broadcasted_iota(jnp.int32, (number, number), 0)
    key = lax.broadcasted_iota(jnp.int32, (number, number), 1)
    ahead = key - query
    reach = ahead + position
    found = []
    for pieces, diagonal in kinds:
        allowed = reach >= pieces * number
        if diagonal:
            allowed = allowed & (ahead <= 0)
        found.append(jnp.where(allowed, 0.0, LOWEST).astype(F32))
    return found


def sine_cosine(angle):
    turns = jnp.floor(angle * (2.0 / math.pi) + 0.5)
    rest = ((angle - turns * 1.5703125) - turns * 4.837512969970703e-4) - turns * 7.549789954891888e-8
    square = rest * rest
    sine = ((-1.9515295891e-4 * square + 8.3321608736e-3) * square - 1.6666654611e-1) * square * rest + rest
    cosine = (
        ((2.443315711809948e-5 * square - 1.388731625493765e-3) * square + 4.166664568298827e-2) * square * square
        - 0.5 * square
        + 1.0
    )
    quarter = turns.astype(jnp.int32)
    swap = (quarter & 1) == 1
    out_sine = jnp.where(swap, cosine, sine)
    out_cosine = jnp.where(swap, sine, cosine)
    out_sine = jnp.where((quarter & 2) == 2, -out_sine, out_sine)
    out_cosine = jnp.where(((quarter + 1) & 2) == 2, -out_cosine, out_cosine)
    return out_sine, out_cosine


def turned(block, cosine, sinus):
    wide = block.astype(F32)
    return (wide * cosine + pltpu.roll(wide, HEAD_SIZE // 2, 1) * sinus).astype(BF16)


def scores_of(query, key, bias):
    raw = lax.dot_general(query, key, (((1,), (1,)), ((), ())), preferred_element_type=F32)
    return raw * SCORE_SCALE + bias


def weighted(weights, value):
    return jnp.dot(weights.astype(BF16), value, preferred_element_type=F32)


def spread(entries):
    return jnp.broadcast_to(entries, (entries.shape[0], HEAD_SIZE))


def head_slices(head, group, width):
    at = slice(head * HEAD_SIZE, (head + 1) * HEAD_SIZE)
    low = head // group * HEAD_SIZE
    return at, slice(low, low + HEAD_SIZE), slice(width + low, width + low + HEAD_SIZE)


def begin_state(query, keys, values, biases):
    scores = [scores_of(query, key, bias) for key, bias in zip(keys, biases)]
    top = jnp.max(functools.reduce(jnp.maximum, scores), axis=1, keepdims=True)
    weights = [jnp.exp2(score - top) for score in scores]
    total = jnp.sum(functools.reduce(jnp.add, weights), axis=1, keepdims=True)
    summed = functools.reduce(jnp.add, [weighted(w, value) for w, value in zip(weights, values)])
    return summed, spread(top), spread(total)


def finish_state(summed, top, total, query, keys, values, biases):
    scores = [scores_of(query, key, bias) for key, bias in zip(keys, biases)]
    largest = spread(jnp.max(functools.reduce(jnp.maximum, scores), axis=1, keepdims=True))
    updated = jnp.maximum(top, largest)
    wide = jnp.concatenate([updated] * (scores[0].shape[1] // HEAD_SIZE), axis=1)
    weights = [jnp.exp2(score - wide) for score in scores]
    factor = jnp.exp2(top - updated)
    total = total * factor + spread(jnp.sum(functools.reduce(jnp.add, weights), axis=1, keepdims=True))
    added = functools.reduce(jnp.add, [weighted(w, value) for w, value in zip(weights, values)])
    return ((summed * factor + added) * (1.0 / total)).astype(BF16)


def keys_kernel(
    count, k_hbm, v_hbm, q_hbm, p_hbm, f_hbm, near_ref, next_ref, rot_ref, v_ref, q_ref, p_ref, cos_ref, sin_ref, k_ref, f_ref, sems
):
    pairs = ((p_hbm, p_ref), (f_hbm, f_ref), (k_hbm, k_ref), (v_hbm, v_ref), (q_hbm, q_ref))
    copies = [pltpu.make_async_copy(source, target, sems.at[i]) for i, (source, target) in enumerate(pairs)]
    for copy in copies:
        copy.start()
    rank = lax.axis_index("ctx")
    half = k_ref.shape[0] // 2
    width = k_ref.shape[1]
    copies[0].wait()
    copies[1].wait()
    position = p_ref[...].astype(F32)
    early = column(position[:, :half], HEAD_SIZE)
    late = column(position[:, half:], HEAD_SIZE)
    lane = lax.broadcasted_iota(jnp.int32, (half, HEAD_SIZE), 1)
    front = lane < HEAD_SIZE // 2
    sine, cosine = sine_cosine(jnp.where(front, early, late) * f_ref[...])
    sine_other = pltpu.roll(sine, HEAD_SIZE // 2, 1)
    cosine_other = pltpu.roll(cosine, HEAD_SIZE // 2, 1)
    cos_ref[:half] = jnp.where(front, cosine, cosine_other)
    cos_ref[half:] = jnp.where(front, cosine_other, cosine)
    sin_ref[:half] = jnp.where(front, -sine, sine_other)
    sin_ref[half:] = jnp.where(front, -sine_other, sine)
    copies[2].wait()
    for head in range(width // HEAD_SIZE):
        at = slice(head * HEAD_SIZE, (head + 1) * HEAD_SIZE)
        rot_ref[:, at] = turned(k_ref[:, at], cos_ref[...], sin_ref[...])
    copies[3].wait()
    wraps = ((rank % 2 == 1) & (rank + 3 >= count), rank + 2 >= count)
    for wrap, send_ref in zip(wraps, (near_ref, next_ref)):
        rows = pl.ds(pl.multiple_of(jnp.where(wrap, half, 0), half), half)
        send_ref[:, :width] = rot_ref[rows, :]
        send_ref[:, width:] = v_ref[rows, :]
    copies[4].wait()


def own_kernel(group, q_ref, k_ref, v_ref, p_ref, cos_ref, sin_ref, out_ref, rot_ref, acc_ref, top_ref, sum_ref):
    rank = lax.axis_index("ctx")
    half = q_ref.shape[0] // 2
    rows = pl.ds(first_begin(rank, half), half)
    biases = tile_biases(half_positions(p_ref, rank, True), [(0, True)])
    for head in range(q_ref.shape[1] // HEAD_SIZE):
        at, shared, _ = head_slices(head, group, 0)
        query = turned(q_ref[rows, at], cos_ref[rows, :], sin_ref[rows, :])
        rot_ref[:, at] = query
        summed, top, total = begin_state(query, [k_ref[rows, shared]], [v_ref[rows, shared]], biases)
        acc_ref[:, at] = summed
        top_ref[:, at] = top
        sum_ref[:, at] = total
        out_ref[:, at] = (summed * (1.0 / total)).astype(BF16)


def first_kernel(count, group, rot_ref, kv_ref, p_ref, acc_ref, top_ref, sum_ref, out_ref):
    rank = lax.axis_index("ctx")
    width = kv_ref.shape[1] // 2
    step = jnp.where(rank % 2 == 1, 1, 3)
    used = waits_for_keys(rank)

    @pl.when(used)
    def _():
        biases = tile_biases(half_positions(p_ref, rank, True), [(distance(rank, step, count), False)])
        for head in range(rot_ref.shape[1] // HEAD_SIZE):
            at, key_at, value_at = head_slices(head, group, width)
            out_ref[:, at] = finish_state(
                acc_ref[:, at], top_ref[:, at], sum_ref[:, at], rot_ref[:, at], [kv_ref[:, key_at]], [kv_ref[:, value_at]], biases
            )

    @pl.when(jnp.logical_not(used))
    def _():
        out_ref[...] = jnp.zeros_like(out_ref)


def second_kernel(
    count, group, q_ref, k_ref, v_ref, p_ref, cos_ref, sin_ref, kv_ref, w_hbm, rot_ref, acc_ref, top_ref, sum_ref, w_ref, sem
):
    copy = pltpu.make_async_copy(w_hbm, w_ref, sem)
    copy.start()
    rank = lax.axis_index("ctx")
    half = q_ref.shape[0] // 2
    width = k_ref.shape[1]
    rows = pl.ds(pl.multiple_of(half - first_begin(rank, half), half), half)
    step = jnp.where(rank % 2 == 1, 1, 3)
    reach = jnp.where(waits_for_keys(rank), FAR, distance(rank, step, count))
    biases = tile_biases(half_positions(p_ref, rank, False), [(0, True), (reach, False)])
    for head in range(q_ref.shape[1] // HEAD_SIZE):
        at, key_at, value_at = head_slices(head, group, width)
        query = turned(q_ref[rows, at], cos_ref[rows, :], sin_ref[rows, :])
        rot_ref[:, at] = query
        keys = [k_ref[rows, key_at], kv_ref[:, key_at]]
        values = [v_ref[rows, key_at], kv_ref[:, value_at]]
        acc_ref[:, at], top_ref[:, at], sum_ref[:, at] = begin_state(query, keys, values, biases)
    copy.wait()


def third_kernel(count, group, begin, rot_ref, kv0_ref, kv1_ref, p_ref, acc_ref, top_ref, sum_ref, out_ref):
    rank = lax.axis_index("ctx")
    width = kv0_ref.shape[1] // 2
    step = jnp.where(rank % 2 == 1, 3, 1)
    kinds = [(distance(rank, 2, count), False), (distance(rank, step, count), False)]
    biases = tile_biases(half_positions(p_ref, rank, False), kinds)
    for head in range(out_ref.shape[1] // HEAD_SIZE):
        at, key_at, value_at = head_slices(begin + head, group, width)
        out_ref[:, head * HEAD_SIZE : (head + 1) * HEAD_SIZE] = finish_state(
            acc_ref[:, at],
            top_ref[:, at],
            sum_ref[:, at],
            rot_ref[:, at],
            [kv0_ref[:, key_at], kv1_ref[:, key_at]],
            [kv0_ref[:, value_at], kv1_ref[:, value_at]],
            biases,
        )


def dot(left, right):
    return jnp.dot(left, right, preferred_element_type=F32)


TILE = 512


def project_kernel(own_ref, late_ref, got_ref, got_late_ref, *rest):
    seconds, (w_ref, out_hbm, part_ref, held_ref, sems) = rest[:-5], rest[-5:]
    rank = lax.axis_index("ctx")
    side = lax.axis_index("head")
    half, depth = own_ref.shape
    rows = pl.ds(first_begin(rank, half), half)
    mine = pl.ds(pl.multiple_of(side * depth, depth), depth)
    other = pl.ds(pl.multiple_of((1 - side) * depth, depth), depth)
    late = waits_for_keys(rank)
    own = jnp.where(late, late_ref[...], own_ref[...])
    got = jnp.where(late, got_late_ref[...], got_ref[...])
    stacked = jnp.concatenate([own, jnp.concatenate([ref[...] for ref in seconds], axis=1)], axis=0)
    copies = []
    for tile in range(w_ref.shape[1] // TILE):
        at = slice(tile * TILE, (tile + 1) * TILE)
        both = dot(stacked, w_ref[mine, at])
        part_ref[:, at] = both[half:]
        held_ref[:, at] = (both[:half] + dot(got, w_ref[other, at])).astype(BF16)
        copies.append(pltpu.make_async_copy(held_ref.at[:, at], out_hbm.at[rows, at], sems.at[tile]))
        copies[-1].start()
    for copy in copies:
        copy.wait()


def add_kernel(got_ref, part_ref, w_ref, out_ref):
    side = lax.axis_index("head")
    depth = got_ref.shape[1]
    rows = pl.ds(pl.multiple_of((1 - side) * (w_ref.shape[0] // 2), depth), depth)
    for tile in range(w_ref.shape[1] // TILE):
        at = slice(tile * TILE, (tile + 1) * TILE)
        out_ref[:, at] = part_ref[:, at] + dot(got_ref[...], w_ref[rows, at])


def last_kernel(got_ref, part_ref, w_ref, begun_hbm, out_hbm, held_ref, sems):
    del begun_hbm
    rank = lax.axis_index("ctx")
    side = lax.axis_index("head")
    half, depth = got_ref.shape
    rows = pl.ds(pl.multiple_of((1 - side) * (w_ref.shape[0] // 2) + w_ref.shape[0] // 2 - depth, depth), depth)
    out_rows = pl.ds(pl.multiple_of(half - first_begin(rank, half), half), half)
    copies = []
    for tile in range(w_ref.shape[1] // TILE):
        at = slice(tile * TILE, (tile + 1) * TILE)
        held_ref[:, at] = (part_ref[:, at] + dot(got_ref[...], w_ref[rows, at])).astype(BF16)
        copies.append(pltpu.make_async_copy(held_ref.at[:, at], out_hbm.at[out_rows, at], sems.at[tile]))
        copies[-1].start()
    for copy in copies:
        copy.wait()


def shards(queries, keys, values, positions, out_weight):
    number, width = queries.shape
    half = number // 2
    count = lax.axis_size("ctx")
    group = width // keys.shape[1]
    heads = width // HEAD_SIZE
    columns = out_weight.shape[1]
    tiles = columns // TILE
    in_hbm = lambda array: pltpu.with_memory_space_constraint(array, pltpu.HBM)
    position_row = positions.reshape(1, number)
    table = np.power(500000.0, -2.0 * np.arange(HEAD_SIZE // 2) / HEAD_SIZE).astype(np.float32)
    frequency = jnp.asarray(np.concatenate([table, table])[None, :])
    shape = jax.ShapeDtypeStruct
    vmem = pl.BlockSpec(memory_space=pltpu.VMEM)
    hbm = pl.BlockSpec(memory_space=pltpu.HBM)
    dma = pltpu.SemaphoreType.DMA

    def call(body, name, ins, outs, flops, nbytes, out_specs=None, scratch=(), aliases={}):
        return pl.pallas_call(
            body,
            name=name,
            in_specs=ins,
            out_shape=outs,
            out_specs=out_specs if out_specs is not None else jax.tree.map(lambda _: vmem, outs),
            scratch_shapes=scratch,
            input_output_aliases=aliases,
            compiler_params=pltpu.CompilerParams(vmem_limit_bytes=32 * MIB),
            cost_estimate=pl.CostEstimate(flops=flops, bytes_accessed=nbytes, transcendentals=0),
        )

    def pairs(target_of):
        found = [(source, target_of(source) % count) for source in range(count)]
        assert sorted(target for _, target in found) == list(range(count))
        return found

    kv_shape = shape((half, 2 * keys.shape[1]), BF16)
    table_shape = shape((number, HEAD_SIZE), F32)
    rows_shape, state = shape((half, width), BF16), shape((half, width), F32)
    near, onward, k_rot, v, q, p, cosine, sinus = call(
        functools.partial(keys_kernel, count),
        "rotate_keys",
        [hbm] * 5,
        [
            kv_shape,
            kv_shape,
            shape(keys.shape, BF16),
            shape(keys.shape, BF16),
            shape(queries.shape, BF16),
            shape((1, number), jnp.int32),
            table_shape,
            table_shape,
        ],
        4 * MIB,
        4 * MIB,
        scratch=[pltpu.VMEM(keys.shape, BF16), pltpu.VMEM((1, HEAD_SIZE), F32), dma((5,))],
    )(*(in_hbm(array) for array in (keys, values, queries, position_row, frequency)))
    near_got = lax.ppermute(near, "ctx", pairs(lambda r: r + 3 if r % 2 else r + 1))
    next_got = lax.ppermute(onward, "ctx", pairs(lambda r: r + 2))
    own, rot, acc, top, total = call(
        functools.partial(own_kernel, group),
        "own_tiles",
        [vmem] * 6,
        [rows_shape, rows_shape, state, state, state],
        256 * MIB,
        4 * MIB,
    )(q, k_rot, v, p, cosine, sinus)

    def swapped(array, blocks):
        flat = [(2 * b + s, 2 * b + 1 - s) for b in range(count) if b in blocks for s in (0, 1)]
        return lax.ppermute(array, ("ctx", "head"), flat)

    got = swapped(own, [b for b in range(count) if b not in (1, 2)])
    late = call(
        functools.partial(first_kernel, count, group), "first_rows", [vmem] * 6, rows_shape, 256 * MIB, 4 * MIB
    )(rot, near_got, p, acc, top, total)
    got_late = swapped(late, [1, 2])
    rot, acc, top, total, w = call(
        functools.partial(second_kernel, count, group),
        "second_rows",
        [vmem] * 7 + [hbm],
        [rows_shape, state, state, state, shape(out_weight.shape, BF16)],
        1024 * MIB,
        12 * MIB,
        scratch=[dma(())],
    )(q, k_rot, v, p, cosine, sinus, near_got, in_hbm(out_weight))
    last_got = lax.ppermute(next_got, "ctx", pairs(lambda r: r + 1 - 2 * (r % 2)))
    seconds, seconds_got = [], []
    for begin in (0, heads // 2):
        seconds.append(
            call(
                functools.partial(third_kernel, count, group, begin),
                "third_rows",
                [vmem] * 7,
                shape((half, width // 2), BF16),
                512 * MIB,
                4 * MIB,
            )(rot, next_got, last_got, p, acc, top, total)
        )
        seconds_got.append(swapped(seconds[-1], range(count)))
        rot, seconds[-1] = lax.optimization_barrier((rot, seconds[-1]))
    begun, part = call(
        project_kernel,
        "project_first",
        [vmem] * 7,
        [shape((number, columns), BF16), shape((half, columns), F32)],
        3072 * MIB,
        8 * MIB,
        out_specs=[hbm, vmem],
        scratch=[pltpu.VMEM((half, columns), BF16), dma((tiles,))],
    )(own, late, got, got_late, *seconds, w)
    part = call(
        add_kernel, "project_second", [vmem] * 3, shape((half, columns), F32), 512 * MIB, 4 * MIB
    )(seconds_got[0], part, w)
    return call(
        last_kernel,
        "project_last",
        [vmem] * 3 + [hbm],
        shape((number, columns), BF16),
        512 * MIB,
        4 * MIB,
        out_specs=hbm,
        scratch=[pltpu.VMEM((half, columns), BF16), dma((tiles,))],
        aliases={3: 0},
    )(seconds_got[1], part, w, begun)


def solution(mesh):
    in_specs = (P("ctx", "head"), P("ctx", "head"), P("ctx", "head"), P("ctx"), P(None, "head"))
    out_specs = P("ctx", "head")
    return jax.shard_map(shards, mesh=mesh, in_specs=in_specs, out_specs=out_specs, check_vma=False)
```

```python
import functools
import math

import jax
import jax.numpy as jnp
import numpy as np
from jax import lax
from jax.experimental import pallas as pl
from jax.experimental.pallas import tpu as pltpu
from jax.sharding import PartitionSpec as P

HEAD_SIZE = 128
LOWEST = -1e30
FAR = 1 << 16
MIB = 1 << 20
SCORE_SCALE = math.log2(math.e) / math.sqrt(HEAD_SIZE)
BF16, F32 = jnp.bfloat16, jnp.float32


def distance(rank, step, count):
    return jnp.where(rank >= step, step, count - step)


def waits_for_keys(rank):
    return (rank == 1) | (rank == 2)


def first_begin(rank, half):
    return pl.multiple_of(jnp.where(rank < 2, 0, half), half)


def half_positions(p_ref, rank, first):
    half = p_ref.shape[1] // 2
    early = (rank < 2) if first else (rank >= 2)
    return jnp.where(early, p_ref[:, :half], p_ref[:, half:])


def column(row, width):
    return jnp.broadcast_to(row, (width, row.shape[1])).T


def tile_biases(position_row, kinds):
    number = position_row.shape[1]
    position = column(position_row, number)
    query = lax.broadcasted_iota(jnp.int32, (number, number), 0)
    key = lax.broadcasted_iota(jnp.int32, (number, number), 1)
    ahead = key - query
    reach = ahead + position
    found = []
    for pieces, diagonal in kinds:
        allowed = reach >= pieces * number
        if diagonal:
            allowed = allowed & (ahead <= 0)
        found.append(jnp.where(allowed, 0.0, LOWEST).astype(F32))
    return found


def sine_cosine(angle):
    turns = jnp.floor(angle * (2.0 / math.pi) + 0.5)
    rest = ((angle - turns * 1.5703125) - turns * 4.837512969970703e-4) - turns * 7.549789954891888e-8
    square = rest * rest
    sine = ((-1.9515295891e-4 * square + 8.3321608736e-3) * square - 1.6666654611e-1) * square * rest + rest
    cosine = (
        ((2.443315711809948e-5 * square - 1.388731625493765e-3) * square + 4.166664568298827e-2) * square * square
        - 0.5 * square
        + 1.0
    )
    quarter = turns.astype(jnp.int32)
    swap = (quarter & 1) == 1
    out_sine = jnp.where(swap, cosine, sine)
    out_cosine = jnp.where(swap, sine, cosine)
    out_sine = jnp.where((quarter & 2) == 2, -out_sine, out_sine)
    out_cosine = jnp.where(((quarter + 1) & 2) == 2, -out_cosine, out_cosine)
    return out_sine, out_cosine


def turned(block, cosine, sinus):
    wide = block.astype(F32)
    return (wide * cosine + pltpu.roll(wide, HEAD_SIZE // 2, 1) * sinus).astype(BF16)


def scores_of(query, key, bias):
    raw = lax.dot_general(query, key, (((1,), (1,)), ((), ())), preferred_element_type=F32)
    return raw * SCORE_SCALE + bias


def weighted(weights, value):
    return jnp.dot(weights.astype(BF16), value, preferred_element_type=F32)


def spread(entries):
    return jnp.broadcast_to(entries, (entries.shape[0], HEAD_SIZE))


def head_slices(head, group, width):
    at = slice(head * HEAD_SIZE, (head + 1) * HEAD_SIZE)
    low = head // group * HEAD_SIZE
    return at, slice(low, low + HEAD_SIZE), slice(width + low, width + low + HEAD_SIZE)


def begin_state(query, keys, values, biases):
    scores = [scores_of(query, key, bias) for key, bias in zip(keys, biases)]
    top = jnp.max(functools.reduce(jnp.maximum, scores), axis=1, keepdims=True)
    weights = [jnp.exp2(score - top) for score in scores]
    total = jnp.sum(functools.reduce(jnp.add, weights), axis=1, keepdims=True)
    summed = functools.reduce(jnp.add, [weighted(w, value) for w, value in zip(weights, values)])
    return summed, spread(top), spread(total)


def added_tile(summed, top, total, query, key, value, bias):
    score = scores_of(query, key, bias)
    updated = jnp.maximum(top, spread(jnp.max(score, axis=1, keepdims=True)))
    weights = jnp.exp2(score - jnp.concatenate([updated] * (score.shape[1] // HEAD_SIZE), axis=1))
    factor = jnp.exp2(top - updated)
    total = total * factor + spread(jnp.sum(weights, axis=1, keepdims=True))
    return summed * factor + weighted(weights, value), updated, total


def finished(state):
    summed, _, total = state
    return (summed * (1.0 / total)).astype(BF16)


def keys_kernel(
    count, k_hbm, v_hbm, q_hbm, p_hbm, f_hbm, near_ref, next_ref, rot_ref, v_ref, q_ref, p_ref, cos_ref, sin_ref,
    k_ref, f_ref, sems,
):
    pairs = ((p_hbm, p_ref), (f_hbm, f_ref), (k_hbm, k_ref), (v_hbm, v_ref), (q_hbm, q_ref))
    copies = [pltpu.make_async_copy(source, target, sems.at[i]) for i, (source, target) in enumerate(pairs)]
    for copy in copies:
        copy.start()
    rank = lax.axis_index("ctx")
    half = k_ref.shape[0] // 2
    width = k_ref.shape[1]
    copies[0].wait()
    copies[1].wait()
    position = p_ref[...].astype(F32)
    early = column(position[:, :half], HEAD_SIZE)
    late = column(position[:, half:], HEAD_SIZE)
    lane = lax.broadcasted_iota(jnp.int32, (half, HEAD_SIZE), 1)
    front = lane < HEAD_SIZE // 2
    sine, cosine = sine_cosine(jnp.where(front, early, late) * f_ref[...])
    sine_other = pltpu.roll(sine, HEAD_SIZE // 2, 1)
    cosine_other = pltpu.roll(cosine, HEAD_SIZE // 2, 1)
    cos_ref[:half] = jnp.where(front, cosine, cosine_other)
    cos_ref[half:] = jnp.where(front, cosine_other, cosine)
    sin_ref[:half] = jnp.where(front, -sine, sine_other)
    sin_ref[half:] = jnp.where(front, -sine_other, sine)
    copies[2].wait()
    for head in range(width // HEAD_SIZE):
        at = slice(head * HEAD_SIZE, (head + 1) * HEAD_SIZE)
        rot_ref[:, at] = turned(k_ref[:, at], cos_ref[...], sin_ref[...])
    copies[3].wait()
    wrap = (rank % 2 == 1) & (rank + 3 >= count)
    rows = pl.ds(pl.multiple_of(jnp.where(wrap, half, 0), half), half)
    near_ref[:, :width] = rot_ref[rows, :]
    near_ref[:, width:] = v_ref[rows, :]
    rows = pl.ds(pl.multiple_of(jnp.where(rank + 2 >= count, half, 0), half), half)
    next_ref[:, :width] = rot_ref[rows, :]
    next_ref[:, width:] = v_ref[rows, :]
    copies[4].wait()


def own_kernel(group, q_ref, k_ref, v_ref, p_ref, cos_ref, sin_ref, out_ref, rot_ref, acc_ref, top_ref, sum_ref):
    rank = lax.axis_index("ctx")
    half = q_ref.shape[0] // 2
    rows = pl.ds(first_begin(rank, half), half)
    biases = tile_biases(half_positions(p_ref, rank, True), [(0, True)])
    for head in range(q_ref.shape[1] // HEAD_SIZE):
        at, shared, _ = head_slices(head, group, 0)
        query = turned(q_ref[rows, at], cos_ref[rows, :], sin_ref[rows, :])
        rot_ref[:, at] = query
        summed, top, total = begin_state(query, [k_ref[rows, shared]], [v_ref[rows, shared]], biases)
        acc_ref[:, at] = summed
        top_ref[:, at] = top
        sum_ref[:, at] = total
        out_ref[:, at] = (summed * (1.0 / total)).astype(BF16)


def first_kernel(count, group, own_ref, rot_ref, kv_ref, p_ref, acc_ref, top_ref, sum_ref, out_ref):
    rank = lax.axis_index("ctx")
    width = kv_ref.shape[1] // 2
    step = jnp.where(rank % 2 == 1, 1, 3)
    used = waits_for_keys(rank)

    @pl.when(used)
    def _():
        biases = tile_biases(half_positions(p_ref, rank, True), [(distance(rank, step, count), False)])
        for head in range(rot_ref.shape[1] // HEAD_SIZE):
            at, key_at, value_at = head_slices(head, group, width)
            state = acc_ref[:, at], top_ref[:, at], sum_ref[:, at]
            out_ref[:, at] = finished(added_tile(*state, rot_ref[:, at], kv_ref[:, key_at], kv_ref[:, value_at], *biases))

    @pl.when(jnp.logical_not(used))
    def _():
        out_ref[...] = own_ref[...]


def second_kernel(
    count, group, q_ref, k_ref, v_ref, p_ref, cos_ref, sin_ref, kv_ref, rot_ref, acc_ref, top_ref, sum_ref
):
    rank = lax.axis_index("ctx")
    half = q_ref.shape[0] // 2
    width = k_ref.shape[1]
    rows = pl.ds(pl.multiple_of(half - first_begin(rank, half), half), half)
    step = jnp.where(rank % 2 == 1, 1, 3)
    reach = jnp.where(waits_for_keys(rank), FAR, distance(rank, step, count))
    biases = tile_biases(half_positions(p_ref, rank, False), [(0, True), (reach, False)])
    for head in range(q_ref.shape[1] // HEAD_SIZE):
        at, key_at, value_at = head_slices(head, group, width)
        query = turned(q_ref[rows, at], cos_ref[rows, :], sin_ref[rows, :])
        rot_ref[:, at] = query
        keys = [k_ref[rows, key_at], kv_ref[:, key_at]]
        values = [v_ref[rows, key_at], kv_ref[:, value_at]]
        acc_ref[:, at], top_ref[:, at], sum_ref[:, at] = begin_state(query, keys, values, biases)


def next_kernel(count, group, rot_ref, kv_ref, p_ref, acc_ref, top_ref, sum_ref, *outs):
    rank = lax.axis_index("ctx")
    width = kv_ref.shape[1] // 2
    biases = tile_biases(half_positions(p_ref, rank, False), [(distance(rank, 2, count), False)])
    for head in range(rot_ref.shape[1] // HEAD_SIZE):
        at, key_at, value_at = head_slices(head, group, width)
        state = acc_ref[:, at], top_ref[:, at], sum_ref[:, at]
        state = added_tile(*state, rot_ref[:, at], kv_ref[:, key_at], kv_ref[:, value_at], *biases)
        for out_ref, entries in zip(outs, state):
            out_ref[:, at] = entries


def third_kernel(count, group, part, rot_ref, kv_ref, p_ref, acc_ref, top_ref, sum_ref, out_ref):
    rank = lax.axis_index("ctx")
    width = kv_ref.shape[1] // 2
    step = jnp.where(rank % 2 == 1, 3, 1)
    biases = tile_biases(half_positions(p_ref, rank, False), [(distance(rank, step, count), False)])
    for head in range(group):
        at, key_at, value_at = head_slices(part * group + head, group, width)
        state = acc_ref[:, at], top_ref[:, at], sum_ref[:, at]
        state = added_tile(*state, rot_ref[:, at], kv_ref[:, key_at], kv_ref[:, value_at], *biases)
        out_ref[:, head * HEAD_SIZE : (head + 1) * HEAD_SIZE] = finished(state)


def dot(left, right):
    return jnp.dot(left, right, preferred_element_type=F32)


TILE = 512


def project_kernel(own_ref, got_ref, *rest):
    seconds, (w_hbm, out_hbm, part_ref, other_ref, mine_ref, held_ref, sems) = rest[:-7], rest[-7:]
    rank = lax.axis_index("ctx")
    side = lax.axis_index("head")
    half, depth = own_ref.shape
    rows = pl.ds(first_begin(rank, half), half)
    tiles = [slice(start, start + TILE) for start in range(0, mine_ref.shape[1], TILE)]
    weights = []
    for tile, at in enumerate(tiles):
        for number, (part, ref) in enumerate(((side, mine_ref), (1 - side, other_ref))):
            source = w_hbm.at[pl.ds(pl.multiple_of(part * depth, depth), depth), at]
            weights.append(pltpu.make_async_copy(source, ref.at[:, at], sems.at[number, tile]))
            weights[-1].start()
    stacked = jnp.concatenate([own_ref[...], jnp.concatenate([ref[...] for ref in seconds], axis=1)], axis=0)
    copies = []
    for tile, at in enumerate(tiles):
        weights[2 * tile].wait()
        both = dot(stacked, mine_ref[:, at])
        part_ref[:, at] = both[half:]
        weights[2 * tile + 1].wait()
        held_ref[:, at] = (both[:half] + dot(got_ref[...], other_ref[:, at])).astype(BF16)
        copies.append(pltpu.make_async_copy(held_ref.at[:, at], out_hbm.at[rows, at], sems.at[2, tile]))
        copies[-1].start()
    for copy in copies:
        copy.wait()


def add_kernel(part, got_ref, part_ref, w_ref, out_ref):
    depth = got_ref.shape[1]
    for tile in range(w_ref.shape[1] // TILE):
        at = slice(tile * TILE, (tile + 1) * TILE)
        out_ref[:, at] = part_ref[:, at] + dot(got_ref[...], w_ref[part * depth : (part + 1) * depth, at])


def last_kernel(part, got_ref, part_ref, w_ref, begun_hbm, out_hbm, held_ref, sems):
    del begun_hbm
    rank = lax.axis_index("ctx")
    half, depth = got_ref.shape
    out_rows = pl.ds(pl.multiple_of(half - first_begin(rank, half), half), half)
    copies = []
    for tile in range(w_ref.shape[1] // TILE):
        at = slice(tile * TILE, (tile + 1) * TILE)
        added = dot(got_ref[...], w_ref[part * depth : (part + 1) * depth, at])
        held_ref[:, at] = (part_ref[:, at] + added).astype(BF16)
        copies.append(pltpu.make_async_copy(held_ref.at[:, at], out_hbm.at[out_rows, at], sems.at[tile]))
        copies[-1].start()
    for copy in copies:
        copy.wait()


def shards(queries, keys, values, positions, out_weight):
    number, width = queries.shape
    half = number // 2
    count = lax.axis_size("ctx")
    group = width // keys.shape[1]
    columns = out_weight.shape[1]
    tiles = columns // TILE
    in_hbm = lambda array: pltpu.with_memory_space_constraint(array, pltpu.HBM)
    position_row = positions.reshape(1, number)
    table = np.power(500000.0, -2.0 * np.arange(HEAD_SIZE // 2) / HEAD_SIZE).astype(np.float32)
    frequency = jnp.asarray(np.concatenate([table, table])[None, :])
    shape = jax.ShapeDtypeStruct
    vmem = pl.BlockSpec(memory_space=pltpu.VMEM)
    hbm = pl.BlockSpec(memory_space=pltpu.HBM)
    dma = pltpu.SemaphoreType.DMA

    def call(body, name, ins, outs, flops, nbytes, out_specs=None, scratch=(), aliases={}):
        return pl.pallas_call(
            body,
            name=name,
            in_specs=ins,
            out_shape=outs,
            out_specs=out_specs if out_specs is not None else jax.tree.map(lambda _: vmem, outs),
            scratch_shapes=scratch,
            input_output_aliases=aliases,
            compiler_params=pltpu.CompilerParams(vmem_limit_bytes=32 * MIB),
            cost_estimate=pl.CostEstimate(flops=flops // 1024, bytes_accessed=nbytes // 1024, transcendentals=0),
        )

    def pairs(target_of):
        found = [(source, target_of(source) % count) for source in range(count)]
        assert sorted(target for _, target in found) == list(range(count))
        return found

    def swapped(array):
        return lax.ppermute(array, "head", [(0, 1), (1, 0)])

    key_heads = keys.shape[1] // HEAD_SIZE
    kv_shape = shape((half, 2 * keys.shape[1]), BF16)
    table_shape = shape((number, HEAD_SIZE), F32)
    rows_shape, state = shape((half, width), BF16), shape((half, width), F32)
    weights_shape = shape((width, columns), BF16)
    near, onward, k_rot, v, q, p, cosine, sinus = call(
        functools.partial(keys_kernel, count),
        "rotate_keys",
        [hbm] * 5,
        [kv_shape, kv_shape]
        + [shape(keys.shape, BF16)] * 2
        + [shape(queries.shape, BF16), shape((1, number), jnp.int32), table_shape, table_shape],
        4 * MIB,
        4 * MIB,
        scratch=[pltpu.VMEM(keys.shape, BF16), pltpu.VMEM((1, HEAD_SIZE), F32), dma((5,))],
    )(*(in_hbm(array) for array in (keys, values, queries, position_row, frequency)))
    near_got = lax.ppermute(near, "ctx", pairs(lambda r: r + 3 if r % 2 else r + 1))
    next_got = lax.ppermute(onward, "ctx", pairs(lambda r: r + 2))
    own, rot, acc, top, total = call(
        functools.partial(own_kernel, group),
        "own_tiles",
        [vmem] * 6,
        [rows_shape, rows_shape, state, state, state],
        256 * MIB,
        4 * MIB,
    )(q, k_rot, v, p, cosine, sinus)
    first = call(
        functools.partial(first_kernel, count, group), "first_rows", [vmem] * 7, rows_shape, 256 * MIB, 4 * MIB
    )(own, rot, near_got, p, acc, top, total)
    first_got = swapped(first)
    q, first = lax.optimization_barrier((q, first))
    rot, *state_now = call(
        functools.partial(second_kernel, count, group),
        "second_rows",
        [vmem] * 7,
        [rows_shape, state, state, state],
        1024 * MIB,
        12 * MIB,
    )(q, k_rot, v, p, cosine, sinus, near_got)
    rot, next_got = lax.optimization_barrier((rot, next_got))
    last_got = lax.ppermute(next_got, "ctx", pairs(lambda r: r + 1 - 2 * (r % 2)))
    state_now = call(
        functools.partial(next_kernel, count, group),
        "next_tile",
        [vmem] * 6,
        [state, state, state],
        512 * MIB,
        4 * MIB,
        aliases={3: 0, 4: 1, 5: 2},
    )(rot, next_got, p, *state_now)
    seconds, seconds_got = [], []
    for part in range(key_heads):
        second = call(
            functools.partial(third_kernel, count, group, part),
            "last_tile",
            [vmem] * 6,
            shape((half, group * HEAD_SIZE), BF16),
            256 * MIB,
            4 * MIB,
        )(rot, last_got, p, *state_now)
        seconds_got.append(swapped(second))
        rot, second = lax.optimization_barrier((rot, second))
        seconds.append(second)
    begun, partial_sum, w_other = call(
        project_kernel,
        "project_first",
        [vmem] * (2 + key_heads) + [hbm],
        [shape((number, columns), BF16), shape((half, columns), F32), weights_shape],
        3072 * MIB,
        8 * MIB,
        out_specs=[hbm, vmem, vmem],
        scratch=[pltpu.VMEM(weights_shape.shape, BF16), pltpu.VMEM((half, columns), BF16), dma((3, tiles))],
    )(first, first_got, *seconds, in_hbm(out_weight))
    for part in range(key_heads - 1):
        partial_sum = call(
            functools.partial(add_kernel, part),
            "project_second",
            [vmem] * 3,
            shape((half, columns), F32),
            512 * MIB,
            4 * MIB,
        )(seconds_got[part], partial_sum, w_other)
    return call(
        functools.partial(last_kernel, key_heads - 1),
        "project_last",
        [vmem] * 3 + [hbm],
        shape((number, columns), BF16),
        512 * MIB,
        4 * MIB,
        out_specs=hbm,
        scratch=[pltpu.VMEM((half, columns), BF16), dma((tiles,))],
        aliases={3: 0},
    )(seconds_got[-1], partial_sum, w_other, begun)


def solution(mesh):
    in_specs = (P("ctx", "head"), P("ctx", "head"), P("ctx", "head"), P("ctx"), P(None, "head"))
    out_specs = P("ctx", "head")
    return jax.shard_map(shards, mesh=mesh, in_specs=in_specs, out_specs=out_specs, check_vma=False)
```

```python
import functools
import math

import jax
import jax.numpy as jnp
import numpy as np
from jax import lax
from jax.experimental import pallas as pl
from jax.experimental.pallas import tpu as pltpu
from jax.sharding import PartitionSpec as P

HEAD_SIZE = 128
LOWEST = -1e30
FAR = 1 << 16
MIB = 1 << 20
SCORE_SCALE = math.log2(math.e) / math.sqrt(HEAD_SIZE)
BF16, F32 = jnp.bfloat16, jnp.float32


def distance(rank, step, count):
    return jnp.where(rank >= step, step, count - step)


def waits_for_keys(rank):
    return (rank == 1) | (rank == 2)


def first_begin(rank, half):
    return pl.multiple_of(jnp.where(rank < 2, 0, half), half)


def half_positions(p_ref, rank, first):
    half = p_ref.shape[1] // 2
    early = (rank < 2) if first else (rank >= 2)
    return jnp.where(early, p_ref[:, :half], p_ref[:, half:])


def column(row, width):
    return jnp.broadcast_to(row, (width, row.shape[1])).T


def tile_biases(position_row, kinds):
    number = position_row.shape[1]
    position = column(position_row, number)
    query = lax.broadcasted_iota(jnp.int32, (number, number), 0)
    key = lax.broadcasted_iota(jnp.int32, (number, number), 1)
    ahead = key - query
    reach = ahead + position
    found = []
    for pieces, diagonal in kinds:
        allowed = reach >= pieces * number
        if diagonal:
            allowed = allowed & (ahead <= 0)
        found.append(jnp.where(allowed, 0.0, LOWEST).astype(F32))
    return found


def sine_cosine(angle):
    turns = jnp.floor(angle * (2.0 / math.pi) + 0.5)
    rest = ((angle - turns * 1.5703125) - turns * 4.837512969970703e-4) - turns * 7.549789954891888e-8
    square = rest * rest
    sine = ((-1.9515295891e-4 * square + 8.3321608736e-3) * square - 1.6666654611e-1) * square * rest + rest
    cosine = (
        ((2.443315711809948e-5 * square - 1.388731625493765e-3) * square + 4.166664568298827e-2) * square * square
        - 0.5 * square
        + 1.0
    )
    quarter = turns.astype(jnp.int32)
    swap = (quarter & 1) == 1
    out_sine = jnp.where(swap, cosine, sine)
    out_cosine = jnp.where(swap, sine, cosine)
    out_sine = jnp.where((quarter & 2) == 2, -out_sine, out_sine)
    out_cosine = jnp.where(((quarter + 1) & 2) == 2, -out_cosine, out_cosine)
    return out_sine, out_cosine


def turned(block, cosine, sinus):
    wide = block.astype(F32)
    return (wide * cosine + pltpu.roll(wide, HEAD_SIZE // 2, 1) * sinus).astype(BF16)


def scores_of(query, key, bias):
    raw = lax.dot_general(query, key, (((1,), (1,)), ((), ())), preferred_element_type=F32)
    return raw * SCORE_SCALE + bias


def weighted(weights, value):
    return jnp.dot(weights.astype(BF16), value, preferred_element_type=F32)


def spread(entries):
    return jnp.broadcast_to(entries, (entries.shape[0], HEAD_SIZE))


def with_ones(value):
    return jnp.concatenate([value, jnp.ones_like(value)], axis=1)


def head_slices(head, group, width):
    at = slice(head * HEAD_SIZE, (head + 1) * HEAD_SIZE)
    low = head // group * HEAD_SIZE
    return at, slice(low, low + HEAD_SIZE), slice(width + low, width + low + HEAD_SIZE)


def begin_state(query, keys, values, biases):
    scores = [scores_of(query, key, bias) for key, bias in zip(keys, biases)]
    top = jnp.max(functools.reduce(jnp.maximum, scores), axis=1, keepdims=True)
    weights = [jnp.exp2(score - top) for score in scores]
    both = functools.reduce(jnp.add, [weighted(w, value) for w, value in zip(weights, values)])
    return both[:, :HEAD_SIZE], spread(top), both[:, HEAD_SIZE:]


def added_tile(summed, top, total, query, key, value, bias):
    score = scores_of(query, key, bias)
    updated = jnp.maximum(top, spread(jnp.max(score, axis=1, keepdims=True)))
    weights = jnp.exp2(score - jnp.concatenate([updated] * (score.shape[1] // HEAD_SIZE), axis=1))
    factor = jnp.exp2(top - updated)
    both = weighted(weights, value)
    return summed * factor + both[:, :HEAD_SIZE], updated, total * factor + both[:, HEAD_SIZE:]


def finished(state):
    summed, _, total = state
    return (summed * (1.0 / total)).astype(BF16)


def keys_kernel(
    count, k_hbm, v_hbm, q_hbm, p_hbm, f_hbm, near_ref, next_ref, rot_ref, v_ref, q_ref, p_ref, cos_ref, sin_ref,
    k_ref, f_ref, sems,
):
    pairs = ((p_hbm, p_ref), (f_hbm, f_ref), (k_hbm, k_ref), (v_hbm, v_ref), (q_hbm, q_ref))
    copies = [pltpu.make_async_copy(source, target, sems.at[i]) for i, (source, target) in enumerate(pairs)]
    for copy in copies:
        copy.start()
    rank = lax.axis_index("ctx")
    half = k_ref.shape[0] // 2
    width = k_ref.shape[1]
    copies[0].wait()
    copies[1].wait()
    position = p_ref[...].astype(F32)
    early = column(position[:, :half], HEAD_SIZE)
    late = column(position[:, half:], HEAD_SIZE)
    lane = lax.broadcasted_iota(jnp.int32, (half, HEAD_SIZE), 1)
    front = lane < HEAD_SIZE // 2
    sine, cosine = sine_cosine(jnp.where(front, early, late) * f_ref[...])
    sine_other = pltpu.roll(sine, HEAD_SIZE // 2, 1)
    cosine_other = pltpu.roll(cosine, HEAD_SIZE // 2, 1)
    cos_ref[:half] = jnp.where(front, cosine, cosine_other)
    cos_ref[half:] = jnp.where(front, cosine_other, cosine)
    sin_ref[:half] = jnp.where(front, -sine, sine_other)
    sin_ref[half:] = jnp.where(front, -sine_other, sine)
    copies[2].wait()
    for head in range(width // HEAD_SIZE):
        at = slice(head * HEAD_SIZE, (head + 1) * HEAD_SIZE)
        rot_ref[:, at] = turned(k_ref[:, at], cos_ref[...], sin_ref[...])
    copies[3].wait()
    wrap = (rank % 2 == 1) & (rank + 3 >= count)
    rows = pl.ds(pl.multiple_of(jnp.where(wrap, half, 0), half), half)
    near_ref[:, :width] = rot_ref[rows, :]
    near_ref[:, width:] = v_ref[rows, :]
    rows = pl.ds(pl.multiple_of(jnp.where(rank + 2 >= count, half, 0), half), half)
    next_ref[:, :width] = rot_ref[rows, :]
    next_ref[:, width:] = v_ref[rows, :]
    copies[4].wait()


def own_kernel(group, q_ref, k_ref, v_ref, p_ref, cos_ref, sin_ref, out_ref, rot_ref, acc_ref, top_ref, sum_ref):
    rank = lax.axis_index("ctx")
    half = q_ref.shape[0] // 2
    rows = pl.ds(first_begin(rank, half), half)
    biases = tile_biases(half_positions(p_ref, rank, True), [(0, True)])
    for head in range(q_ref.shape[1] // HEAD_SIZE):
        at, shared, _ = head_slices(head, group, 0)
        query = turned(q_ref[rows, at], cos_ref[rows, :], sin_ref[rows, :])
        rot_ref[:, at] = query
        if head % group == 0:
            value = with_ones(v_ref[rows, shared])
        summed, top, total = begin_state(query, [k_ref[rows, shared]], [value], biases)
        acc_ref[:, at] = summed
        top_ref[:, at] = top
        sum_ref[:, at] = total
        out_ref[:, at] = (summed * (1.0 / total)).astype(BF16)


def first_kernel(count, group, heads, own_ref, rot_ref, kv_ref, p_ref, acc_ref, top_ref, sum_ref, out_ref):
    rank = lax.axis_index("ctx")
    width = kv_ref.shape[1] // 2
    step = jnp.where(rank % 2 == 1, 1, 3)
    used = waits_for_keys(rank)

    @pl.when(used)
    def _():
        biases = tile_biases(half_positions(p_ref, rank, True), [(distance(rank, step, count), False)])
        for number, head in enumerate(heads):
            at, key_at, value_at = head_slices(head, group, width)
            state = acc_ref[:, at], top_ref[:, at], sum_ref[:, at]
            if number == 0 or head % group == 0:
                value = with_ones(kv_ref[:, value_at])
            state = added_tile(*state, rot_ref[:, at], kv_ref[:, key_at], value, *biases)
            out_ref[:, number * HEAD_SIZE : (number + 1) * HEAD_SIZE] = finished(state)

    @pl.when(jnp.logical_not(used))
    def _():
        out_ref[...] = own_ref[:, heads[0] * HEAD_SIZE : (heads[-1] + 1) * HEAD_SIZE]


def second_kernel(
    count, group, q_ref, k_ref, v_ref, p_ref, cos_ref, sin_ref, kv_ref, rot_ref, acc_ref, top_ref, sum_ref
):
    rank = lax.axis_index("ctx")
    half = q_ref.shape[0] // 2
    width = k_ref.shape[1]
    rows = pl.ds(pl.multiple_of(half - first_begin(rank, half), half), half)
    step = jnp.where(rank % 2 == 1, 1, 3)
    reach = jnp.where(waits_for_keys(rank), FAR, distance(rank, step, count))
    biases = tile_biases(half_positions(p_ref, rank, False), [(0, True), (reach, False)])
    for head in range(q_ref.shape[1] // HEAD_SIZE):
        at, key_at, value_at = head_slices(head, group, width)
        query = turned(q_ref[rows, at], cos_ref[rows, :], sin_ref[rows, :])
        rot_ref[:, at] = query
        keys = [k_ref[rows, key_at], kv_ref[:, key_at]]
        if head % group == 0:
            values = [with_ones(v_ref[rows, key_at]), with_ones(kv_ref[:, value_at])]
        acc_ref[:, at], top_ref[:, at], sum_ref[:, at] = begin_state(query, keys, values, biases)


def next_kernel(count, group, rot_ref, kv_ref, p_ref, acc_ref, top_ref, sum_ref, *outs):
    rank = lax.axis_index("ctx")
    width = kv_ref.shape[1] // 2
    biases = tile_biases(half_positions(p_ref, rank, False), [(distance(rank, 2, count), False)])
    for head in range(rot_ref.shape[1] // HEAD_SIZE):
        at, key_at, value_at = head_slices(head, group, width)
        state = acc_ref[:, at], top_ref[:, at], sum_ref[:, at]
        if head % group == 0:
            value = with_ones(kv_ref[:, value_at])
        state = added_tile(*state, rot_ref[:, at], kv_ref[:, key_at], value, *biases)
        for out_ref, entries in zip(outs, state):
            out_ref[:, at] = entries


def third_kernel(count, group, heads, rot_ref, kv_ref, p_ref, acc_ref, top_ref, sum_ref, *rest):
    out_ref = rest[-1]
    held = 0
    for ref in rest[:-1]:
        held = ref.shape[1]
        out_ref[:, :held] = ref[...]
    rank = lax.axis_index("ctx")
    width = kv_ref.shape[1] // 2
    step = jnp.where(rank % 2 == 1, 3, 1)
    biases = tile_biases(half_positions(p_ref, rank, False), [(distance(rank, step, count), False)])
    for number, head in enumerate(heads):
        at, key_at, value_at = head_slices(head, group, width)
        state = acc_ref[:, at], top_ref[:, at], sum_ref[:, at]
        if number == 0 or head % group == 0:
            value = with_ones(kv_ref[:, value_at])
        state = added_tile(*state, rot_ref[:, at], kv_ref[:, key_at], value, *biases)
        out_ref[:, held + number * HEAD_SIZE : held + (number + 1) * HEAD_SIZE] = finished(state)


def dot(left, right):
    return jnp.dot(left, right, preferred_element_type=F32)


TILE = 512


def project_kernel(
    first0_ref, first1_ref, got0_ref, second0_ref, second1_ref, w_hbm, part_ref, other_ref, sum_ref, mine_ref, sems
):
    side = lax.axis_index("head")
    half, depth = first0_ref.shape[0], mine_ref.shape[0]
    carried = first1_ref.shape[1]
    tiles = [slice(start, start + TILE) for start in range(0, mine_ref.shape[1], TILE)]
    weights = []
    for tile, at in enumerate(tiles):
        for number, (part, ref) in enumerate(((side, mine_ref), (1 - side, other_ref))):
            source = w_hbm.at[pl.ds(pl.multiple_of(part * depth, depth), depth), at]
            weights.append(pltpu.make_async_copy(source, ref.at[:, at], sems.at[number, tile]))
            weights[-1].start()
    first = jnp.concatenate([first0_ref[...], first1_ref[...]], axis=1)
    second = jnp.concatenate([second0_ref[:, carried:], second1_ref[...]], axis=1)
    stacked = jnp.concatenate([first, second], axis=0)
    for tile, at in enumerate(tiles):
        weights[2 * tile].wait()
        both = dot(stacked, mine_ref[:, at])
        part_ref[:, at] = both[half:]
        weights[2 * tile + 1].wait()
        sum_ref[:, at] = both[:half] + dot(got0_ref[...], other_ref[: got0_ref.shape[1], at])


def add_kernel(carried, got_ref, first_ref, part_ref, w_ref, out_hbm, out_ref, held_ref, sems):
    rank = lax.axis_index("ctx")
    half = got_ref.shape[0]
    depth = w_ref.shape[0]
    rows = pl.ds(first_begin(rank, half), half)
    copies = []
    for tile in range(w_ref.shape[1] // TILE):
        at = slice(tile * TILE, (tile + 1) * TILE)
        added = dot(got_ref[:, :carried], w_ref[depth - carried :, at])
        held_ref[:, at] = (first_ref[:, at] + added).astype(BF16)
        copies.append(pltpu.make_async_copy(held_ref.at[:, at], out_hbm.at[rows, at], sems.at[tile]))
        copies[-1].start()
        out_ref[:, at] = part_ref[:, at] + dot(got_ref[:, carried:], w_ref[: depth - carried, at])
    for copy in copies:
        copy.wait()


def last_kernel(begin, got_ref, part_ref, w_ref, begun_hbm, out_hbm, held_ref, sems):
    del begun_hbm
    rank = lax.axis_index("ctx")
    half, depth = got_ref.shape
    out_rows = pl.ds(pl.multiple_of(half - first_begin(rank, half), half), half)
    copies = []
    for tile in range(w_ref.shape[1] // TILE):
        at = slice(tile * TILE, (tile + 1) * TILE)
        added = dot(got_ref[...], w_ref[begin : begin + depth, at])
        held_ref[:, at] = (part_ref[:, at] + added).astype(BF16)
        copies.append(pltpu.make_async_copy(held_ref.at[:, at], out_hbm.at[out_rows, at], sems.at[tile]))
        copies[-1].start()
    for copy in copies:
        copy.wait()


def shards(queries, keys, values, positions, out_weight):
    number, width = queries.shape
    half = number // 2
    count = lax.axis_size("ctx")
    group = width // keys.shape[1]
    columns = out_weight.shape[1]
    tiles = columns // TILE
    in_hbm = lambda array: pltpu.with_memory_space_constraint(array, pltpu.HBM)
    position_row = positions.reshape(1, number)
    table = np.power(500000.0, -2.0 * np.arange(HEAD_SIZE // 2) / HEAD_SIZE).astype(np.float32)
    frequency = jnp.asarray(np.concatenate([table, table])[None, :])
    shape = jax.ShapeDtypeStruct
    vmem = pl.BlockSpec(memory_space=pltpu.VMEM)
    hbm = pl.BlockSpec(memory_space=pltpu.HBM)
    dma = pltpu.SemaphoreType.DMA

    def call(body, name, ins, outs, flops, nbytes, out_specs=None, scratch=(), aliases={}):
        return pl.pallas_call(
            body,
            name=name,
            in_specs=ins,
            out_shape=outs,
            out_specs=out_specs if out_specs is not None else jax.tree.map(lambda _: vmem, outs),
            scratch_shapes=scratch,
            input_output_aliases=aliases,
            compiler_params=pltpu.CompilerParams(vmem_limit_bytes=32 * MIB),
            cost_estimate=pl.CostEstimate(flops=flops // 1024, bytes_accessed=nbytes // 1024, transcendentals=0),
        )

    def pairs(target_of):
        found = [(source, target_of(source) % count) for source in range(count)]
        assert sorted(target for _, target in found) == list(range(count))
        return found

    def swapped(array):
        return lax.ppermute(array, "head", [(0, 1), (1, 0)])

    kv_shape = shape((half, 2 * keys.shape[1]), BF16)
    table_shape = shape((number, HEAD_SIZE), F32)
    rows_shape, state = shape((half, width), BF16), shape((half, width), F32)
    weights_shape = shape((width, columns), BF16)
    near, onward, k_rot, v, q, p, cosine, sinus = call(
        functools.partial(keys_kernel, count),
        "rotate_keys",
        [hbm] * 5,
        [kv_shape, kv_shape]
        + [shape(keys.shape, BF16)] * 2
        + [shape(queries.shape, BF16), shape((1, number), jnp.int32), table_shape, table_shape],
        4 * MIB,
        4 * MIB,
        scratch=[pltpu.VMEM(keys.shape, BF16), pltpu.VMEM((1, HEAD_SIZE), F32), dma((5,))],
    )(*(in_hbm(array) for array in (keys, values, queries, position_row, frequency)))
    near_got = lax.ppermute(near, "ctx", pairs(lambda r: r + 3 if r % 2 else r + 1))
    own, rot, acc, top, total = call(
        functools.partial(own_kernel, group),
        "own_tiles",
        [vmem] * 6,
        [rows_shape, rows_shape, state, state, state],
        256 * MIB,
        4 * MIB,
    )(q, k_rot, v, p, cosine, sinus)
    onward, rot = lax.optimization_barrier((onward, rot))
    next_got = lax.ppermute(onward, "ctx", pairs(lambda r: r + 2))
    heads = width // HEAD_SIZE
    cut = heads - max(heads // 4, 1)
    parts = range(cut), range(cut, heads)
    firsts = []
    for part in parts:
        first = call(
            functools.partial(first_kernel, count, group, part),
            "first_rows",
            [vmem] * 7,
            shape((half, len(part) * HEAD_SIZE), BF16),
            256 * MIB,
            4 * MIB,
        )(own, rot, near_got, p, acc, top, total)
        if not firsts:
            first_got = swapped(first)
        q, rot, first = lax.optimization_barrier((q, rot, first))
        firsts.append(first)
    rot, *state_now = call(
        functools.partial(second_kernel, count, group),
        "second_rows",
        [vmem] * 7,
        [rows_shape, state, state, state],
        1024 * MIB,
        12 * MIB,
    )(q, k_rot, v, p, cosine, sinus, near_got)
    rot, next_got = lax.optimization_barrier((rot, next_got))
    last_got = lax.ppermute(next_got, "ctx", pairs(lambda r: r + 1 - 2 * (r % 2)))
    state_now = call(
        functools.partial(next_kernel, count, group),
        "next_tile",
        [vmem] * 6,
        [state, state, state],
        512 * MIB,
        4 * MIB,
        aliases={3: 0, 4: 1, 5: 2},
    )(rot, next_got, p, *state_now)
    seconds = []
    for part, along in zip(parts, (firsts[1:], [])):
        held = sum(array.shape[1] for array in along)
        second = call(
            functools.partial(third_kernel, count, group, part),
            "last_tile",
            [vmem] * (6 + len(along)),
            shape((half, held + len(part) * HEAD_SIZE), BF16),
            256 * MIB,
            4 * MIB,
        )(rot, last_got, p, *state_now, *along)
        if along:
            second, first_got = lax.optimization_barrier((second, first_got))
            second_got = swapped(second)
        rot, second = lax.optimization_barrier((rot, second))
        seconds.append(second)
    sum_shape = shape((half, columns), F32)
    partial_sum, w_other, first_sum = call(
        project_kernel,
        "project_first",
        [vmem] * 5 + [hbm],
        [sum_shape, weights_shape, sum_shape],
        3072 * MIB,
        8 * MIB,
        scratch=[pltpu.VMEM(weights_shape.shape, BF16), dma((2, tiles))],
    )(*firsts, first_got, *seconds, in_hbm(out_weight))
    third, partial_sum = lax.optimization_barrier((seconds[1], partial_sum))
    third_got = swapped(third)
    begun, partial_sum = call(
        functools.partial(add_kernel, (heads - cut) * HEAD_SIZE),
        "project_second",
        [vmem] * 4,
        [shape((number, columns), BF16), sum_shape],
        1024 * MIB,
        4 * MIB,
        out_specs=[hbm, vmem],
        scratch=[pltpu.VMEM((half, columns), BF16), dma((tiles,))],
    )(second_got, first_sum, partial_sum, w_other)
    return call(
        functools.partial(last_kernel, cut * HEAD_SIZE),
        "project_last",
        [vmem] * 3 + [hbm],
        shape((number, columns), BF16),
        512 * MIB,
        4 * MIB,
        out_specs=hbm,
        scratch=[pltpu.VMEM((half, columns), BF16), dma((tiles,))],
        aliases={3: 0},
    )(third_got, partial_sum, w_other, begun)


def solution(mesh):
    in_specs = (P("ctx", "head"), P("ctx", "head"), P("ctx", "head"), P("ctx"), P(None, "head"))
    out_specs = P("ctx", "head")
    return jax.shard_map(shards, mesh=mesh, in_specs=in_specs, out_specs=out_specs, check_vma=False)
```

```python
import functools
import math

import jax
import jax.numpy as jnp
import numpy as np
from jax import lax
from jax.experimental import pallas as pl
from jax.experimental.pallas import tpu as pltpu
from jax.sharding import PartitionSpec as P

HEAD_SIZE = 128
LOWEST = -1e30
FAR = 1 << 16
MIB = 1 << 20
SCORE_SCALE = math.log2(math.e) / math.sqrt(HEAD_SIZE)
BF16, F32 = jnp.bfloat16, jnp.float32


def distance(rank, step, count):
    return jnp.where(rank >= step, step, count - step)


def waits_for_keys(rank):
    return (rank == 1) | (rank == 2)


def first_begin(rank, half):
    return pl.multiple_of(jnp.where(rank < 2, 0, half), half)


def half_positions(p_ref, rank, first):
    half = p_ref.shape[1] // 2
    early = (rank < 2) if first else (rank >= 2)
    return jnp.where(early, p_ref[:, :half], p_ref[:, half:])


def column(row, width):
    return jnp.broadcast_to(row, (width, row.shape[1])).T


def tile_biases(position_row, kinds):
    number = position_row.shape[1]
    position = column(position_row, number)
    query = lax.broadcasted_iota(jnp.int32, (number, number), 0)
    key = lax.broadcasted_iota(jnp.int32, (number, number), 1)
    ahead = key - query
    reach = ahead + position
    found = []
    for pieces, diagonal in kinds:
        allowed = reach >= pieces * number
        if diagonal:
            allowed = allowed & (ahead <= 0)
        found.append(jnp.where(allowed, 0.0, LOWEST).astype(F32))
    return found


def sine_cosine(angle):
    turns = jnp.floor(angle * (2.0 / math.pi) + 0.5)
    rest = ((angle - turns * 1.5703125) - turns * 4.837512969970703e-4) - turns * 7.549789954891888e-8
    square = rest * rest
    sine = ((-1.9515295891e-4 * square + 8.3321608736e-3) * square - 1.6666654611e-1) * square * rest + rest
    cosine = (
        ((2.443315711809948e-5 * square - 1.388731625493765e-3) * square + 4.166664568298827e-2) * square * square
        - 0.5 * square
        + 1.0
    )
    quarter = turns.astype(jnp.int32)
    swap = (quarter & 1) == 1
    out_sine = jnp.where(swap, cosine, sine)
    out_cosine = jnp.where(swap, sine, cosine)
    out_sine = jnp.where((quarter & 2) == 2, -out_sine, out_sine)
    out_cosine = jnp.where(((quarter + 1) & 2) == 2, -out_cosine, out_cosine)
    return out_sine, out_cosine


def turned(block, cosine, sinus):
    wide = block.astype(F32)
    return (wide * cosine + pltpu.roll(wide, HEAD_SIZE // 2, 1) * sinus).astype(BF16)


def scores_of(query, key, bias):
    raw = lax.dot_general(query, key, (((1,), (1,)), ((), ())), preferred_element_type=F32)
    return raw * SCORE_SCALE + bias


def weighted(weights, value):
    return jnp.dot(weights.astype(BF16), value, preferred_element_type=F32)


def spread(entries):
    return jnp.broadcast_to(entries, (entries.shape[0], HEAD_SIZE))


def with_ones(value):
    return jnp.concatenate([value, jnp.ones_like(value)], axis=1)


def head_slices(head, group, width):
    at = slice(head * HEAD_SIZE, (head + 1) * HEAD_SIZE)
    low = head // group * HEAD_SIZE
    return at, slice(low, low + HEAD_SIZE), slice(width + low, width + low + HEAD_SIZE)


def begin_state(query, keys, values, biases):
    scores = [scores_of(query, key, bias) for key, bias in zip(keys, biases)]
    top = jnp.max(functools.reduce(jnp.maximum, scores), axis=1, keepdims=True)
    weights = [jnp.exp2(score - top) for score in scores]
    both = functools.reduce(jnp.add, [weighted(w, value) for w, value in zip(weights, values)])
    return both[:, :HEAD_SIZE], spread(top), both[:, HEAD_SIZE:]


def added_tile(summed, top, total, query, key, value, bias):
    score = scores_of(query, key, bias)
    updated = jnp.maximum(top, spread(jnp.max(score, axis=1, keepdims=True)))
    weights = jnp.exp2(score - jnp.concatenate([updated] * (score.shape[1] // HEAD_SIZE), axis=1))
    factor = jnp.exp2(top - updated)
    both = weighted(weights, value)
    return summed * factor + both[:, :HEAD_SIZE], updated, total * factor + both[:, HEAD_SIZE:]


def finished(state):
    summed, _, total = state
    return (summed * (1.0 / total)).astype(BF16)


def keys_kernel(
    count, k_hbm, v_hbm, q_hbm, p_hbm, f_hbm, near_ref, next_ref, rot_ref, v_ref, q_ref, p_ref, cos_ref, sin_ref,
    k_ref, f_ref, sems,
):
    pairs = ((p_hbm, p_ref), (f_hbm, f_ref), (k_hbm, k_ref), (v_hbm, v_ref), (q_hbm, q_ref))
    copies = [pltpu.make_async_copy(source, target, sems.at[i]) for i, (source, target) in enumerate(pairs)]
    for copy in copies:
        copy.start()
    rank = lax.axis_index("ctx")
    half = k_ref.shape[0] // 2
    width = k_ref.shape[1]
    copies[0].wait()
    copies[1].wait()
    position = p_ref[...].astype(F32)
    early = column(position[:, :half], HEAD_SIZE)
    late = column(position[:, half:], HEAD_SIZE)
    lane = lax.broadcasted_iota(jnp.int32, (half, HEAD_SIZE), 1)
    front = lane < HEAD_SIZE // 2
    sine, cosine = sine_cosine(jnp.where(front, early, late) * f_ref[...])
    sine_other = pltpu.roll(sine, HEAD_SIZE // 2, 1)
    cosine_other = pltpu.roll(cosine, HEAD_SIZE // 2, 1)
    cos_ref[:half] = jnp.where(front, cosine, cosine_other)
    cos_ref[half:] = jnp.where(front, cosine_other, cosine)
    sin_ref[:half] = jnp.where(front, -sine, sine_other)
    sin_ref[half:] = jnp.where(front, -sine_other, sine)
    copies[2].wait()
    for head in range(width // HEAD_SIZE):
        at = slice(head * HEAD_SIZE, (head + 1) * HEAD_SIZE)
        rot_ref[:, at] = turned(k_ref[:, at], cos_ref[...], sin_ref[...])
    copies[3].wait()
    wrap = (rank % 2 == 1) & (rank + 3 >= count)
    rows = pl.ds(pl.multiple_of(jnp.where(wrap, half, 0), half), half)
    near_ref[:, :width] = rot_ref[rows, :]
    near_ref[:, width:] = v_ref[rows, :]
    rows = pl.ds(pl.multiple_of(jnp.where(rank + 2 >= count, half, 0), half), half)
    next_ref[:, :width] = rot_ref[rows, :]
    next_ref[:, width:] = v_ref[rows, :]
    copies[4].wait()


def own_kernel(group, q_ref, k_ref, v_ref, p_ref, cos_ref, sin_ref, out_ref, rot_ref, acc_ref, top_ref, sum_ref):
    rank = lax.axis_index("ctx")
    half = q_ref.shape[0] // 2
    rows = pl.ds(first_begin(rank, half), half)
    biases = tile_biases(half_positions(p_ref, rank, True), [(0, True)])
    for head in range(q_ref.shape[1] // HEAD_SIZE):
        at, shared, _ = head_slices(head, group, 0)
        query = turned(q_ref[rows, at], cos_ref[rows, :], sin_ref[rows, :])
        rot_ref[:, at] = query
        if head % group == 0:
            value = with_ones(v_ref[rows, shared])
        summed, top, total = begin_state(query, [k_ref[rows, shared]], [value], biases)
        acc_ref[:, at] = summed
        top_ref[:, at] = top
        sum_ref[:, at] = total
        out_ref[:, at] = (summed * (1.0 / total)).astype(BF16)


def first_kernel(count, group, heads, own_ref, rot_ref, kv_ref, p_ref, acc_ref, top_ref, sum_ref, out_ref):
    rank = lax.axis_index("ctx")
    width = kv_ref.shape[1] // 2
    step = jnp.where(rank % 2 == 1, 1, 3)
    used = waits_for_keys(rank)

    @pl.when(used)
    def _():
        biases = tile_biases(half_positions(p_ref, rank, True), [(distance(rank, step, count), False)])
        for number, head in enumerate(heads):
            at, key_at, value_at = head_slices(head, group, width)
            state = acc_ref[:, at], top_ref[:, at], sum_ref[:, at]
            if number == 0 or head % group == 0:
                value = with_ones(kv_ref[:, value_at])
            state = added_tile(*state, rot_ref[:, at], kv_ref[:, key_at], value, *biases)
            out_ref[:, number * HEAD_SIZE : (number + 1) * HEAD_SIZE] = finished(state)

    @pl.when(jnp.logical_not(used))
    def _():
        out_ref[...] = own_ref[:, heads[0] * HEAD_SIZE : (heads[-1] + 1) * HEAD_SIZE]


def second_kernel(
    count, group, q_ref, k_ref, v_ref, p_ref, cos_ref, sin_ref, kv_ref, rot_ref, acc_ref, top_ref, sum_ref
):
    rank = lax.axis_index("ctx")
    half = q_ref.shape[0] // 2
    width = k_ref.shape[1]
    rows = pl.ds(pl.multiple_of(half - first_begin(rank, half), half), half)
    step = jnp.where(rank % 2 == 1, 1, 3)
    reach = jnp.where(waits_for_keys(rank), FAR, distance(rank, step, count))
    biases = tile_biases(half_positions(p_ref, rank, False), [(0, True), (reach, False)])
    for head in range(q_ref.shape[1] // HEAD_SIZE):
        at, key_at, value_at = head_slices(head, group, width)
        query = turned(q_ref[rows, at], cos_ref[rows, :], sin_ref[rows, :])
        rot_ref[:, at] = query
        keys = [k_ref[rows, key_at], kv_ref[:, key_at]]
        if head % group == 0:
            values = [with_ones(v_ref[rows, key_at]), with_ones(kv_ref[:, value_at])]
        acc_ref[:, at], top_ref[:, at], sum_ref[:, at] = begin_state(query, keys, values, biases)


def next_kernel(count, group, rot_ref, kv_ref, p_ref, acc_ref, top_ref, sum_ref, *outs):
    rank = lax.axis_index("ctx")
    width = kv_ref.shape[1] // 2
    biases = tile_biases(half_positions(p_ref, rank, False), [(distance(rank, 2, count), False)])
    for head in range(rot_ref.shape[1] // HEAD_SIZE):
        at, key_at, value_at = head_slices(head, group, width)
        state = acc_ref[:, at], top_ref[:, at], sum_ref[:, at]
        if head % group == 0:
            value = with_ones(kv_ref[:, value_at])
        state = added_tile(*state, rot_ref[:, at], kv_ref[:, key_at], value, *biases)
        for out_ref, entries in zip(outs, state):
            out_ref[:, at] = entries


def third_kernel(count, group, heads, rot_ref, kv_ref, p_ref, acc_ref, top_ref, sum_ref, out_ref):
    rank = lax.axis_index("ctx")
    width = kv_ref.shape[1] // 2
    step = jnp.where(rank % 2 == 1, 3, 1)
    biases = tile_biases(half_positions(p_ref, rank, False), [(distance(rank, step, count), False)])
    for number, head in enumerate(heads):
        at, key_at, value_at = head_slices(head, group, width)
        state = acc_ref[:, at], top_ref[:, at], sum_ref[:, at]
        if number == 0 or head % group == 0:
            value = with_ones(kv_ref[:, value_at])
        state = added_tile(*state, rot_ref[:, at], kv_ref[:, key_at], value, *biases)
        out_ref[:, number * HEAD_SIZE : (number + 1) * HEAD_SIZE] = finished(state)


def dot(left, right):
    return jnp.dot(left, right, preferred_element_type=F32)


TILE = 512


def project_kernel(own_ref, got_ref, second0_ref, second1_ref, w_hbm, out_hbm, part_ref, other_ref, mine_ref, held_ref, sems):
    rank = lax.axis_index("ctx")
    side = lax.axis_index("head")
    half, depth = own_ref.shape
    rows = pl.ds(first_begin(rank, half), half)
    tiles = [slice(start, start + TILE) for start in range(0, mine_ref.shape[1], TILE)]
    weights = []
    for tile, at in enumerate(tiles):
        for number, (part, ref) in enumerate(((side, mine_ref), (1 - side, other_ref))):
            source = w_hbm.at[pl.ds(pl.multiple_of(part * depth, depth), depth), at]
            weights.append(pltpu.make_async_copy(source, ref.at[:, at], sems.at[number, tile]))
            weights[-1].start()
    second = jnp.concatenate([second0_ref[...], second1_ref[...]], axis=1)
    stacked = jnp.concatenate([own_ref[...], second], axis=0)
    copies = []
    for tile, at in enumerate(tiles):
        weights[2 * tile].wait()
        both = dot(stacked, mine_ref[:, at])
        part_ref[:, at] = both[half:]
        weights[2 * tile + 1].wait()
        held_ref[:, at] = (both[:half] + dot(got_ref[...], other_ref[:, at])).astype(BF16)
        copies.append(pltpu.make_async_copy(held_ref.at[:, at], out_hbm.at[rows, at], sems.at[2, tile]))
        copies[-1].start()
    for copy in copies:
        copy.wait()


def add_kernel(got_ref, part_ref, w_ref, out_ref):
    depth = got_ref.shape[1]
    for start in range(0, w_ref.shape[1], TILE):
        at = slice(start, start + TILE)
        out_ref[:, at] = part_ref[:, at] + dot(got_ref[...], w_ref[:depth, at])


def last_kernel(begin, got_ref, part_ref, w_ref, begun_hbm, out_hbm, held_ref, sems):
    del begun_hbm
    rank = lax.axis_index("ctx")
    half, depth = got_ref.shape
    out_rows = pl.ds(pl.multiple_of(half - first_begin(rank, half), half), half)
    copies = []
    for tile in range(w_ref.shape[1] // TILE):
        at = slice(tile * TILE, (tile + 1) * TILE)
        added = dot(got_ref[...], w_ref[begin : begin + depth, at])
        held_ref[:, at] = (part_ref[:, at] + added).astype(BF16)
        copies.append(pltpu.make_async_copy(held_ref.at[:, at], out_hbm.at[out_rows, at], sems.at[tile]))
        copies[-1].start()
    for copy in copies:
        copy.wait()


def shards(queries, keys, values, positions, out_weight):
    number, width = queries.shape
    half = number // 2
    count = lax.axis_size("ctx")
    group = width // keys.shape[1]
    columns = out_weight.shape[1]
    tiles = columns // TILE
    in_hbm = lambda array: pltpu.with_memory_space_constraint(array, pltpu.HBM)
    position_row = positions.reshape(1, number)
    table = np.power(500000.0, -2.0 * np.arange(HEAD_SIZE // 2) / HEAD_SIZE).astype(np.float32)
    frequency = jnp.asarray(np.concatenate([table, table])[None, :])
    shape = jax.ShapeDtypeStruct
    vmem = pl.BlockSpec(memory_space=pltpu.VMEM)
    hbm = pl.BlockSpec(memory_space=pltpu.HBM)
    dma = pltpu.SemaphoreType.DMA

    def call(body, name, ins, outs, flops, nbytes, out_specs=None, scratch=(), aliases={}):
        return pl.pallas_call(
            body,
            name=name,
            in_specs=ins,
            out_shape=outs,
            out_specs=out_specs if out_specs is not None else jax.tree.map(lambda _: vmem, outs),
            scratch_shapes=scratch,
            input_output_aliases=aliases,
            compiler_params=pltpu.CompilerParams(vmem_limit_bytes=32 * MIB),
            cost_estimate=pl.CostEstimate(flops=flops // 1024, bytes_accessed=nbytes // 1024, transcendentals=0),
        )

    def pairs(target_of):
        found = [(source, target_of(source) % count) for source in range(count)]
        assert sorted(target for _, target in found) == list(range(count))
        return found

    def swapped(array):
        return lax.ppermute(array, "head", [(0, 1), (1, 0)])

    kv_shape = shape((half, 2 * keys.shape[1]), BF16)
    table_shape = shape((number, HEAD_SIZE), F32)
    rows_shape, state = shape((half, width), BF16), shape((half, width), F32)
    weights_shape = shape((width, columns), BF16)
    near, onward, k_rot, v, q, p, cosine, sinus = call(
        functools.partial(keys_kernel, count),
        "rotate_keys",
        [hbm] * 5,
        [kv_shape, kv_shape]
        + [shape(keys.shape, BF16)] * 2
        + [shape(queries.shape, BF16), shape((1, number), jnp.int32), table_shape, table_shape],
        4 * MIB,
        4 * MIB,
        scratch=[pltpu.VMEM(keys.shape, BF16), pltpu.VMEM((1, HEAD_SIZE), F32), dma((5,))],
    )(*(in_hbm(array) for array in (keys, values, queries, position_row, frequency)))
    near_got = lax.ppermute(near, "ctx", pairs(lambda r: r + 3 if r % 2 else r + 1))
    own, rot, acc, top, total = call(
        functools.partial(own_kernel, group),
        "own_tiles",
        [vmem] * 6,
        [rows_shape, rows_shape, state, state, state],
        256 * MIB,
        4 * MIB,
    )(q, k_rot, v, p, cosine, sinus)
    onward, rot = lax.optimization_barrier((onward, rot))
    next_got = lax.ppermute(onward, "ctx", pairs(lambda r: r + 2))
    heads = width // HEAD_SIZE
    cut = heads // 2
    parts = range(cut), range(cut, heads)
    first = call(
        functools.partial(first_kernel, count, group, range(heads)),
        "first_rows",
        [vmem] * 7,
        rows_shape,
        256 * MIB,
        4 * MIB,
    )(own, rot, near_got, p, acc, top, total)
    first_got = swapped(first)
    q, first = lax.optimization_barrier((q, first))
    rot, *state_now = call(
        functools.partial(second_kernel, count, group),
        "second_rows",
        [vmem] * 7,
        [rows_shape, state, state, state],
        1024 * MIB,
        12 * MIB,
    )(q, k_rot, v, p, cosine, sinus, near_got)
    rot, next_got = lax.optimization_barrier((rot, next_got))
    last_got = lax.ppermute(next_got, "ctx", pairs(lambda r: r + 1 - 2 * (r % 2)))
    state_now = call(
        functools.partial(next_kernel, count, group),
        "next_tile",
        [vmem] * 6,
        [state, state, state],
        512 * MIB,
        4 * MIB,
        aliases={3: 0, 4: 1, 5: 2},
    )(rot, next_got, p, *state_now)
    seconds, seconds_got = [], []
    for part in parts:
        second = call(
            functools.partial(third_kernel, count, group, part),
            "last_tile",
            [vmem] * 6,
            shape((half, len(part) * HEAD_SIZE), BF16),
            256 * MIB,
            4 * MIB,
        )(rot, last_got, p, *state_now)
        seconds_got.append(swapped(second))
        rot, second, first_got = lax.optimization_barrier((rot, second, first_got))
        seconds.append(second)
    sum_shape = shape((half, columns), F32)
    begun, partial_sum, w_other = call(
        project_kernel,
        "project_first",
        [vmem] * 4 + [hbm],
        [shape((number, columns), BF16), sum_shape, weights_shape],
        3072 * MIB,
        8 * MIB,
        out_specs=[hbm, vmem, vmem],
        scratch=[pltpu.VMEM(weights_shape.shape, BF16), pltpu.VMEM((half, columns), BF16), dma((3, tiles))],
    )(first, first_got, *seconds, in_hbm(out_weight))
    partial_sum = call(add_kernel, "project_second", [vmem] * 3, sum_shape, 512 * MIB, 4 * MIB)(
        seconds_got[0], partial_sum, w_other
    )
    return call(
        functools.partial(last_kernel, cut * HEAD_SIZE),
        "project_last",
        [vmem] * 3 + [hbm],
        shape((number, columns), BF16),
        512 * MIB,
        4 * MIB,
        out_specs=hbm,
        scratch=[pltpu.VMEM((half, columns), BF16), dma((tiles,))],
        aliases={3: 0},
    )(seconds_got[1], partial_sum, w_other, begun)


def solution(mesh):
    in_specs = (P("ctx", "head"), P("ctx", "head"), P("ctx", "head"), P("ctx"), P(None, "head"))
    out_specs = P("ctx", "head")
    return jax.shard_map(shards, mesh=mesh, in_specs=in_specs, out_specs=out_specs, check_vma=False)
```

```python
import functools
import math

import jax
import jax.numpy as jnp
import numpy as np
from jax import lax
from jax.experimental import pallas as pl
from jax.experimental.pallas import tpu as pltpu
from jax.sharding import PartitionSpec as P

HEAD_SIZE = 128
LOWEST = -1e30
FAR = 1 << 16
MIB = 1 << 20
SCORE_SCALE = math.log2(math.e) / math.sqrt(HEAD_SIZE)
BF16, F32 = jnp.bfloat16, jnp.float32


def distance(rank, step, count):
    return jnp.where(rank >= step, step, count - step)


def waits_for_keys(rank):
    return (rank == 1) | (rank == 2)


def first_begin(rank, half):
    return pl.multiple_of(jnp.where(rank < 2, 0, half), half)


def half_positions(p_ref, rank, first):
    half = p_ref.shape[1] // 2
    early = (rank < 2) if first else (rank >= 2)
    return jnp.where(early, p_ref[:, :half], p_ref[:, half:])


def column(row, width):
    return jnp.broadcast_to(row, (width, row.shape[1])).T


def tile_biases(position_row, kinds):
    number = position_row.shape[1]
    position = column(position_row, number)
    query = lax.broadcasted_iota(jnp.int32, (number, number), 0)
    key = lax.broadcasted_iota(jnp.int32, (number, number), 1)
    ahead = key - query
    reach = ahead + position
    found = []
    for pieces, diagonal in kinds:
        allowed = reach >= pieces * number
        if diagonal:
            allowed = allowed & (ahead <= 0)
        found.append(jnp.where(allowed, 0.0, LOWEST).astype(F32))
    return found


def sine_cosine(angle):
    turns = jnp.floor(angle * (2.0 / math.pi) + 0.5)
    rest = ((angle - turns * 1.5703125) - turns * 4.837512969970703e-4) - turns * 7.549789954891888e-8
    square = rest * rest
    sine = ((-1.9515295891e-4 * square + 8.3321608736e-3) * square - 1.6666654611e-1) * square * rest + rest
    cosine = (
        ((2.443315711809948e-5 * square - 1.388731625493765e-3) * square + 4.166664568298827e-2) * square * square
        - 0.5 * square
        + 1.0
    )
    quarter = turns.astype(jnp.int32)
    swap = (quarter & 1) == 1
    out_sine = jnp.where(swap, cosine, sine)
    out_cosine = jnp.where(swap, sine, cosine)
    out_sine = jnp.where((quarter & 2) == 2, -out_sine, out_sine)
    out_cosine = jnp.where(((quarter + 1) & 2) == 2, -out_cosine, out_cosine)
    return out_sine, out_cosine


def turned(block, cosine, sinus):
    wide = block.astype(F32)
    return (wide * cosine + pltpu.roll(wide, HEAD_SIZE // 2, 1) * sinus).astype(BF16)


def scores_of(query, key, bias):
    raw = lax.dot_general(query, key, (((1,), (1,)), ((), ())), preferred_element_type=F32)
    return raw * SCORE_SCALE + bias


def weighted(weights, value):
    return jnp.dot(weights.astype(BF16), value, preferred_element_type=F32)


def spread(entries):
    return jnp.broadcast_to(entries, (entries.shape[0], HEAD_SIZE))


def with_ones(value):
    return jnp.concatenate([value, jnp.ones_like(value)], axis=1)


def head_slices(head, group, width):
    at = slice(head * HEAD_SIZE, (head + 1) * HEAD_SIZE)
    low = head // group * HEAD_SIZE
    return at, slice(low, low + HEAD_SIZE), slice(width + low, width + low + HEAD_SIZE)


def begin_state(query, keys, values, biases):
    scores = [scores_of(query, key, bias) for key, bias in zip(keys, biases)]
    top = jnp.max(functools.reduce(jnp.maximum, scores), axis=1, keepdims=True)
    weights = [jnp.exp2(score - top) for score in scores]
    both = functools.reduce(jnp.add, [weighted(w, value) for w, value in zip(weights, values)])
    return both[:, :HEAD_SIZE], spread(top), both[:, HEAD_SIZE:]


def added_tile(summed, top, total, query, key, value, bias):
    score = scores_of(query, key, bias)
    updated = jnp.maximum(top, spread(jnp.max(score, axis=1, keepdims=True)))
    weights = jnp.exp2(score - jnp.concatenate([updated] * (score.shape[1] // HEAD_SIZE), axis=1))
    factor = jnp.exp2(top - updated)
    both = weighted(weights, value)
    return summed * factor + both[:, :HEAD_SIZE], updated, total * factor + both[:, HEAD_SIZE:]


def finished(state):
    summed, _, total = state
    return (summed * (1.0 / total)).astype(BF16)


def keys_kernel(
    count, k_hbm, v_hbm, q_hbm, p_hbm, f_hbm, near_ref, next_ref, rot_ref, v_ref, q_ref, p_ref, cos_ref, sin_ref,
    k_ref, f_ref, sems,
):
    pairs = ((p_hbm, p_ref), (f_hbm, f_ref), (k_hbm, k_ref), (v_hbm, v_ref), (q_hbm, q_ref))
    copies = [pltpu.make_async_copy(source, target, sems.at[i]) for i, (source, target) in enumerate(pairs)]
    for copy in copies:
        copy.start()
    rank = lax.axis_index("ctx")
    half = k_ref.shape[0] // 2
    width = k_ref.shape[1]
    copies[0].wait()
    copies[1].wait()
    position = p_ref[...].astype(F32)
    early = column(position[:, :half], HEAD_SIZE)
    late = column(position[:, half:], HEAD_SIZE)
    lane = lax.broadcasted_iota(jnp.int32, (half, HEAD_SIZE), 1)
    front = lane < HEAD_SIZE // 2
    sine, cosine = sine_cosine(jnp.where(front, early, late) * f_ref[...])
    sine_other = pltpu.roll(sine, HEAD_SIZE // 2, 1)
    cosine_other = pltpu.roll(cosine, HEAD_SIZE // 2, 1)
    cos_ref[:half] = jnp.where(front, cosine, cosine_other)
    cos_ref[half:] = jnp.where(front, cosine_other, cosine)
    sin_ref[:half] = jnp.where(front, -sine, sine_other)
    sin_ref[half:] = jnp.where(front, -sine_other, sine)
    copies[2].wait()
    for head in range(width // HEAD_SIZE):
        at = slice(head * HEAD_SIZE, (head + 1) * HEAD_SIZE)
        rot_ref[:, at] = turned(k_ref[:, at], cos_ref[...], sin_ref[...])
    copies[3].wait()
    wrap = (rank % 2 == 1) & (rank + 3 >= count)
    rows = pl.ds(pl.multiple_of(jnp.where(wrap, half, 0), half), half)
    near_ref[:, :width] = rot_ref[rows, :]
    near_ref[:, width:] = v_ref[rows, :]
    rows = pl.ds(pl.multiple_of(jnp.where(rank + 2 >= count, half, 0), half), half)
    next_ref[:, :width] = rot_ref[rows, :]
    next_ref[:, width:] = v_ref[rows, :]
    copies[4].wait()


def own_kernel(group, q_ref, k_ref, v_ref, p_ref, cos_ref, sin_ref, out_ref, rot_ref, acc_ref, top_ref, sum_ref):
    rank = lax.axis_index("ctx")
    half = q_ref.shape[0] // 2
    rows = pl.ds(first_begin(rank, half), half)
    biases = tile_biases(half_positions(p_ref, rank, True), [(0, True)])
    for head in range(q_ref.shape[1] // HEAD_SIZE):
        at, shared, _ = head_slices(head, group, 0)
        query = turned(q_ref[rows, at], cos_ref[rows, :], sin_ref[rows, :])
        rot_ref[:, at] = query
        if head % group == 0:
            value = with_ones(v_ref[rows, shared])
        summed, top, total = begin_state(query, [k_ref[rows, shared]], [value], biases)
        acc_ref[:, at] = summed
        top_ref[:, at] = top
        sum_ref[:, at] = total
        out_ref[:, at] = (summed * (1.0 / total)).astype(BF16)


def first_kernel(count, group, heads, own_ref, rot_ref, kv_ref, p_ref, acc_ref, top_ref, sum_ref, out_ref):
    rank = lax.axis_index("ctx")
    width = kv_ref.shape[1] // 2
    step = jnp.where(rank % 2 == 1, 1, 3)
    used = waits_for_keys(rank)

    @pl.when(used)
    def _():
        biases = tile_biases(half_positions(p_ref, rank, True), [(distance(rank, step, count), False)])
        for number, head in enumerate(heads):
            at, key_at, value_at = head_slices(head, group, width)
            state = acc_ref[:, at], top_ref[:, at], sum_ref[:, at]
            if number == 0 or head % group == 0:
                value = with_ones(kv_ref[:, value_at])
            state = added_tile(*state, rot_ref[:, at], kv_ref[:, key_at], value, *biases)
            out_ref[:, number * HEAD_SIZE : (number + 1) * HEAD_SIZE] = finished(state)

    @pl.when(jnp.logical_not(used))
    def _():
        out_ref[...] = own_ref[:, heads[0] * HEAD_SIZE : (heads[-1] + 1) * HEAD_SIZE]


def second_kernel(
    count, group, q_ref, k_ref, v_ref, p_ref, cos_ref, sin_ref, kv_ref, rot_ref, acc_ref, top_ref, sum_ref
):
    rank = lax.axis_index("ctx")
    half = q_ref.shape[0] // 2
    width = k_ref.shape[1]
    rows = pl.ds(pl.multiple_of(half - first_begin(rank, half), half), half)
    step = jnp.where(rank % 2 == 1, 1, 3)
    reach = jnp.where(waits_for_keys(rank), FAR, distance(rank, step, count))
    biases = tile_biases(half_positions(p_ref, rank, False), [(0, True), (reach, False)])
    for head in range(q_ref.shape[1] // HEAD_SIZE):
        at, key_at, value_at = head_slices(head, group, width)
        query = turned(q_ref[rows, at], cos_ref[rows, :], sin_ref[rows, :])
        rot_ref[:, at] = query
        keys = [k_ref[rows, key_at], kv_ref[:, key_at]]
        if head % group == 0:
            values = [with_ones(v_ref[rows, key_at]), with_ones(kv_ref[:, value_at])]
        acc_ref[:, at], top_ref[:, at], sum_ref[:, at] = begin_state(query, keys, values, biases)


def next_kernel(count, group, rot_ref, kv_ref, p_ref, acc_ref, top_ref, sum_ref, *outs):
    rank = lax.axis_index("ctx")
    width = kv_ref.shape[1] // 2
    biases = tile_biases(half_positions(p_ref, rank, False), [(distance(rank, 2, count), False)])
    for head in range(rot_ref.shape[1] // HEAD_SIZE):
        at, key_at, value_at = head_slices(head, group, width)
        state = acc_ref[:, at], top_ref[:, at], sum_ref[:, at]
        if head % group == 0:
            value = with_ones(kv_ref[:, value_at])
        state = added_tile(*state, rot_ref[:, at], kv_ref[:, key_at], value, *biases)
        for out_ref, entries in zip(outs, state):
            out_ref[:, at] = entries


def third_kernel(count, group, heads, rot_ref, kv_ref, p_ref, acc_ref, top_ref, sum_ref, out_ref):
    rank = lax.axis_index("ctx")
    width = kv_ref.shape[1] // 2
    step = jnp.where(rank % 2 == 1, 3, 1)
    biases = tile_biases(half_positions(p_ref, rank, False), [(distance(rank, step, count), False)])
    for number, head in enumerate(heads):
        at, key_at, value_at = head_slices(head, group, width)
        state = acc_ref[:, at], top_ref[:, at], sum_ref[:, at]
        if number == 0 or head % group == 0:
            value = with_ones(kv_ref[:, value_at])
        state = added_tile(*state, rot_ref[:, at], kv_ref[:, key_at], value, *biases)
        out_ref[:, number * HEAD_SIZE : (number + 1) * HEAD_SIZE] = finished(state)


def dot(left, right):
    return jnp.dot(left, right, preferred_element_type=F32)


TILE = 512


def project_kernel(own_ref, got_ref, second0_ref, second1_ref, w_hbm, out_hbm, part_ref, other_ref, mine_ref, held_ref, sems):
    rank = lax.axis_index("ctx")
    side = lax.axis_index("head")
    half, depth = own_ref.shape
    rows = pl.ds(first_begin(rank, half), half)
    tiles = [slice(start, start + TILE) for start in range(0, mine_ref.shape[1], TILE)]
    weights = []
    for tile, at in enumerate(tiles):
        for number, (part, ref) in enumerate(((side, mine_ref), (1 - side, other_ref))):
            source = w_hbm.at[pl.ds(pl.multiple_of(part * depth, depth), depth), at]
            weights.append(pltpu.make_async_copy(source, ref.at[:, at], sems.at[number, tile]))
            weights[-1].start()
    second = jnp.concatenate([second0_ref[...], second1_ref[...]], axis=1)
    stacked = jnp.concatenate([own_ref[...], second], axis=0)
    copies = []
    for tile, at in enumerate(tiles):
        weights[2 * tile].wait()
        both = dot(stacked, mine_ref[:, at])
        part_ref[:, at] = both[half:]
        weights[2 * tile + 1].wait()
        held_ref[:, at] = (both[:half] + dot(got_ref[...], other_ref[:, at])).astype(BF16)
        copies.append(pltpu.make_async_copy(held_ref.at[:, at], out_hbm.at[rows, at], sems.at[2, tile]))
        copies[-1].start()
    for copy in copies:
        copy.wait()


def add_kernel(got_ref, part_ref, w_ref, out_ref):
    depth = got_ref.shape[1]
    for start in range(0, w_ref.shape[1], TILE):
        at = slice(start, start + TILE)
        out_ref[:, at] = part_ref[:, at] + dot(got_ref[...], w_ref[:depth, at])


def last_kernel(begin, got_ref, part_ref, w_ref, begun_hbm, out_hbm, held_ref, sems):
    del begun_hbm
    rank = lax.axis_index("ctx")
    half, depth = got_ref.shape
    out_rows = pl.ds(pl.multiple_of(half - first_begin(rank, half), half), half)
    copies = []
    for tile in range(w_ref.shape[1] // TILE):
        at = slice(tile * TILE, (tile + 1) * TILE)
        added = dot(got_ref[...], w_ref[begin : begin + depth, at])
        held_ref[:, at] = (part_ref[:, at] + added).astype(BF16)
        copies.append(pltpu.make_async_copy(held_ref.at[:, at], out_hbm.at[out_rows, at], sems.at[tile]))
        copies[-1].start()
    for copy in copies:
        copy.wait()


def shards(queries, keys, values, positions, out_weight):
    number, width = queries.shape
    half = number // 2
    count = lax.axis_size("ctx")
    group = width // keys.shape[1]
    columns = out_weight.shape[1]
    tiles = columns // TILE
    in_hbm = lambda array: pltpu.with_memory_space_constraint(array, pltpu.HBM)
    position_row = positions.reshape(1, number)
    table = np.power(500000.0, -2.0 * np.arange(HEAD_SIZE // 2) / HEAD_SIZE).astype(np.float32)
    frequency = jnp.asarray(np.concatenate([table, table])[None, :])
    shape = jax.ShapeDtypeStruct
    vmem = pl.BlockSpec(memory_space=pltpu.VMEM)
    hbm = pl.BlockSpec(memory_space=pltpu.HBM)
    dma = pltpu.SemaphoreType.DMA

    def call(body, name, ins, outs, flops, nbytes, out_specs=None, scratch=(), aliases={}):
        return pl.pallas_call(
            body,
            name=name,
            in_specs=ins,
            out_shape=outs,
            out_specs=out_specs if out_specs is not None else jax.tree.map(lambda _: vmem, outs),
            scratch_shapes=scratch,
            input_output_aliases=aliases,
            compiler_params=pltpu.CompilerParams(vmem_limit_bytes=32 * MIB),
            cost_estimate=pl.CostEstimate(flops=flops // 1024, bytes_accessed=nbytes // 1024, transcendentals=0),
        )

    def pairs(target_of):
        found = [(source, target_of(source) % count) for source in range(count)]
        assert sorted(target for _, target in found) == list(range(count))
        return found

    def swapped(array):
        return lax.ppermute(array, "head", [(0, 1), (1, 0)])

    kv_shape = shape((half, 2 * keys.shape[1]), BF16)
    table_shape = shape((number, HEAD_SIZE), F32)
    rows_shape, state = shape((half, width), BF16), shape((half, width), F32)
    weights_shape = shape((width, columns), BF16)
    near, onward, k_rot, v, q, p, cosine, sinus = call(
        functools.partial(keys_kernel, count),
        "rotate_keys",
        [hbm] * 5,
        [kv_shape, kv_shape]
        + [shape(keys.shape, BF16)] * 2
        + [shape(queries.shape, BF16), shape((1, number), jnp.int32), table_shape, table_shape],
        4 * MIB,
        4 * MIB,
        scratch=[pltpu.VMEM(keys.shape, BF16), pltpu.VMEM((1, HEAD_SIZE), F32), dma((5,))],
    )(*(in_hbm(array) for array in (keys, values, queries, position_row, frequency)))
    near_got = lax.ppermute(near, "ctx", pairs(lambda r: r + 3 if r % 2 else r + 1))
    own, rot, acc, top, total = call(
        functools.partial(own_kernel, group),
        "own_tiles",
        [vmem] * 6,
        [rows_shape, rows_shape, state, state, state],
        256 * MIB,
        4 * MIB,
    )(q, k_rot, v, p, cosine, sinus)
    onward, rot = lax.optimization_barrier((onward, rot))
    next_got = lax.ppermute(onward, "ctx", pairs(lambda r: r + 2))
    heads = width // HEAD_SIZE
    cut = heads // 2
    parts = range(cut), range(cut, heads)
    first = call(
        functools.partial(first_kernel, count, group, range(heads)),
        "first_rows",
        [vmem] * 7,
        rows_shape,
        256 * MIB,
        4 * MIB,
    )(own, rot, near_got, p, acc, top, total)
    first_got = swapped(first)
    q, first = lax.optimization_barrier((q, first))
    rot, *state_now = call(
        functools.partial(second_kernel, count, group),
        "second_rows",
        [vmem] * 7,
        [rows_shape, state, state, state],
        1024 * MIB,
        12 * MIB,
    )(q, k_rot, v, p, cosine, sinus, near_got)
    rot, next_got = lax.optimization_barrier((rot, next_got))
    last_got = lax.ppermute(next_got, "ctx", pairs(lambda r: r + 1 - 2 * (r % 2)))
    state_now = call(
        functools.partial(next_kernel, count, group),
        "next_tile",
        [vmem] * 6,
        [state, state, state],
        512 * MIB,
        4 * MIB,
        aliases={3: 0, 4: 1, 5: 2},
    )(rot, next_got, p, *state_now)
    seconds, seconds_got = [], []
    for part in parts:
        second = call(
            functools.partial(third_kernel, count, group, part),
            "last_tile",
            [vmem] * 6,
            shape((half, len(part) * HEAD_SIZE), BF16),
            256 * MIB,
            4 * MIB,
        )(rot, last_got, p, *state_now)
        seconds_got.append(swapped(second))
        rot, second = lax.optimization_barrier((rot, second))
        seconds.append(second)
    sum_shape = shape((half, columns), F32)
    begun, partial_sum, w_other = call(
        project_kernel,
        "project_first",
        [vmem] * 4 + [hbm],
        [shape((number, columns), BF16), sum_shape, weights_shape],
        3072 * MIB,
        8 * MIB,
        out_specs=[hbm, vmem, vmem],
        scratch=[pltpu.VMEM(weights_shape.shape, BF16), pltpu.VMEM((half, columns), BF16), dma((3, tiles))],
    )(first, first_got, *seconds, in_hbm(out_weight))
    partial_sum = call(add_kernel, "project_second", [vmem] * 3, sum_shape, 512 * MIB, 4 * MIB)(
        seconds_got[0], partial_sum, w_other
    )
    return call(
        functools.partial(last_kernel, cut * HEAD_SIZE),
        "project_last",
        [vmem] * 3 + [hbm],
        shape((number, columns), BF16),
        512 * MIB,
        4 * MIB,
        out_specs=hbm,
        scratch=[pltpu.VMEM((half, columns), BF16), dma((tiles,))],
        aliases={3: 0},
    )(seconds_got[1], partial_sum, w_other, begun)


def solution(mesh):
    in_specs = (P("ctx", "head"), P("ctx", "head"), P("ctx", "head"), P("ctx"), P(None, "head"))
    out_specs = P("ctx", "head")
    return jax.shard_map(shards, mesh=mesh, in_specs=in_specs, out_specs=out_specs, check_vma=False)
```

```python
import functools
import math

import jax
import jax.numpy as jnp
import numpy as np
from jax import lax
from jax.experimental import pallas as pl
from jax.experimental.pallas import tpu as pltpu
from jax.sharding import PartitionSpec as P

HEAD_SIZE = 128
LOWEST = -1e30
FAR = 1 << 16
MIB = 1 << 20
SCORE_SCALE = math.log2(math.e) / math.sqrt(HEAD_SIZE)
BF16, F32 = jnp.bfloat16, jnp.float32


def distance(rank, step, count):
    return jnp.where(rank >= step, step, count - step)


def waits_for_keys(rank):
    return (rank == 1) | (rank == 2)


def first_begin(rank, half):
    return pl.multiple_of(jnp.where(rank < 2, 0, half), half)


def half_positions(p_ref, rank, first):
    half = p_ref.shape[1] // 2
    early = (rank < 2) if first else (rank >= 2)
    return jnp.where(early, p_ref[:, :half], p_ref[:, half:])


def column(row, width):
    return jnp.broadcast_to(row, (width, row.shape[1])).T


def tile_biases(position_row, kinds):
    number = position_row.shape[1]
    position = column(position_row, number)
    query = lax.broadcasted_iota(jnp.int32, (number, number), 0)
    key = lax.broadcasted_iota(jnp.int32, (number, number), 1)
    ahead = key - query
    reach = ahead + position
    found = []
    for pieces, diagonal in kinds:
        allowed = reach >= pieces * number
        if diagonal:
            allowed = allowed & (ahead <= 0)
        found.append(jnp.where(allowed, 0.0, LOWEST).astype(F32))
    return found


def sine_cosine(angle):
    turns = jnp.floor(angle * (2.0 / math.pi) + 0.5)
    rest = ((angle - turns * 1.5703125) - turns * 4.837512969970703e-4) - turns * 7.549789954891888e-8
    square = rest * rest
    sine = ((-1.9515295891e-4 * square + 8.3321608736e-3) * square - 1.6666654611e-1) * square * rest + rest
    cosine = (
        ((2.443315711809948e-5 * square - 1.388731625493765e-3) * square + 4.166664568298827e-2) * square * square
        - 0.5 * square
        + 1.0
    )
    quarter = turns.astype(jnp.int32)
    swap = (quarter & 1) == 1
    out_sine = jnp.where(swap, cosine, sine)
    out_cosine = jnp.where(swap, sine, cosine)
    out_sine = jnp.where((quarter & 2) == 2, -out_sine, out_sine)
    out_cosine = jnp.where(((quarter + 1) & 2) == 2, -out_cosine, out_cosine)
    return out_sine, out_cosine


def turned(block, cosine, sinus):
    wide = block.astype(F32)
    return (wide * cosine + pltpu.roll(wide, HEAD_SIZE // 2, 1) * sinus).astype(BF16)


def scores_of(query, key, bias):
    raw = lax.dot_general(query, key, (((1,), (1,)), ((), ())), preferred_element_type=F32)
    return raw * SCORE_SCALE + bias


def weighted(weights, value):
    return jnp.dot(weights.astype(BF16), value, preferred_element_type=F32)


def spread(entries):
    return jnp.broadcast_to(entries, (entries.shape[0], HEAD_SIZE))


def with_ones(value):
    return jnp.concatenate([value, jnp.ones_like(value)], axis=1)


def head_slices(head, group, width):
    at = slice(head * HEAD_SIZE, (head + 1) * HEAD_SIZE)
    low = head // group * HEAD_SIZE
    return at, slice(low, low + HEAD_SIZE), slice(width + low, width + low + HEAD_SIZE)


def begin_state(query, keys, values, biases):
    scores = [scores_of(query, key, bias) for key, bias in zip(keys, biases)]
    top = jnp.max(functools.reduce(jnp.maximum, scores), axis=1, keepdims=True)
    weights = [jnp.exp2(score - top) for score in scores]
    both = functools.reduce(jnp.add, [weighted(w, value) for w, value in zip(weights, values)])
    return both[:, :HEAD_SIZE], spread(top), both[:, HEAD_SIZE:]


def added_tile(summed, top, total, query, key, value, bias):
    score = scores_of(query, key, bias)
    updated = jnp.maximum(top, spread(jnp.max(score, axis=1, keepdims=True)))
    weights = jnp.exp2(score - jnp.concatenate([updated] * (score.shape[1] // HEAD_SIZE), axis=1))
    factor = jnp.exp2(top - updated)
    both = weighted(weights, value)
    return summed * factor + both[:, :HEAD_SIZE], updated, total * factor + both[:, HEAD_SIZE:]


def finished(state):
    summed, _, total = state
    return (summed * (1.0 / total)).astype(BF16)


def keys_kernel(
    count, k_hbm, v_hbm, q_hbm, p_hbm, f_hbm, near_ref, next_ref, rot_ref, v_ref, q_ref, p_ref, cos_ref, sin_ref,
    k_ref, f_ref, sems,
):
    pairs = ((p_hbm, p_ref), (f_hbm, f_ref), (k_hbm, k_ref), (v_hbm, v_ref), (q_hbm, q_ref))
    copies = [pltpu.make_async_copy(source, target, sems.at[i]) for i, (source, target) in enumerate(pairs)]
    for copy in copies:
        copy.start()
    rank = lax.axis_index("ctx")
    half = k_ref.shape[0] // 2
    width = k_ref.shape[1]
    copies[0].wait()
    copies[1].wait()
    position = p_ref[...].astype(F32)
    early = column(position[:, :half], HEAD_SIZE)
    late = column(position[:, half:], HEAD_SIZE)
    lane = lax.broadcasted_iota(jnp.int32, (half, HEAD_SIZE), 1)
    front = lane < HEAD_SIZE // 2
    sine, cosine = sine_cosine(jnp.where(front, early, late) * f_ref[...])
    sine_other = pltpu.roll(sine, HEAD_SIZE // 2, 1)
    cosine_other = pltpu.roll(cosine, HEAD_SIZE // 2, 1)
    cos_ref[:half] = jnp.where(front, cosine, cosine_other)
    cos_ref[half:] = jnp.where(front, cosine_other, cosine)
    sin_ref[:half] = jnp.where(front, -sine, sine_other)
    sin_ref[half:] = jnp.where(front, -sine_other, sine)
    copies[2].wait()
    for head in range(width // HEAD_SIZE):
        at = slice(head * HEAD_SIZE, (head + 1) * HEAD_SIZE)
        rot_ref[:, at] = turned(k_ref[:, at], cos_ref[...], sin_ref[...])
    copies[3].wait()
    wrap = (rank % 2 == 1) & (rank + 3 >= count)
    rows = pl.ds(pl.multiple_of(jnp.where(wrap, half, 0), half), half)
    near_ref[:, :width] = rot_ref[rows, :]
    near_ref[:, width:] = v_ref[rows, :]
    rows = pl.ds(pl.multiple_of(jnp.where(rank + 2 >= count, half, 0), half), half)
    next_ref[:, :width] = rot_ref[rows, :]
    next_ref[:, width:] = v_ref[rows, :]
    copies[4].wait()


def own_kernel(group, q_ref, k_ref, v_ref, p_ref, cos_ref, sin_ref, out_ref, rot_ref, acc_ref, top_ref, sum_ref):
    rank = lax.axis_index("ctx")
    half = q_ref.shape[0] // 2
    rows = pl.ds(first_begin(rank, half), half)
    biases = tile_biases(half_positions(p_ref, rank, True), [(0, True)])
    for head in range(q_ref.shape[1] // HEAD_SIZE):
        at, shared, _ = head_slices(head, group, 0)
        query = turned(q_ref[rows, at], cos_ref[rows, :], sin_ref[rows, :])
        rot_ref[:, at] = query
        if head % group == 0:
            key = k_ref[rows, shared]
            value = with_ones(v_ref[rows, shared])
        for low, high in ((0, half // 2), (half // 2, half)):
            part = slice(low, high)
            summed, top, total = begin_state(query[part], [key[:high]], [value[:high]], [biases[0][part, :high]])
            acc_ref[part, at] = summed
            top_ref[part, at] = top
            sum_ref[part, at] = total
            out_ref[part, at] = (summed * (1.0 / total)).astype(BF16)


def first_kernel(count, group, heads, own_ref, rot_ref, kv_ref, p_ref, acc_ref, top_ref, sum_ref, out_ref):
    rank = lax.axis_index("ctx")
    width = kv_ref.shape[1] // 2
    step = jnp.where(rank % 2 == 1, 1, 3)
    used = waits_for_keys(rank)

    @pl.when(used)
    def _():
        biases = tile_biases(half_positions(p_ref, rank, True), [(distance(rank, step, count), False)])
        for number, head in enumerate(heads):
            at, key_at, value_at = head_slices(head, group, width)
            state = acc_ref[:, at], top_ref[:, at], sum_ref[:, at]
            if number == 0 or head % group == 0:
                value = with_ones(kv_ref[:, value_at])
            state = added_tile(*state, rot_ref[:, at], kv_ref[:, key_at], value, *biases)
            out_ref[:, number * HEAD_SIZE : (number + 1) * HEAD_SIZE] = finished(state)

    @pl.when(jnp.logical_not(used))
    def _():
        out_ref[...] = own_ref[:, heads[0] * HEAD_SIZE : (heads[-1] + 1) * HEAD_SIZE]


def second_kernel(
    count, group, q_ref, k_ref, v_ref, p_ref, cos_ref, sin_ref, kv_ref, rot_ref, acc_ref, top_ref, sum_ref
):
    rank = lax.axis_index("ctx")
    half = q_ref.shape[0] // 2
    width = k_ref.shape[1]
    rows = pl.ds(pl.multiple_of(half - first_begin(rank, half), half), half)
    step = jnp.where(rank % 2 == 1, 1, 3)
    reach = jnp.where(waits_for_keys(rank), FAR, distance(rank, step, count))
    biases = tile_biases(half_positions(p_ref, rank, False), [(0, True), (reach, False)])
    for head in range(q_ref.shape[1] // HEAD_SIZE):
        at, key_at, value_at = head_slices(head, group, width)
        query = turned(q_ref[rows, at], cos_ref[rows, :], sin_ref[rows, :])
        rot_ref[:, at] = query
        keys = [k_ref[rows, key_at], kv_ref[:, key_at]]
        if head % group == 0:
            values = [with_ones(v_ref[rows, key_at]), with_ones(kv_ref[:, value_at])]
        acc_ref[:, at], top_ref[:, at], sum_ref[:, at] = begin_state(query, keys, values, biases)


def next_kernel(count, group, rot_ref, kv_ref, p_ref, acc_ref, top_ref, sum_ref, *outs):
    rank = lax.axis_index("ctx")
    width = kv_ref.shape[1] // 2
    biases = tile_biases(half_positions(p_ref, rank, False), [(distance(rank, 2, count), False)])
    for head in range(rot_ref.shape[1] // HEAD_SIZE):
        at, key_at, value_at = head_slices(head, group, width)
        state = acc_ref[:, at], top_ref[:, at], sum_ref[:, at]
        if head % group == 0:
            value = with_ones(kv_ref[:, value_at])
        state = added_tile(*state, rot_ref[:, at], kv_ref[:, key_at], value, *biases)
        for out_ref, entries in zip(outs, state):
            out_ref[:, at] = entries


def third_kernel(count, group, heads, rot_ref, kv_ref, p_ref, acc_ref, top_ref, sum_ref, out_ref):
    rank = lax.axis_index("ctx")
    width = kv_ref.shape[1] // 2
    step = jnp.where(rank % 2 == 1, 3, 1)
    biases = tile_biases(half_positions(p_ref, rank, False), [(distance(rank, step, count), False)])
    for number, head in enumerate(heads):
        at, key_at, value_at = head_slices(head, group, width)
        state = acc_ref[:, at], top_ref[:, at], sum_ref[:, at]
        if number == 0 or head % group == 0:
            value = with_ones(kv_ref[:, value_at])
        state = added_tile(*state, rot_ref[:, at], kv_ref[:, key_at], value, *biases)
        out_ref[:, number * HEAD_SIZE : (number + 1) * HEAD_SIZE] = finished(state)


def dot(left, right):
    return jnp.dot(left, right, preferred_element_type=F32)


TILE = 512
LAST_TILE = 256


def project_kernel(own_ref, got_ref, second0_ref, second1_ref, second2_ref, w_hbm, out_hbm, part_ref, other_ref, mine_ref, held_ref, sems):
    rank = lax.axis_index("ctx")
    side = lax.axis_index("head")
    half, depth = own_ref.shape
    rows = pl.ds(first_begin(rank, half), half)
    tiles = [slice(start, start + TILE) for start in range(0, mine_ref.shape[1], TILE)]
    weights = []
    for tile, at in enumerate(tiles):
        for number, (part, ref) in enumerate(((side, mine_ref), (1 - side, other_ref))):
            source = w_hbm.at[pl.ds(pl.multiple_of(part * depth, depth), depth), at]
            weights.append(pltpu.make_async_copy(source, ref.at[:, at], sems.at[number, tile]))
            weights[-1].start()
    second = jnp.concatenate([second0_ref[...], second1_ref[...], second2_ref[...]], axis=1)
    stacked = jnp.concatenate([own_ref[...], second], axis=0)
    copies = []
    for tile, at in enumerate(tiles):
        weights[2 * tile].wait()
        both = dot(stacked, mine_ref[:, at])
        part_ref[:, at] = both[half:]
        weights[2 * tile + 1].wait()
        held_ref[:, at] = (both[:half] + dot(got_ref[...], other_ref[:, at])).astype(BF16)
        copies.append(pltpu.make_async_copy(held_ref.at[:, at], out_hbm.at[rows, at], sems.at[2, tile]))
        copies[-1].start()
    for copy in copies:
        copy.wait()


def add_kernel(begin, got_ref, part_ref, w_ref, out_ref):
    end = begin + got_ref.shape[1]
    for start in range(0, w_ref.shape[1], TILE):
        at = slice(start, start + TILE)
        out_ref[:, at] = part_ref[:, at] + dot(got_ref[...], w_ref[begin:end, at])


def last_kernel(begin, got_ref, part_ref, w_ref, begun_hbm, out_hbm, held_ref, sems):
    del begun_hbm
    rank = lax.axis_index("ctx")
    half, depth = got_ref.shape
    out_rows = pl.ds(pl.multiple_of(half - first_begin(rank, half), half), half)
    copies = []
    for tile in range(w_ref.shape[1] // LAST_TILE):
        at = slice(tile * LAST_TILE, (tile + 1) * LAST_TILE)
        added = dot(got_ref[...], w_ref[begin : begin + depth, at])
        held_ref[:, at] = (part_ref[:, at] + added).astype(BF16)
        copies.append(pltpu.make_async_copy(held_ref.at[:, at], out_hbm.at[out_rows, at], sems.at[tile]))
        copies[-1].start()
    for copy in copies:
        copy.wait()


def shards(queries, keys, values, positions, out_weight):
    number, width = queries.shape
    half = number // 2
    count = lax.axis_size("ctx")
    group = width // keys.shape[1]
    columns = out_weight.shape[1]
    tiles = columns // TILE
    in_hbm = lambda array: pltpu.with_memory_space_constraint(array, pltpu.HBM)
    position_row = positions.reshape(1, number)
    table = np.power(500000.0, -2.0 * np.arange(HEAD_SIZE // 2) / HEAD_SIZE).astype(np.float32)
    frequency = jnp.asarray(np.concatenate([table, table])[None, :])
    shape = jax.ShapeDtypeStruct
    vmem = pl.BlockSpec(memory_space=pltpu.VMEM)
    hbm = pl.BlockSpec(memory_space=pltpu.HBM)
    dma = pltpu.SemaphoreType.DMA

    def call(body, name, ins, outs, flops, nbytes, out_specs=None, scratch=(), aliases={}):
        return pl.pallas_call(
            body,
            name=name,
            in_specs=ins,
            out_shape=outs,
            out_specs=out_specs if out_specs is not None else jax.tree.map(lambda _: vmem, outs),
            scratch_shapes=scratch,
            input_output_aliases=aliases,
            compiler_params=pltpu.CompilerParams(vmem_limit_bytes=32 * MIB),
            cost_estimate=pl.CostEstimate(flops=flops // 1024, bytes_accessed=nbytes // 1024, transcendentals=0),
        )

    def pairs(target_of):
        found = [(source, target_of(source) % count) for source in range(count)]
        assert sorted(target for _, target in found) == list(range(count))
        return found

    def swapped(array):
        return lax.ppermute(array, "head", [(0, 1), (1, 0)])

    kv_shape = shape((half, 2 * keys.shape[1]), BF16)
    table_shape = shape((number, HEAD_SIZE), F32)
    rows_shape, state = shape((half, width), BF16), shape((half, width), F32)
    weights_shape = shape((width, columns), BF16)
    near, onward, k_rot, v, q, p, cosine, sinus = call(
        functools.partial(keys_kernel, count),
        "rotate_keys",
        [hbm] * 5,
        [kv_shape, kv_shape]
        + [shape(keys.shape, BF16)] * 2
        + [shape(queries.shape, BF16), shape((1, number), jnp.int32), table_shape, table_shape],
        4 * MIB,
        4 * MIB,
        scratch=[pltpu.VMEM(keys.shape, BF16), pltpu.VMEM((1, HEAD_SIZE), F32), dma((5,))],
    )(*(in_hbm(array) for array in (keys, values, queries, position_row, frequency)))
    near_got = lax.ppermute(near, "ctx", pairs(lambda r: r + 3 if r % 2 else r + 1))
    own, rot, acc, top, total = call(
        functools.partial(own_kernel, group),
        "own_tiles",
        [vmem] * 6,
        [rows_shape, rows_shape, state, state, state],
        256 * MIB,
        4 * MIB,
    )(q, k_rot, v, p, cosine, sinus)
    onward, rot = lax.optimization_barrier((onward, rot))
    next_got = lax.ppermute(onward, "ctx", pairs(lambda r: r + 2))
    heads = width // HEAD_SIZE
    cut = heads // 2
    parts = range(cut), range(cut, heads - 1), range(heads - 1, heads)
    first = call(
        functools.partial(first_kernel, count, group, range(heads)),
        "first_rows",
        [vmem] * 7,
        rows_shape,
        256 * MIB,
        4 * MIB,
    )(own, rot, near_got, p, acc, top, total)
    first_got = swapped(first)
    q, first = lax.optimization_barrier((q, first))
    rot, *state_now = call(
        functools.partial(second_kernel, count, group),
        "second_rows",
        [vmem] * 7,
        [rows_shape, state, state, state],
        1024 * MIB,
        12 * MIB,
    )(q, k_rot, v, p, cosine, sinus, near_got)
    rot, next_got = lax.optimization_barrier((rot, next_got))
    last_got = lax.ppermute(next_got, "ctx", pairs(lambda r: r + 1 - 2 * (r % 2)))
    state_now = call(
        functools.partial(next_kernel, count, group),
        "next_tile",
        [vmem] * 6,
        [state, state, state],
        512 * MIB,
        4 * MIB,
        aliases={3: 0, 4: 1, 5: 2},
    )(rot, next_got, p, *state_now)
    seconds, seconds_got = [], []
    for part in parts:
        second = call(
            functools.partial(third_kernel, count, group, part),
            "last_tile",
            [vmem] * 6,
            shape((half, len(part) * HEAD_SIZE), BF16),
            256 * MIB,
            4 * MIB,
        )(rot, last_got, p, *state_now)
        seconds_got.append(swapped(second))
        rot, second = lax.optimization_barrier((rot, second))
        seconds.append(second)
    sum_shape = shape((half, columns), F32)
    begun, partial_sum, w_other = call(
        project_kernel,
        "project_first",
        [vmem] * 5 + [hbm],
        [shape((number, columns), BF16), sum_shape, weights_shape],
        3072 * MIB,
        8 * MIB,
        out_specs=[hbm, vmem, vmem],
        scratch=[pltpu.VMEM(weights_shape.shape, BF16), pltpu.VMEM((half, columns), BF16), dma((3, tiles))],
    )(first, first_got, *seconds, in_hbm(out_weight))
    for part, got in zip(parts[:-1], seconds_got):
        partial_sum = call(
            functools.partial(add_kernel, part[0] * HEAD_SIZE),
            "project_second",
            [vmem] * 3,
            sum_shape,
            512 * MIB,
            4 * MIB,
        )(got, partial_sum, w_other)
    return call(
        functools.partial(last_kernel, parts[-1][0] * HEAD_SIZE),
        "project_last",
        [vmem] * 3 + [hbm],
        shape((number, columns), BF16),
        512 * MIB,
        4 * MIB,
        out_specs=hbm,
        scratch=[pltpu.VMEM((half, columns), BF16), dma((columns // LAST_TILE,))],
        aliases={3: 0},
    )(seconds_got[-1], partial_sum, w_other, begun)


def solution(mesh):
    in_specs = (P("ctx", "head"), P("ctx", "head"), P("ctx", "head"), P("ctx"), P(None, "head"))
    out_specs = P("ctx", "head")
    return jax.shard_map(shards, mesh=mesh, in_specs=in_specs, out_specs=out_specs, check_vma=False)
```

```python
import functools
import math

import jax
import jax.numpy as jnp
import numpy as np
from jax import lax
from jax.experimental import pallas as pl
from jax.experimental.pallas import tpu as pltpu
from jax.sharding import PartitionSpec as P

HEAD_SIZE = 128
LOWEST = -1e30
FAR = 1 << 16
MIB = 1 << 20
SCORE_SCALE = math.log2(math.e) / math.sqrt(HEAD_SIZE)
BF16, F32 = jnp.bfloat16, jnp.float32


def distance(rank, step, count):
    return jnp.where(rank >= step, step, count - step)


def waits_for_keys(rank):
    return (rank == 1) | (rank == 2)


def first_begin(rank, half):
    return pl.multiple_of(jnp.where(rank < 2, 0, half), half)


def half_positions(p_ref, rank, first):
    half = p_ref.shape[1] // 2
    early = (rank < 2) if first else (rank >= 2)
    return jnp.where(early, p_ref[:, :half], p_ref[:, half:])


def column(row, width):
    return jnp.broadcast_to(row, (width, row.shape[1])).T


def tile_biases(position_row, kinds):
    number = position_row.shape[1]
    position = column(position_row, number)
    query = lax.broadcasted_iota(jnp.int32, (number, number), 0)
    key = lax.broadcasted_iota(jnp.int32, (number, number), 1)
    ahead = key - query
    reach = ahead + position
    found = []
    for pieces, diagonal in kinds:
        allowed = reach >= pieces * number
        if diagonal:
            allowed = allowed & (ahead <= 0)
        found.append(jnp.where(allowed, 0.0, LOWEST).astype(F32))
    return found


def sine_cosine(angle):
    turns = jnp.floor(angle * (2.0 / math.pi) + 0.5)
    rest = ((angle - turns * 1.5703125) - turns * 4.837512969970703e-4) - turns * 7.549789954891888e-8
    square = rest * rest
    sine = ((-1.9515295891e-4 * square + 8.3321608736e-3) * square - 1.6666654611e-1) * square * rest + rest
    cosine = (
        ((2.443315711809948e-5 * square - 1.388731625493765e-3) * square + 4.166664568298827e-2) * square * square
        - 0.5 * square
        + 1.0
    )
    quarter = turns.astype(jnp.int32)
    swap = (quarter & 1) == 1
    out_sine = jnp.where(swap, cosine, sine)
    out_cosine = jnp.where(swap, sine, cosine)
    out_sine = jnp.where((quarter & 2) == 2, -out_sine, out_sine)
    out_cosine = jnp.where(((quarter + 1) & 2) == 2, -out_cosine, out_cosine)
    return out_sine, out_cosine


def turned(block, cosine, sinus):
    wide = block.astype(F32)
    return (wide * cosine + pltpu.roll(wide, HEAD_SIZE // 2, 1) * sinus).astype(BF16)


def scores_of(query, key, bias):
    raw = lax.dot_general(query, key, (((1,), (1,)), ((), ())), preferred_element_type=F32)
    return raw * SCORE_SCALE + bias


def weighted(weights, value):
    return jnp.dot(weights.astype(BF16), value, preferred_element_type=F32)


def spread(entries):
    return jnp.broadcast_to(entries, (entries.shape[0], HEAD_SIZE))


def with_ones(value):
    return jnp.concatenate([value, jnp.ones_like(value)], axis=1)


def head_slices(head, group, width):
    at = slice(head * HEAD_SIZE, (head + 1) * HEAD_SIZE)
    low = head // group * HEAD_SIZE
    return at, slice(low, low + HEAD_SIZE), slice(width + low, width + low + HEAD_SIZE)


def begin_state(query, keys, values, biases):
    scores = [scores_of(query, key, bias) for key, bias in zip(keys, biases)]
    top = jnp.max(functools.reduce(jnp.maximum, scores), axis=1, keepdims=True)
    weights = [jnp.exp2(score - top) for score in scores]
    both = functools.reduce(jnp.add, [weighted(w, value) for w, value in zip(weights, values)])
    return both[:, :HEAD_SIZE], spread(top), both[:, HEAD_SIZE:]


def added_tile(summed, top, total, query, key, value, bias):
    score = scores_of(query, key, bias)
    updated = jnp.maximum(top, spread(jnp.max(score, axis=1, keepdims=True)))
    weights = jnp.exp2(score - jnp.concatenate([updated] * (score.shape[1] // HEAD_SIZE), axis=1))
    factor = jnp.exp2(top - updated)
    both = weighted(weights, value)
    return summed * factor + both[:, :HEAD_SIZE], updated, total * factor + both[:, HEAD_SIZE:]


def finished(state):
    summed, _, total = state
    return (summed * (1.0 / total)).astype(BF16)


def keys_kernel(
    count, k_hbm, v_hbm, q_hbm, p_hbm, f_hbm, early_ref, near_ref, next_ref, rot_ref, v_ref, q_ref, p_ref, cos_ref, sin_ref,
    k_ref, f_ref, sems,
):
    pairs = ((p_hbm, p_ref), (f_hbm, f_ref), (k_hbm, k_ref), (v_hbm, v_ref), (q_hbm, q_ref))
    copies = [pltpu.make_async_copy(source, target, sems.at[i]) for i, (source, target) in enumerate(pairs)]
    for copy in copies:
        copy.start()
    rank = lax.axis_index("ctx")
    half = k_ref.shape[0] // 2
    width = k_ref.shape[1]
    copies[0].wait()
    copies[1].wait()
    position = p_ref[...].astype(F32)
    early = column(position[:, :half], HEAD_SIZE)
    late = column(position[:, half:], HEAD_SIZE)
    lane = lax.broadcasted_iota(jnp.int32, (half, HEAD_SIZE), 1)
    front = lane < HEAD_SIZE // 2
    sine, cosine = sine_cosine(jnp.where(front, early, late) * f_ref[...])
    sine_other = pltpu.roll(sine, HEAD_SIZE // 2, 1)
    cosine_other = pltpu.roll(cosine, HEAD_SIZE // 2, 1)
    cos_ref[:half] = jnp.where(front, cosine, cosine_other)
    cos_ref[half:] = jnp.where(front, cosine_other, cosine)
    sin_ref[:half] = jnp.where(front, -sine, sine_other)
    sin_ref[half:] = jnp.where(front, -sine_other, sine)
    copies[2].wait()
    for head in range(width // HEAD_SIZE):
        at = slice(head * HEAD_SIZE, (head + 1) * HEAD_SIZE)
        rot_ref[:, at] = turned(k_ref[:, at], cos_ref[...], sin_ref[...])
    copies[3].wait()
    wrap = (rank % 2 == 1) & (rank + 3 >= count)
    rows = pl.ds(pl.multiple_of(jnp.where(wrap, half, 0), half), half)
    near_ref[:, :width] = rot_ref[rows, :]
    near_ref[:, width:] = v_ref[rows, :]
    rows = pl.ds(pl.multiple_of(jnp.where(rank + 2 >= count, half, 0), half), half)
    next_ref[:, :width] = rot_ref[rows, :]
    next_ref[:, width:] = v_ref[rows, :]
    rows = pl.ds(first_begin(rank, half), half)
    begin, late = early_ref.shape[1] - 2 * HEAD_SIZE, slice(width - HEAD_SIZE, width)
    early_ref[:, begin : begin + HEAD_SIZE] = rot_ref[rows, late]
    early_ref[:, begin + HEAD_SIZE :] = v_ref[rows, late]
    copies[4].wait()
    low = q_ref.shape[1] - begin
    for head in range(begin // HEAD_SIZE):
        at = slice(head * HEAD_SIZE, (head + 1) * HEAD_SIZE)
        source = slice(low + head * HEAD_SIZE, low + (head + 1) * HEAD_SIZE)
        early_ref[:, at] = turned(q_ref[rows, source], cos_ref[rows, :], sin_ref[rows, :])


def own_kernel(group, q_ref, k_ref, v_ref, p_ref, cos_ref, sin_ref, out_ref, rot_ref, acc_ref, top_ref, sum_ref):
    rank = lax.axis_index("ctx")
    half = q_ref.shape[0] // 2
    rows = pl.ds(first_begin(rank, half), half)
    biases = tile_biases(half_positions(p_ref, rank, True), [(0, True)])
    for head in range(rot_ref.shape[1] // HEAD_SIZE):
        at, shared, _ = head_slices(head, group, 0)
        query = turned(q_ref[rows, at], cos_ref[rows, :], sin_ref[rows, :])
        rot_ref[:, at] = query
        if head % group == 0:
            key = k_ref[rows, shared]
            value = with_ones(v_ref[rows, shared])
        for low, high in ((0, half // 2), (half // 2, half)):
            part = slice(low, high)
            summed, top, total = begin_state(query[part], [key[:high]], [value[:high]], [biases[0][part, :high]])
            acc_ref[part, at] = summed
            top_ref[part, at] = top
            sum_ref[part, at] = total
            out_ref[part, at] = (summed * (1.0 / total)).astype(BF16)


def first_kernel(count, group, own_ref, rot_ref, kv_ref, p_ref, acc_ref, top_ref, sum_ref, out_ref):
    rank = lax.axis_index("ctx")
    width = kv_ref.shape[1] // 2
    depth = rot_ref.shape[1]
    step = jnp.where(rank % 2 == 1, 1, 3)
    used = waits_for_keys(rank)
    out_ref[:, depth : depth + HEAD_SIZE] = kv_ref[:, width - HEAD_SIZE : width]
    out_ref[:, depth + HEAD_SIZE :] = kv_ref[:, 2 * width - HEAD_SIZE :]

    @pl.when(used)
    def _():
        biases = tile_biases(half_positions(p_ref, rank, True), [(distance(rank, step, count), False)])
        for head in range(depth // HEAD_SIZE):
            at, key_at, value_at = head_slices(head, group, width)
            state = acc_ref[:, at], top_ref[:, at], sum_ref[:, at]
            if head % group == 0:
                value = with_ones(kv_ref[:, value_at])
            out_ref[:, at] = finished(added_tile(*state, rot_ref[:, at], kv_ref[:, key_at], value, *biases))

    @pl.when(jnp.logical_not(used))
    def _():
        out_ref[:, :depth] = own_ref[...]


def early_kernel(count, early_ref, near_ref, p_ref, out_ref):
    rank = lax.axis_index("ctx")
    depth = out_ref.shape[1]
    step = jnp.where(rank % 2 == 1, 1, 3)
    reach = jnp.where(waits_for_keys(rank), distance(rank, step, count), FAR)
    biases = tile_biases(half_positions(p_ref, rank, True), [(0, True), (reach, False)])
    keys, values = [], []
    for ref in (early_ref, near_ref):
        begin = ref.shape[1] - 2 * HEAD_SIZE
        keys.append(ref[:, begin : begin + HEAD_SIZE])
        values.append(with_ones(ref[:, begin + HEAD_SIZE :]))
    for head in range(depth // HEAD_SIZE):
        at = slice(head * HEAD_SIZE, (head + 1) * HEAD_SIZE)
        out_ref[:, at] = finished(begin_state(early_ref[:, at], keys, values, biases))


def second_kernel(
    count, group, q_ref, k_ref, v_ref, p_ref, cos_ref, sin_ref, kv_ref, w_hbm, rot_ref, acc_ref, top_ref, sum_ref, w_ref, sem
):
    copy = pltpu.make_async_copy(w_hbm, w_ref, sem)
    copy.start()
    rank = lax.axis_index("ctx")
    half = q_ref.shape[0] // 2
    width = k_ref.shape[1]
    rows = pl.ds(pl.multiple_of(half - first_begin(rank, half), half), half)
    step = jnp.where(rank % 2 == 1, 1, 3)
    reach = jnp.where(waits_for_keys(rank), FAR, distance(rank, step, count))
    biases = tile_biases(half_positions(p_ref, rank, False), [(0, True), (reach, False)])
    for head in range(q_ref.shape[1] // HEAD_SIZE):
        at, key_at, value_at = head_slices(head, group, width)
        query = turned(q_ref[rows, at], cos_ref[rows, :], sin_ref[rows, :])
        rot_ref[:, at] = query
        keys = [k_ref[rows, key_at], kv_ref[:, key_at]]
        if head % group == 0:
            values = [with_ones(v_ref[rows, key_at]), with_ones(kv_ref[:, value_at])]
        acc_ref[:, at], top_ref[:, at], sum_ref[:, at] = begin_state(query, keys, values, biases)
    copy.wait()


def next_kernel(count, group, rot_ref, kv_ref, p_ref, acc_ref, top_ref, sum_ref, *outs):
    rank = lax.axis_index("ctx")
    width = kv_ref.shape[1] // 2
    biases = tile_biases(half_positions(p_ref, rank, False), [(distance(rank, 2, count), False)])
    for head in range(rot_ref.shape[1] // HEAD_SIZE):
        at, key_at, value_at = head_slices(head, group, width)
        state = acc_ref[:, at], top_ref[:, at], sum_ref[:, at]
        if head % group == 0:
            value = with_ones(kv_ref[:, value_at])
        state = added_tile(*state, rot_ref[:, at], kv_ref[:, key_at], value, *biases)
        for out_ref, entries in zip(outs, state):
            out_ref[:, at] = entries


def third_kernel(count, group, heads, rot_ref, kv_ref, p_ref, acc_ref, top_ref, sum_ref, out_ref):
    rank = lax.axis_index("ctx")
    width = kv_ref.shape[1] // 2
    step = jnp.where(rank % 2 == 1, 3, 1)
    biases = tile_biases(half_positions(p_ref, rank, False), [(distance(rank, step, count), False)])
    for number, head in enumerate(heads):
        at, key_at, value_at = head_slices(head, group, width)
        state = acc_ref[:, at], top_ref[:, at], sum_ref[:, at]
        if number == 0 or head % group == 0:
            value = with_ones(kv_ref[:, value_at])
        state = added_tile(*state, rot_ref[:, at], kv_ref[:, key_at], value, *biases)
        out_ref[:, number * HEAD_SIZE : (number + 1) * HEAD_SIZE] = finished(state)


def dot(left, right):
    return jnp.dot(left, right, preferred_element_type=F32)


TILE = 512
LAST_TILE = 256


def other_rows(w_ref, begin, end):
    depth = w_ref.shape[0] // 2
    base = (1 - lax.axis_index("head")) * depth
    return pl.ds(pl.multiple_of(base + begin, HEAD_SIZE), end - begin)


def project_kernel(
    first_ref, last_ref, got_ref, got_last_ref, second0_ref, second1_ref, second2_ref, w_ref, out_hbm, part_ref, held_ref, sems
):
    rank = lax.axis_index("ctx")
    half, depth = first_ref.shape[0], w_ref.shape[0] // 2
    cut = depth - last_ref.shape[1]
    rows = pl.ds(first_begin(rank, half), half)
    mine = pl.ds(pl.multiple_of(lax.axis_index("head") * depth, depth), depth)
    other = other_rows(w_ref, 0, depth)
    first = jnp.concatenate([first_ref[:, :cut], last_ref[...]], axis=1)
    got = jnp.concatenate([got_ref[:, :cut], got_last_ref[...]], axis=1)
    second = jnp.concatenate([second0_ref[...], second1_ref[...], second2_ref[...]], axis=1)
    stacked = jnp.concatenate([first, second], axis=0)
    copies = []
    for tile in range(w_ref.shape[1] // TILE):
        at = slice(tile * TILE, (tile + 1) * TILE)
        both = dot(stacked, w_ref[mine, at])
        part_ref[:, at] = both[half:]
        held_ref[:, at] = (both[:half] + dot(got, w_ref[other, at])).astype(BF16)
        copies.append(pltpu.make_async_copy(held_ref.at[:, at], out_hbm.at[rows, at], sems.at[tile]))
        copies[-1].start()
    for copy in copies:
        copy.wait()


def add_kernel(begin, got_ref, part_ref, w_ref, out_ref):
    rows = other_rows(w_ref, begin, begin + got_ref.shape[1])
    for start in range(0, w_ref.shape[1], TILE):
        at = slice(start, start + TILE)
        out_ref[:, at] = part_ref[:, at] + dot(got_ref[...], w_ref[rows, at])


def last_kernel(begin, got_ref, part_ref, w_ref, begun_hbm, out_hbm, held_ref, sems):
    del begun_hbm
    rank = lax.axis_index("ctx")
    half, depth = got_ref.shape
    out_rows = pl.ds(pl.multiple_of(half - first_begin(rank, half), half), half)
    rows = other_rows(w_ref, begin, begin + depth)
    copies = []
    for tile in range(w_ref.shape[1] // LAST_TILE):
        at = slice(tile * LAST_TILE, (tile + 1) * LAST_TILE)
        added = dot(got_ref[...], w_ref[rows, at])
        held_ref[:, at] = (part_ref[:, at] + added).astype(BF16)
        copies.append(pltpu.make_async_copy(held_ref.at[:, at], out_hbm.at[out_rows, at], sems.at[tile]))
        copies[-1].start()
    for copy in copies:
        copy.wait()


def shards(queries, keys, values, positions, out_weight):
    number, width = queries.shape
    half = number // 2
    count = lax.axis_size("ctx")
    group = width // keys.shape[1]
    columns = out_weight.shape[1]
    tiles = columns // TILE
    in_hbm = lambda array: pltpu.with_memory_space_constraint(array, pltpu.HBM)
    position_row = positions.reshape(1, number)
    table = np.power(500000.0, -2.0 * np.arange(HEAD_SIZE // 2) / HEAD_SIZE).astype(np.float32)
    frequency = jnp.asarray(np.concatenate([table, table])[None, :])
    shape = jax.ShapeDtypeStruct
    vmem = pl.BlockSpec(memory_space=pltpu.VMEM)
    hbm = pl.BlockSpec(memory_space=pltpu.HBM)
    dma = pltpu.SemaphoreType.DMA

    def call(body, name, ins, outs, flops, nbytes, out_specs=None, scratch=(), aliases={}):
        return pl.pallas_call(
            body,
            name=name,
            in_specs=ins,
            out_shape=outs,
            out_specs=out_specs if out_specs is not None else jax.tree.map(lambda _: vmem, outs),
            scratch_shapes=scratch,
            input_output_aliases=aliases,
            compiler_params=pltpu.CompilerParams(vmem_limit_bytes=32 * MIB),
            cost_estimate=pl.CostEstimate(flops=flops // 1024, bytes_accessed=nbytes // 1024, transcendentals=0),
        )

    def pairs(target_of):
        found = [(source, target_of(source) % count) for source in range(count)]
        assert sorted(target for _, target in found) == list(range(count))
        return found

    def swapped(array):
        return lax.ppermute(array, "head", [(0, 1), (1, 0)])

    kv_shape = shape((half, 2 * keys.shape[1]), BF16)
    table_shape = shape((number, HEAD_SIZE), F32)
    rows_shape, state = shape((half, width), BF16), shape((half, width), F32)
    heads = width // HEAD_SIZE
    cut = heads - group
    some_shape = shape((half, cut * HEAD_SIZE), BF16)
    some_state = shape((half, cut * HEAD_SIZE), F32)
    last_shape = shape((half, group * HEAD_SIZE), BF16)
    early, near, onward, k_rot, v, q, p, cosine, sinus = call(
        functools.partial(keys_kernel, count),
        "rotate_keys",
        [hbm] * 5,
        [shape((half, (group + 2) * HEAD_SIZE), BF16), kv_shape, kv_shape]
        + [shape(keys.shape, BF16)] * 2
        + [shape(queries.shape, BF16), shape((1, number), jnp.int32), table_shape, table_shape],
        4 * MIB,
        4 * MIB,
        scratch=[pltpu.VMEM(keys.shape, BF16), pltpu.VMEM((1, HEAD_SIZE), F32), dma((5,))],
    )(*(in_hbm(array) for array in (keys, values, queries, position_row, frequency)))
    early_got = swapped(early)
    near_got = lax.ppermute(near, "ctx", pairs(lambda r: r + 3 if r % 2 else r + 1))
    own, rot, acc, top, total = call(
        functools.partial(own_kernel, group),
        "own_tiles",
        [vmem] * 6,
        [some_shape, some_shape, some_state, some_state, some_state],
        256 * MIB,
        4 * MIB,
    )(q, k_rot, v, p, cosine, sinus)
    onward, rot = lax.optimization_barrier((onward, rot))
    next_got = lax.ppermute(onward, "ctx", pairs(lambda r: r + 2))
    first = call(
        functools.partial(first_kernel, count, group),
        "first_rows",
        [vmem] * 7,
        shape((half, (cut + 2) * HEAD_SIZE), BF16),
        256 * MIB,
        4 * MIB,
    )(own, rot, near_got, p, acc, top, total)
    first_got = swapped(first)
    q, first = lax.optimization_barrier((q, first))
    rot, *state_now, w = call(
        functools.partial(second_kernel, count, group),
        "second_rows",
        [vmem] * 7 + [hbm],
        [rows_shape, state, state, state, shape(out_weight.shape, BF16)],
        1024 * MIB,
        12 * MIB,
        scratch=[dma(())],
    )(q, k_rot, v, p, cosine, sinus, near_got, in_hbm(out_weight))
    early, rot = lax.optimization_barrier((early, rot))
    attend_early = call(
        functools.partial(early_kernel, count), "early_rows", [vmem] * 3, last_shape, 256 * MIB, 4 * MIB
    )
    last = attend_early(early, first, p)
    rot, next_got, last, early_got = lax.optimization_barrier((rot, next_got, last, early_got))
    last_got = lax.ppermute(next_got, "ctx", pairs(lambda r: r + 1 - 2 * (r % 2)))
    state_now = call(
        functools.partial(next_kernel, count, group),
        "next_tile",
        [vmem] * 6,
        [state, state, state],
        512 * MIB,
        4 * MIB,
        aliases={3: 0, 4: 1, 5: 2},
    )(rot, next_got, p, *state_now)
    parts = range(cut), range(cut, heads - 1), range(heads - 1, heads)
    seconds, seconds_got = [], []
    for part in parts:
        second = call(
            functools.partial(third_kernel, count, group, part),
            "last_tile",
            [vmem] * 6,
            shape((half, len(part) * HEAD_SIZE), BF16),
            256 * MIB,
            4 * MIB,
        )(rot, last_got, p, *state_now)
        seconds_got.append(swapped(second))
        rot, second, first_got = lax.optimization_barrier((rot, second, first_got))
        seconds.append(second)
    sum_shape = shape((half, columns), F32)
    early_got, seconds[-1] = lax.optimization_barrier((early_got, seconds[-1]))
    begun, partial_sum = call(
        project_kernel,
        "project_first",
        [vmem] * 8,
        [shape((number, columns), BF16), sum_shape],
        3072 * MIB,
        8 * MIB,
        out_specs=[hbm, vmem],
        scratch=[pltpu.VMEM((half, columns), BF16), dma((tiles,))],
    )(first, last, first_got, attend_early(early_got, first_got, p), *seconds, w)
    for part, got in zip(parts[:-1], seconds_got):
        partial_sum = call(
            functools.partial(add_kernel, part[0] * HEAD_SIZE),
            "project_second",
            [vmem] * 3,
            sum_shape,
            512 * MIB,
            4 * MIB,
        )(got, partial_sum, w)
    return call(
        functools.partial(last_kernel, parts[-1][0] * HEAD_SIZE),
        "project_last",
        [vmem] * 3 + [hbm],
        shape((number, columns), BF16),
        512 * MIB,
        4 * MIB,
        out_specs=hbm,
        scratch=[pltpu.VMEM((half, columns), BF16), dma((columns // LAST_TILE,))],
        aliases={3: 0},
    )(seconds_got[-1], partial_sum, w, begun)


def solution(mesh):
    in_specs = (P("ctx", "head"), P("ctx", "head"), P("ctx", "head"), P("ctx"), P(None, "head"))
    out_specs = P("ctx", "head")
    return jax.shard_map(shards, mesh=mesh, in_specs=in_specs, out_specs=out_specs, check_vma=False)
```

```python
import functools
import math

import jax
import jax.numpy as jnp
import numpy as np
from jax import lax
from jax.experimental import pallas as pl
from jax.experimental.pallas import tpu as pltpu
from jax.sharding import PartitionSpec as P

HEAD_SIZE = 128
LOWEST = -1e30
FAR = 1 << 16
MIB = 1 << 20
SCORE_SCALE = math.log2(math.e) / math.sqrt(HEAD_SIZE)
BF16, F32 = jnp.bfloat16, jnp.float32


def distance(rank, step, count):
    return jnp.where(rank >= step, step, count - step)


def waits_for_keys(rank):
    return (rank == 1) | (rank == 2)


def first_begin(rank, half):
    return pl.multiple_of(jnp.where(rank < 2, 0, half), half)


def half_positions(p_ref, rank, first):
    half = p_ref.shape[1] // 2
    early = (rank < 2) if first else (rank >= 2)
    return jnp.where(early, p_ref[:, :half], p_ref[:, half:])


def column(row, width):
    return jnp.broadcast_to(row, (width, row.shape[1])).T


def tile_biases(position_row, kinds):
    number = position_row.shape[1]
    position = column(position_row, number)
    query = lax.broadcasted_iota(jnp.int32, (number, number), 0)
    key = lax.broadcasted_iota(jnp.int32, (number, number), 1)
    ahead = key - query
    reach = ahead + position
    found = []
    for pieces, diagonal in kinds:
        allowed = reach >= pieces * number
        if diagonal:
            allowed = allowed & (ahead <= 0)
        found.append(jnp.where(allowed, 0.0, LOWEST).astype(F32))
    return found


def sine_cosine(angle):
    turns = jnp.floor(angle * (2.0 / math.pi) + 0.5)
    rest = ((angle - turns * 1.5703125) - turns * 4.837512969970703e-4) - turns * 7.549789954891888e-8
    square = rest * rest
    sine = ((-1.9515295891e-4 * square + 8.3321608736e-3) * square - 1.6666654611e-1) * square * rest + rest
    cosine = (
        ((2.443315711809948e-5 * square - 1.388731625493765e-3) * square + 4.166664568298827e-2) * square * square
        - 0.5 * square
        + 1.0
    )
    quarter = turns.astype(jnp.int32)
    swap = (quarter & 1) == 1
    out_sine = jnp.where(swap, cosine, sine)
    out_cosine = jnp.where(swap, sine, cosine)
    out_sine = jnp.where((quarter & 2) == 2, -out_sine, out_sine)
    out_cosine = jnp.where(((quarter + 1) & 2) == 2, -out_cosine, out_cosine)
    return out_sine, out_cosine


def turned(block, cosine, sinus):
    wide = block.astype(F32)
    return (wide * cosine + pltpu.roll(wide, HEAD_SIZE // 2, 1) * sinus).astype(BF16)


def scores_of(query, key, bias):
    raw = lax.dot_general(query, key, (((1,), (1,)), ((), ())), preferred_element_type=F32)
    return raw * SCORE_SCALE + bias


def weighted(weights, value):
    return jnp.dot(weights.astype(BF16), value, preferred_element_type=F32)


def spread(entries):
    return jnp.broadcast_to(entries, (entries.shape[0], HEAD_SIZE))


def with_ones(value):
    return jnp.concatenate([value, jnp.ones_like(value)], axis=1)


def head_slices(head, group, width):
    at = slice(head * HEAD_SIZE, (head + 1) * HEAD_SIZE)
    low = head // group * HEAD_SIZE
    return at, slice(low, low + HEAD_SIZE), slice(width + low, width + low + HEAD_SIZE)


def begin_state(query, keys, values, biases):
    scores = [scores_of(query, key, bias) for key, bias in zip(keys, biases)]
    top = jnp.max(functools.reduce(jnp.maximum, scores), axis=1, keepdims=True)
    weights = [jnp.exp2(score - top) for score in scores]
    both = functools.reduce(jnp.add, [weighted(w, value) for w, value in zip(weights, values)])
    return both[:, :HEAD_SIZE], spread(top), both[:, HEAD_SIZE:]


def added_tile(summed, top, total, query, key, value, bias):
    score = scores_of(query, key, bias)
    updated = jnp.maximum(top, spread(jnp.max(score, axis=1, keepdims=True)))
    weights = jnp.exp2(score - jnp.concatenate([updated] * (score.shape[1] // HEAD_SIZE), axis=1))
    factor = jnp.exp2(top - updated)
    both = weighted(weights, value)
    return summed * factor + both[:, :HEAD_SIZE], updated, total * factor + both[:, HEAD_SIZE:]


def finished(state):
    summed, _, total = state
    return (summed * (1.0 / total)).astype(BF16)


def keys_kernel(
    count, k_hbm, v_hbm, q_hbm, p_hbm, f_hbm, near_ref, next_ref, rot_ref, v_ref, q_ref, p_ref, cos_ref, sin_ref,
    k_ref, f_ref, sems,
):
    pairs = ((p_hbm, p_ref), (f_hbm, f_ref), (k_hbm, k_ref), (v_hbm, v_ref), (q_hbm, q_ref))
    copies = [pltpu.make_async_copy(source, target, sems.at[i]) for i, (source, target) in enumerate(pairs)]
    for copy in copies:
        copy.start()
    rank = lax.axis_index("ctx")
    half = k_ref.shape[0] // 2
    width = k_ref.shape[1]
    copies[0].wait()
    copies[1].wait()
    position = p_ref[...].astype(F32)
    early = column(position[:, :half], HEAD_SIZE)
    late = column(position[:, half:], HEAD_SIZE)
    lane = lax.broadcasted_iota(jnp.int32, (half, HEAD_SIZE), 1)
    front = lane < HEAD_SIZE // 2
    sine, cosine = sine_cosine(jnp.where(front, early, late) * f_ref[...])
    sine_other = pltpu.roll(sine, HEAD_SIZE // 2, 1)
    cosine_other = pltpu.roll(cosine, HEAD_SIZE // 2, 1)
    cos_ref[:half] = jnp.where(front, cosine, cosine_other)
    cos_ref[half:] = jnp.where(front, cosine_other, cosine)
    sin_ref[:half] = jnp.where(front, -sine, sine_other)
    sin_ref[half:] = jnp.where(front, -sine_other, sine)
    copies[2].wait()
    for head in range(width // HEAD_SIZE):
        at = slice(head * HEAD_SIZE, (head + 1) * HEAD_SIZE)
        rot_ref[:, at] = turned(k_ref[:, at], cos_ref[...], sin_ref[...])
    copies[3].wait()
    wrap = (rank % 2 == 1) & (rank + 3 >= count)
    rows = pl.ds(pl.multiple_of(jnp.where(wrap, half, 0), half), half)
    near_ref[:, :width] = rot_ref[rows, :]
    near_ref[:, width:] = v_ref[rows, :]
    rows = pl.ds(pl.multiple_of(jnp.where(rank + 2 >= count, half, 0), half), half)
    next_ref[:, :width] = rot_ref[rows, :]
    next_ref[:, width:] = v_ref[rows, :]
    copies[4].wait()


def pack_kernel(q_ref, k_ref, v_ref, cos_ref, sin_ref, out_ref):
    rank = lax.axis_index("ctx")
    half, width = out_ref.shape[0], k_ref.shape[1]
    rows = pl.ds(first_begin(rank, half), half)
    begin, late = out_ref.shape[1] - 2 * HEAD_SIZE, slice(width - HEAD_SIZE, width)
    out_ref[:, begin : begin + HEAD_SIZE] = k_ref[rows, late]
    out_ref[:, begin + HEAD_SIZE :] = v_ref[rows, late]
    low = q_ref.shape[1] - begin
    for head in range(begin // HEAD_SIZE):
        at = slice(head * HEAD_SIZE, (head + 1) * HEAD_SIZE)
        source = slice(low + head * HEAD_SIZE, low + (head + 1) * HEAD_SIZE)
        out_ref[:, at] = turned(q_ref[rows, source], cos_ref[rows, :], sin_ref[rows, :])


def own_kernel(group, q_ref, k_ref, v_ref, p_ref, cos_ref, sin_ref, out_ref, rot_ref, acc_ref, top_ref, sum_ref):
    rank = lax.axis_index("ctx")
    half = q_ref.shape[0] // 2
    rows = pl.ds(first_begin(rank, half), half)
    biases = tile_biases(half_positions(p_ref, rank, True), [(0, True)])
    for head in range(rot_ref.shape[1] // HEAD_SIZE):
        at, shared, _ = head_slices(head, group, 0)
        query = turned(q_ref[rows, at], cos_ref[rows, :], sin_ref[rows, :])
        rot_ref[:, at] = query
        if head % group == 0:
            key = k_ref[rows, shared]
            value = with_ones(v_ref[rows, shared])
        for low, high in ((0, half // 2), (half // 2, half)):
            part = slice(low, high)
            summed, top, total = begin_state(query[part], [key[:high]], [value[:high]], [biases[0][part, :high]])
            acc_ref[part, at] = summed
            top_ref[part, at] = top
            sum_ref[part, at] = total
            out_ref[part, at] = (summed * (1.0 / total)).astype(BF16)


def first_kernel(count, group, own_ref, rot_ref, kv_ref, p_ref, acc_ref, top_ref, sum_ref, out_ref):
    rank = lax.axis_index("ctx")
    width = kv_ref.shape[1] // 2
    depth = rot_ref.shape[1]
    step = jnp.where(rank % 2 == 1, 1, 3)
    used = waits_for_keys(rank)
    out_ref[:, depth : depth + HEAD_SIZE] = kv_ref[:, width - HEAD_SIZE : width]
    out_ref[:, depth + HEAD_SIZE :] = kv_ref[:, 2 * width - HEAD_SIZE :]

    @pl.when(used)
    def _():
        biases = tile_biases(half_positions(p_ref, rank, True), [(distance(rank, step, count), False)])
        for head in range(depth // HEAD_SIZE):
            at, key_at, value_at = head_slices(head, group, width)
            state = acc_ref[:, at], top_ref[:, at], sum_ref[:, at]
            if head % group == 0:
                value = with_ones(kv_ref[:, value_at])
            out_ref[:, at] = finished(added_tile(*state, rot_ref[:, at], kv_ref[:, key_at], value, *biases))

    @pl.when(jnp.logical_not(used))
    def _():
        out_ref[:, :depth] = own_ref[...]


def early_kernel(count, early_ref, near_ref, p_ref, out_ref):
    rank = lax.axis_index("ctx")
    depth = out_ref.shape[1]
    step = jnp.where(rank % 2 == 1, 1, 3)
    reach = jnp.where(waits_for_keys(rank), distance(rank, step, count), FAR)
    biases = tile_biases(half_positions(p_ref, rank, True), [(0, True), (reach, False)])
    keys, values = [], []
    for ref in (early_ref, near_ref):
        begin = ref.shape[1] - 2 * HEAD_SIZE
        keys.append(ref[:, begin : begin + HEAD_SIZE])
        values.append(with_ones(ref[:, begin + HEAD_SIZE :]))
    for head in range(depth // HEAD_SIZE):
        at = slice(head * HEAD_SIZE, (head + 1) * HEAD_SIZE)
        out_ref[:, at] = finished(begin_state(early_ref[:, at], keys, values, biases))


def second_kernel(
    count, group, q_ref, k_ref, v_ref, p_ref, cos_ref, sin_ref, kv_ref, w_hbm, rot_ref, acc_ref, top_ref, sum_ref, w_ref, sem
):
    copy = pltpu.make_async_copy(w_hbm, w_ref, sem)
    copy.start()
    rank = lax.axis_index("ctx")
    half = q_ref.shape[0] // 2
    width = k_ref.shape[1]
    rows = pl.ds(pl.multiple_of(half - first_begin(rank, half), half), half)
    step = jnp.where(rank % 2 == 1, 1, 3)
    reach = jnp.where(waits_for_keys(rank), FAR, distance(rank, step, count))
    biases = tile_biases(half_positions(p_ref, rank, False), [(0, True), (reach, False)])
    for head in range(q_ref.shape[1] // HEAD_SIZE):
        at, key_at, value_at = head_slices(head, group, width)
        query = turned(q_ref[rows, at], cos_ref[rows, :], sin_ref[rows, :])
        rot_ref[:, at] = query
        keys = [k_ref[rows, key_at], kv_ref[:, key_at]]
        if head % group == 0:
            values = [with_ones(v_ref[rows, key_at]), with_ones(kv_ref[:, value_at])]
        acc_ref[:, at], top_ref[:, at], sum_ref[:, at] = begin_state(query, keys, values, biases)
    copy.wait()


def next_kernel(count, group, rot_ref, kv_ref, p_ref, acc_ref, top_ref, sum_ref, *outs):
    rank = lax.axis_index("ctx")
    width = kv_ref.shape[1] // 2
    biases = tile_biases(half_positions(p_ref, rank, False), [(distance(rank, 2, count), False)])
    for head in range(rot_ref.shape[1] // HEAD_SIZE):
        at, key_at, value_at = head_slices(head, group, width)
        state = acc_ref[:, at], top_ref[:, at], sum_ref[:, at]
        if head % group == 0:
            value = with_ones(kv_ref[:, value_at])
        state = added_tile(*state, rot_ref[:, at], kv_ref[:, key_at], value, *biases)
        for out_ref, entries in zip(outs, state):
            out_ref[:, at] = entries


def third_kernel(count, group, heads, rot_ref, kv_ref, p_ref, acc_ref, top_ref, sum_ref, out_ref):
    rank = lax.axis_index("ctx")
    width = kv_ref.shape[1] // 2
    step = jnp.where(rank % 2 == 1, 3, 1)
    biases = tile_biases(half_positions(p_ref, rank, False), [(distance(rank, step, count), False)])
    for number, head in enumerate(heads):
        at, key_at, value_at = head_slices(head, group, width)
        state = acc_ref[:, at], top_ref[:, at], sum_ref[:, at]
        if number == 0 or head % group == 0:
            value = with_ones(kv_ref[:, value_at])
        state = added_tile(*state, rot_ref[:, at], kv_ref[:, key_at], value, *biases)
        out_ref[:, number * HEAD_SIZE : (number + 1) * HEAD_SIZE] = finished(state)


def dot(left, right):
    return jnp.dot(left, right, preferred_element_type=F32)


TILE = 512
LAST_TILE = 256


def other_rows(w_ref, begin, end):
    depth = w_ref.shape[0] // 2
    base = (1 - lax.axis_index("head")) * depth
    return pl.ds(pl.multiple_of(base + begin, HEAD_SIZE), end - begin)


def project_kernel(
    first_ref, last_ref, got_ref, got_last_ref, second0_ref, second1_ref, second2_ref, w_ref, out_hbm, part_ref, held_ref, sems
):
    rank = lax.axis_index("ctx")
    half, depth = first_ref.shape[0], w_ref.shape[0] // 2
    cut = depth - last_ref.shape[1]
    rows = pl.ds(first_begin(rank, half), half)
    mine = pl.ds(pl.multiple_of(lax.axis_index("head") * depth, depth), depth)
    other = other_rows(w_ref, 0, depth)
    first = jnp.concatenate([first_ref[:, :cut], last_ref[...]], axis=1)
    got = jnp.concatenate([got_ref[:, :cut], got_last_ref[...]], axis=1)
    second = jnp.concatenate([second0_ref[...], second1_ref[...], second2_ref[...]], axis=1)
    stacked = jnp.concatenate([first, second], axis=0)
    copies = []
    for tile in range(w_ref.shape[1] // TILE):
        at = slice(tile * TILE, (tile + 1) * TILE)
        both = dot(stacked, w_ref[mine, at])
        part_ref[:, at] = both[half:]
        held_ref[:, at] = (both[:half] + dot(got, w_ref[other, at])).astype(BF16)
        copies.append(pltpu.make_async_copy(held_ref.at[:, at], out_hbm.at[rows, at], sems.at[tile]))
        copies[-1].start()
    for copy in copies:
        copy.wait()


def add_kernel(begin, got_ref, part_ref, w_ref, out_ref):
    rows = other_rows(w_ref, begin, begin + got_ref.shape[1])
    for start in range(0, w_ref.shape[1], TILE):
        at = slice(start, start + TILE)
        out_ref[:, at] = part_ref[:, at] + dot(got_ref[...], w_ref[rows, at])


def last_kernel(begin, got_ref, part_ref, w_ref, begun_hbm, out_hbm, held_ref, sems):
    del begun_hbm
    rank = lax.axis_index("ctx")
    half, depth = got_ref.shape
    out_rows = pl.ds(pl.multiple_of(half - first_begin(rank, half), half), half)
    rows = other_rows(w_ref, begin, begin + depth)
    copies = []
    for tile in range(w_ref.shape[1] // LAST_TILE):
        at = slice(tile * LAST_TILE, (tile + 1) * LAST_TILE)
        added = dot(got_ref[...], w_ref[rows, at])
        held_ref[:, at] = (part_ref[:, at] + added).astype(BF16)
        copies.append(pltpu.make_async_copy(held_ref.at[:, at], out_hbm.at[out_rows, at], sems.at[tile]))
        copies[-1].start()
    for copy in copies:
        copy.wait()


def shards(queries, keys, values, positions, out_weight):
    number, width = queries.shape
    half = number // 2
    count = lax.axis_size("ctx")
    group = width // keys.shape[1]
    columns = out_weight.shape[1]
    tiles = columns // TILE
    in_hbm = lambda array: pltpu.with_memory_space_constraint(array, pltpu.HBM)
    position_row = positions.reshape(1, number)
    table = np.power(500000.0, -2.0 * np.arange(HEAD_SIZE // 2) / HEAD_SIZE).astype(np.float32)
    frequency = jnp.asarray(np.concatenate([table, table])[None, :])
    shape = jax.ShapeDtypeStruct
    vmem = pl.BlockSpec(memory_space=pltpu.VMEM)
    hbm = pl.BlockSpec(memory_space=pltpu.HBM)
    dma = pltpu.SemaphoreType.DMA

    def call(body, name, ins, outs, flops, nbytes, out_specs=None, scratch=(), aliases={}):
        return pl.pallas_call(
            body,
            name=name,
            in_specs=ins,
            out_shape=outs,
            out_specs=out_specs if out_specs is not None else jax.tree.map(lambda _: vmem, outs),
            scratch_shapes=scratch,
            input_output_aliases=aliases,
            compiler_params=pltpu.CompilerParams(vmem_limit_bytes=32 * MIB),
            cost_estimate=pl.CostEstimate(flops=flops, bytes_accessed=nbytes, transcendentals=0),
        )

    def pairs(target_of):
        found = [(source, target_of(source) % count) for source in range(count)]
        assert sorted(target for _, target in found) == list(range(count))
        return found

    def swapped(array):
        return lax.ppermute(array, "head", [(0, 1), (1, 0)])

    kv_shape = shape((half, 2 * keys.shape[1]), BF16)
    table_shape = shape((number, HEAD_SIZE), F32)
    rows_shape, state = shape((half, width), BF16), shape((half, width), F32)
    heads = width // HEAD_SIZE
    cut = heads - group
    some_shape = shape((half, cut * HEAD_SIZE), BF16)
    some_state = shape((half, cut * HEAD_SIZE), F32)
    last_shape = shape((half, group * HEAD_SIZE), BF16)
    near, onward, k_rot, v, q, p, cosine, sinus = call(
        functools.partial(keys_kernel, count),
        "rotate_keys",
        [hbm] * 5,
        [kv_shape, kv_shape]
        + [shape(keys.shape, BF16)] * 2
        + [shape(queries.shape, BF16), shape((1, number), jnp.int32), table_shape, table_shape],
        4 * MIB,
        4 * MIB,
        scratch=[pltpu.VMEM(keys.shape, BF16), pltpu.VMEM((1, HEAD_SIZE), F32), dma((5,))],
    )(*(in_hbm(array) for array in (keys, values, queries, position_row, frequency)))
    near_got = lax.ppermute(near, "ctx", pairs(lambda r: r + 3 if r % 2 else r + 1))
    early = call(pack_kernel, "pack_early", [vmem] * 5, shape((half, (group + 2) * HEAD_SIZE), BF16), MIB, MIB)(
        q, k_rot, v, cosine, sinus
    )
    early, q = lax.optimization_barrier((early, q))
    early_got = swapped(early)
    own, rot, acc, top, total = call(
        functools.partial(own_kernel, group),
        "own_tiles",
        [vmem] * 6,
        [some_shape, some_shape, some_state, some_state, some_state],
        256 * MIB,
        4 * MIB,
    )(q, k_rot, v, p, cosine, sinus)
    onward, rot = lax.optimization_barrier((onward, rot))
    next_got = lax.ppermute(onward, "ctx", pairs(lambda r: r + 2))
    first = call(
        functools.partial(first_kernel, count, group),
        "first_rows",
        [vmem] * 7,
        shape((half, (cut + 2) * HEAD_SIZE), BF16),
        256 * MIB,
        4 * MIB,
    )(own, rot, near_got, p, acc, top, total)
    first_got = swapped(first)
    q, first = lax.optimization_barrier((q, first))
    rot, *state_now, w = call(
        functools.partial(second_kernel, count, group),
        "second_rows",
        [vmem] * 7 + [hbm],
        [rows_shape, state, state, state, shape(out_weight.shape, BF16)],
        1024 * MIB,
        12 * MIB,
        scratch=[dma(())],
    )(q, k_rot, v, p, cosine, sinus, near_got, in_hbm(out_weight))
    early, rot = lax.optimization_barrier((early, rot))
    attend_early = call(
        functools.partial(early_kernel, count), "early_rows", [vmem] * 3, last_shape, 256 * MIB, 4 * MIB
    )
    last = attend_early(early, first, p)
    rot, next_got, last, early_got = lax.optimization_barrier((rot, next_got, last, early_got))
    last_got = lax.ppermute(next_got, "ctx", pairs(lambda r: r + 1 - 2 * (r % 2)))
    state_now = call(
        functools.partial(next_kernel, count, group),
        "next_tile",
        [vmem] * 6,
        [state, state, state],
        512 * MIB,
        4 * MIB,
        aliases={3: 0, 4: 1, 5: 2},
    )(rot, next_got, p, *state_now)
    parts = range(cut), range(cut, heads - 1), range(heads - 1, heads)
    seconds, seconds_got = [], []
    for part in parts:
        second = call(
            functools.partial(third_kernel, count, group, part),
            "last_tile",
            [vmem] * 6,
            shape((half, len(part) * HEAD_SIZE), BF16),
            256 * MIB,
            4 * MIB,
        )(rot, last_got, p, *state_now)
        seconds_got.append(swapped(second))
        rot, second, first_got = lax.optimization_barrier((rot, second, first_got))
        seconds.append(second)
    sum_shape = shape((half, columns), F32)
    early_got, seconds[-1] = lax.optimization_barrier((early_got, seconds[-1]))
    begun, partial_sum = call(
        project_kernel,
        "project_first",
        [vmem] * 8,
        [shape((number, columns), BF16), sum_shape],
        3072 * MIB,
        8 * MIB,
        out_specs=[hbm, vmem],
        scratch=[pltpu.VMEM((half, columns), BF16), dma((tiles,))],
    )(first, last, first_got, attend_early(early_got, first_got, p), *seconds, w)
    for part, got in zip(parts[:-1], seconds_got):
        partial_sum = call(
            functools.partial(add_kernel, part[0] * HEAD_SIZE),
            "project_second",
            [vmem] * 3,
            sum_shape,
            512 * MIB,
            4 * MIB,
        )(got, partial_sum, w)
    return call(
        functools.partial(last_kernel, parts[-1][0] * HEAD_SIZE),
        "project_last",
        [vmem] * 3 + [hbm],
        shape((number, columns), BF16),
        512 * MIB,
        4 * MIB,
        out_specs=hbm,
        scratch=[pltpu.VMEM((half, columns), BF16), dma((columns // LAST_TILE,))],
        aliases={3: 0},
    )(seconds_got[-1], partial_sum, w, begun)


def solution(mesh):
    in_specs = (P("ctx", "head"), P("ctx", "head"), P("ctx", "head"), P("ctx"), P(None, "head"))
    out_specs = P("ctx", "head")
    return jax.shard_map(shards, mesh=mesh, in_specs=in_specs, out_specs=out_specs, check_vma=False)
```

```python
import functools
import math

import jax
import jax.numpy as jnp
import numpy as np
from jax import lax
from jax.experimental import pallas as pl
from jax.experimental.pallas import tpu as pltpu
from jax.sharding import PartitionSpec as P

HEAD_SIZE = 128
LOWEST = -1e30
FAR = 1 << 16
MIB = 1 << 20
SCORE_SCALE = math.log2(math.e) / math.sqrt(HEAD_SIZE)
BF16, F32 = jnp.bfloat16, jnp.float32


def distance(rank, step, count):
    return jnp.where(rank >= step, step, count - step)


def waits_for_keys(rank):
    return (rank == 1) | (rank == 2)


def first_begin(rank, half):
    return pl.multiple_of(jnp.where(rank < 2, 0, half), half)


def half_positions(p_ref, rank, first):
    half = p_ref.shape[1] // 2
    early = (rank < 2) if first else (rank >= 2)
    return jnp.where(early, p_ref[:, :half], p_ref[:, half:])


def column(row, width):
    return jnp.broadcast_to(row, (width, row.shape[1])).T


def tile_biases(position_row, kinds):
    number = position_row.shape[1]
    position = column(position_row, number)
    query = lax.broadcasted_iota(jnp.int32, (number, number), 0)
    key = lax.broadcasted_iota(jnp.int32, (number, number), 1)
    ahead = key - query
    reach = ahead + position
    found = []
    for pieces, diagonal in kinds:
        allowed = reach >= pieces * number
        if diagonal:
            allowed = allowed & (ahead <= 0)
        found.append(jnp.where(allowed, 0.0, LOWEST).astype(F32))
    return found


def sine_cosine(angle):
    turns = jnp.floor(angle * (2.0 / math.pi) + 0.5)
    rest = ((angle - turns * 1.5703125) - turns * 4.837512969970703e-4) - turns * 7.549789954891888e-8
    square = rest * rest
    sine = ((-1.9515295891e-4 * square + 8.3321608736e-3) * square - 1.6666654611e-1) * square * rest + rest
    cosine = (
        ((2.443315711809948e-5 * square - 1.388731625493765e-3) * square + 4.166664568298827e-2) * square * square
        - 0.5 * square
        + 1.0
    )
    quarter = turns.astype(jnp.int32)
    swap = (quarter & 1) == 1
    out_sine = jnp.where(swap, cosine, sine)
    out_cosine = jnp.where(swap, sine, cosine)
    out_sine = jnp.where((quarter & 2) == 2, -out_sine, out_sine)
    out_cosine = jnp.where(((quarter + 1) & 2) == 2, -out_cosine, out_cosine)
    return out_sine, out_cosine


def turned(block, cosine, sinus):
    wide = block.astype(F32)
    return (wide * cosine + pltpu.roll(wide, HEAD_SIZE // 2, 1) * sinus).astype(BF16)


def scores_of(query, key, bias):
    raw = lax.dot_general(query, key, (((1,), (1,)), ((), ())), preferred_element_type=F32)
    return raw * SCORE_SCALE + bias


def weighted(weights, value):
    return jnp.dot(weights.astype(BF16), value, preferred_element_type=F32)


def spread(entries):
    return jnp.broadcast_to(entries, (entries.shape[0], HEAD_SIZE))


def with_ones(value):
    return jnp.concatenate([value, jnp.ones_like(value)], axis=1)


def head_slices(head, group, width):
    at = slice(head * HEAD_SIZE, (head + 1) * HEAD_SIZE)
    low = head // group * HEAD_SIZE
    return at, slice(low, low + HEAD_SIZE), slice(width + low, width + low + HEAD_SIZE)


def begin_state(query, keys, values, biases):
    scores = [scores_of(query, key, bias) for key, bias in zip(keys, biases)]
    top = jnp.max(functools.reduce(jnp.maximum, scores), axis=1, keepdims=True)
    weights = [jnp.exp2(score - top) for score in scores]
    both = functools.reduce(jnp.add, [weighted(w, value) for w, value in zip(weights, values)])
    return both[:, :HEAD_SIZE], spread(top), both[:, HEAD_SIZE:]


def added_tile(summed, top, total, query, key, value, bias):
    score = scores_of(query, key, bias)
    updated = jnp.maximum(top, spread(jnp.max(score, axis=1, keepdims=True)))
    weights = jnp.exp2(score - jnp.concatenate([updated] * (score.shape[1] // HEAD_SIZE), axis=1))
    factor = jnp.exp2(top - updated)
    both = weighted(weights, value)
    return summed * factor + both[:, :HEAD_SIZE], updated, total * factor + both[:, HEAD_SIZE:]


def finished(state):
    summed, _, total = state
    return (summed * (1.0 / total)).astype(BF16)


def keys_kernel(
    count, k_hbm, v_hbm, q_hbm, p_hbm, f_hbm, near_ref, next_ref, rot_ref, v_ref, q_ref, p_ref, cos_ref, sin_ref,
    k_ref, f_ref, sems,
):
    pairs = ((p_hbm, p_ref), (f_hbm, f_ref), (k_hbm, k_ref), (v_hbm, v_ref), (q_hbm, q_ref))
    copies = [pltpu.make_async_copy(source, target, sems.at[i]) for i, (source, target) in enumerate(pairs)]
    for copy in copies:
        copy.start()
    rank = lax.axis_index("ctx")
    half = k_ref.shape[0] // 2
    width = k_ref.shape[1]
    copies[0].wait()
    copies[1].wait()
    position = p_ref[...].astype(F32)
    early = column(position[:, :half], HEAD_SIZE)
    late = column(position[:, half:], HEAD_SIZE)
    lane = lax.broadcasted_iota(jnp.int32, (half, HEAD_SIZE), 1)
    front = lane < HEAD_SIZE // 2
    sine, cosine = sine_cosine(jnp.where(front, early, late) * f_ref[...])
    sine_other = pltpu.roll(sine, HEAD_SIZE // 2, 1)
    cosine_other = pltpu.roll(cosine, HEAD_SIZE // 2, 1)
    cos_ref[:half] = jnp.where(front, cosine, cosine_other)
    cos_ref[half:] = jnp.where(front, cosine_other, cosine)
    sin_ref[:half] = jnp.where(front, -sine, sine_other)
    sin_ref[half:] = jnp.where(front, -sine_other, sine)
    copies[2].wait()
    for head in range(width // HEAD_SIZE):
        at = slice(head * HEAD_SIZE, (head + 1) * HEAD_SIZE)
        rot_ref[:, at] = turned(k_ref[:, at], cos_ref[...], sin_ref[...])
    copies[3].wait()
    wrap = (rank % 2 == 1) & (rank + 3 >= count)
    rows = pl.ds(pl.multiple_of(jnp.where(wrap, half, 0), half), half)
    near_ref[:, :width] = rot_ref[rows, :]
    near_ref[:, width:] = v_ref[rows, :]
    rows = pl.ds(pl.multiple_of(jnp.where(rank + 2 >= count, half, 0), half), half)
    next_ref[:, :width] = rot_ref[rows, :]
    next_ref[:, width:] = v_ref[rows, :]
    copies[4].wait()


def pack_kernel(q_ref, k_ref, v_ref, cos_ref, sin_ref, out_ref):
    rank = lax.axis_index("ctx")
    half, width = out_ref.shape[0], k_ref.shape[1]
    rows = pl.ds(first_begin(rank, half), half)
    begin, late = out_ref.shape[1] - 2 * HEAD_SIZE, slice(width - HEAD_SIZE, width)
    out_ref[:, begin : begin + HEAD_SIZE] = k_ref[rows, late]
    out_ref[:, begin + HEAD_SIZE :] = v_ref[rows, late]
    low = q_ref.shape[1] - begin
    for head in range(begin // HEAD_SIZE):
        at = slice(head * HEAD_SIZE, (head + 1) * HEAD_SIZE)
        source = slice(low + head * HEAD_SIZE, low + (head + 1) * HEAD_SIZE)
        out_ref[:, at] = turned(q_ref[rows, source], cos_ref[rows, :], sin_ref[rows, :])


def own_kernel(group, q_ref, k_ref, v_ref, p_ref, cos_ref, sin_ref, out_ref, rot_ref, acc_ref, top_ref, sum_ref):
    rank = lax.axis_index("ctx")
    half = q_ref.shape[0] // 2
    rows = pl.ds(first_begin(rank, half), half)
    biases = tile_biases(half_positions(p_ref, rank, True), [(0, True)])
    for head in range(rot_ref.shape[1] // HEAD_SIZE):
        at, shared, _ = head_slices(head, group, 0)
        query = turned(q_ref[rows, at], cos_ref[rows, :], sin_ref[rows, :])
        rot_ref[:, at] = query
        if head % group == 0:
            key = k_ref[rows, shared]
            value = with_ones(v_ref[rows, shared])
        for low, high in ((0, half // 2), (half // 2, half)):
            part = slice(low, high)
            summed, top, total = begin_state(query[part], [key[:high]], [value[:high]], [biases[0][part, :high]])
            acc_ref[part, at] = summed
            top_ref[part, at] = top
            sum_ref[part, at] = total
            out_ref[part, at] = (summed * (1.0 / total)).astype(BF16)


def first_kernel(count, group, own_ref, rot_ref, kv_ref, p_ref, acc_ref, top_ref, sum_ref, out_ref):
    rank = lax.axis_index("ctx")
    width = kv_ref.shape[1] // 2
    depth = rot_ref.shape[1]
    step = jnp.where(rank % 2 == 1, 1, 3)
    used = waits_for_keys(rank)
    @pl.when(used)
    def _():
        biases = tile_biases(half_positions(p_ref, rank, True), [(distance(rank, step, count), False)])
        for head in range(depth // HEAD_SIZE):
            at, key_at, value_at = head_slices(head, group, width)
            state = acc_ref[:, at], top_ref[:, at], sum_ref[:, at]
            if head % group == 0:
                value = with_ones(kv_ref[:, value_at])
            out_ref[:, at] = finished(added_tile(*state, rot_ref[:, at], kv_ref[:, key_at], value, *biases))

    @pl.when(jnp.logical_not(used))
    def _():
        out_ref[...] = own_ref[...]


def early_kernel(count, early_ref, near_ref, p_ref, out_ref):
    rank = lax.axis_index("ctx")
    depth = out_ref.shape[1]
    width = near_ref.shape[1] // 2
    step = jnp.where(rank % 2 == 1, 1, 3)
    reach = jnp.where(waits_for_keys(rank), distance(rank, step, count), FAR)
    biases = tile_biases(half_positions(p_ref, rank, True), [(0, True), (reach, False)])
    keys = [early_ref[:, depth : depth + HEAD_SIZE], near_ref[:, width - HEAD_SIZE : width]]
    values = [with_ones(early_ref[:, depth + HEAD_SIZE :]), with_ones(near_ref[:, 2 * width - HEAD_SIZE :])]
    for head in range(depth // HEAD_SIZE):
        at = slice(head * HEAD_SIZE, (head + 1) * HEAD_SIZE)
        out_ref[:, at] = finished(begin_state(early_ref[:, at], keys, values, biases))


def second_kernel(
    count, group, q_ref, k_ref, v_ref, p_ref, cos_ref, sin_ref, kv_ref, w_hbm, rot_ref, acc_ref, top_ref, sum_ref, w_ref, sem
):
    copy = pltpu.make_async_copy(w_hbm, w_ref, sem)
    copy.start()
    rank = lax.axis_index("ctx")
    half = q_ref.shape[0] // 2
    width = k_ref.shape[1]
    rows = pl.ds(pl.multiple_of(half - first_begin(rank, half), half), half)
    step = jnp.where(rank % 2 == 1, 1, 3)
    reach = jnp.where(waits_for_keys(rank), FAR, distance(rank, step, count))
    biases = tile_biases(half_positions(p_ref, rank, False), [(0, True), (reach, False)])
    for head in range(q_ref.shape[1] // HEAD_SIZE):
        at, key_at, value_at = head_slices(head, group, width)
        query = turned(q_ref[rows, at], cos_ref[rows, :], sin_ref[rows, :])
        rot_ref[:, at] = query
        keys = [k_ref[rows, key_at], kv_ref[:, key_at]]
        if head % group == 0:
            values = [with_ones(v_ref[rows, key_at]), with_ones(kv_ref[:, value_at])]
        acc_ref[:, at], top_ref[:, at], sum_ref[:, at] = begin_state(query, keys, values, biases)
    copy.wait()


def next_kernel(count, group, rot_ref, kv_ref, p_ref, acc_ref, top_ref, sum_ref, *outs):
    rank = lax.axis_index("ctx")
    width = kv_ref.shape[1] // 2
    biases = tile_biases(half_positions(p_ref, rank, False), [(distance(rank, 2, count), False)])
    for head in range(rot_ref.shape[1] // HEAD_SIZE):
        at, key_at, value_at = head_slices(head, group, width)
        state = acc_ref[:, at], top_ref[:, at], sum_ref[:, at]
        if head % group == 0:
            value = with_ones(kv_ref[:, value_at])
        state = added_tile(*state, rot_ref[:, at], kv_ref[:, key_at], value, *biases)
        for out_ref, entries in zip(outs, state):
            out_ref[:, at] = entries


def third_kernel(count, group, heads, rot_ref, kv_ref, p_ref, acc_ref, top_ref, sum_ref, out_ref):
    rank = lax.axis_index("ctx")
    width = kv_ref.shape[1] // 2
    step = jnp.where(rank % 2 == 1, 3, 1)
    biases = tile_biases(half_positions(p_ref, rank, False), [(distance(rank, step, count), False)])
    for number, head in enumerate(heads):
        at, key_at, value_at = head_slices(head, group, width)
        state = acc_ref[:, at], top_ref[:, at], sum_ref[:, at]
        if number == 0 or head % group == 0:
            value = with_ones(kv_ref[:, value_at])
        state = added_tile(*state, rot_ref[:, at], kv_ref[:, key_at], value, *biases)
        out_ref[:, number * HEAD_SIZE : (number + 1) * HEAD_SIZE] = finished(state)


def dot(left, right):
    return jnp.dot(left, right, preferred_element_type=F32)


TILE = 512
LAST_TILE = 256


def other_rows(w_ref, begin, end):
    depth = w_ref.shape[0] // 2
    base = (1 - lax.axis_index("head")) * depth
    return pl.ds(pl.multiple_of(base + begin, HEAD_SIZE), end - begin)


def project_kernel(first_ref, last_ref, second0_ref, second1_ref, second2_ref, w_ref, sum_ref, part_ref):
    half, depth = first_ref.shape[0], w_ref.shape[0] // 2
    mine = pl.ds(pl.multiple_of(lax.axis_index("head") * depth, depth), depth)
    first = jnp.concatenate([first_ref[...], last_ref[...]], axis=1)
    second = jnp.concatenate([second0_ref[...], second1_ref[...], second2_ref[...]], axis=1)
    stacked = jnp.concatenate([first, second], axis=0)
    for tile in range(w_ref.shape[1] // TILE):
        at = slice(tile * TILE, (tile + 1) * TILE)
        both = dot(stacked, w_ref[mine, at])
        sum_ref[:, at] = both[:half]
        part_ref[:, at] = both[half:]


def first_out_kernel(got_ref, got_last_ref, sum_ref, w_ref, out_hbm, held_ref, sems):
    rank = lax.axis_index("ctx")
    half, depth = got_ref.shape[0], w_ref.shape[0] // 2
    rows = pl.ds(first_begin(rank, half), half)
    other = other_rows(w_ref, 0, depth)
    got = jnp.concatenate([got_ref[...], got_last_ref[...]], axis=1)
    copies = []
    for tile in range(w_ref.shape[1] // TILE):
        at = slice(tile * TILE, (tile + 1) * TILE)
        held_ref[:, at] = (sum_ref[:, at] + dot(got, w_ref[other, at])).astype(BF16)
        copies.append(pltpu.make_async_copy(held_ref.at[:, at], out_hbm.at[rows, at], sems.at[tile]))
        copies[-1].start()
    for copy in copies:
        copy.wait()


def add_kernel(begin, got_ref, part_ref, w_ref, out_ref):
    rows = other_rows(w_ref, begin, begin + got_ref.shape[1])
    for start in range(0, w_ref.shape[1], TILE):
        at = slice(start, start + TILE)
        out_ref[:, at] = part_ref[:, at] + dot(got_ref[...], w_ref[rows, at])


def last_kernel(begin, got_ref, part_ref, w_ref, begun_hbm, out_hbm, held_ref, sems):
    del begun_hbm
    rank = lax.axis_index("ctx")
    half, depth = got_ref.shape
    out_rows = pl.ds(pl.multiple_of(half - first_begin(rank, half), half), half)
    rows = other_rows(w_ref, begin, begin + depth)
    copies = []
    for tile in range(w_ref.shape[1] // LAST_TILE):
        at = slice(tile * LAST_TILE, (tile + 1) * LAST_TILE)
        added = dot(got_ref[...], w_ref[rows, at])
        held_ref[:, at] = (part_ref[:, at] + added).astype(BF16)
        copies.append(pltpu.make_async_copy(held_ref.at[:, at], out_hbm.at[out_rows, at], sems.at[tile]))
        copies[-1].start()
    for copy in copies:
        copy.wait()


def shards(queries, keys, values, positions, out_weight):
    number, width = queries.shape
    half = number // 2
    count = lax.axis_size("ctx")
    group = width // keys.shape[1]
    columns = out_weight.shape[1]
    tiles = columns // TILE
    in_hbm = lambda array: pltpu.with_memory_space_constraint(array, pltpu.HBM)
    position_row = positions.reshape(1, number)
    table = np.power(500000.0, -2.0 * np.arange(HEAD_SIZE // 2) / HEAD_SIZE).astype(np.float32)
    frequency = jnp.asarray(np.concatenate([table, table])[None, :])
    shape = jax.ShapeDtypeStruct
    vmem = pl.BlockSpec(memory_space=pltpu.VMEM)
    hbm = pl.BlockSpec(memory_space=pltpu.HBM)
    dma = pltpu.SemaphoreType.DMA

    def call(body, name, ins, outs, flops, nbytes, out_specs=None, scratch=(), aliases={}):
        return pl.pallas_call(
            body,
            name=name,
            in_specs=ins,
            out_shape=outs,
            out_specs=out_specs if out_specs is not None else jax.tree.map(lambda _: vmem, outs),
            scratch_shapes=scratch,
            input_output_aliases=aliases,
            compiler_params=pltpu.CompilerParams(vmem_limit_bytes=32 * MIB),
            cost_estimate=pl.CostEstimate(flops=flops, bytes_accessed=nbytes, transcendentals=0),
        )

    def pairs(target_of):
        found = [(source, target_of(source) % count) for source in range(count)]
        assert sorted(target for _, target in found) == list(range(count))
        return found

    def swapped(array):
        return lax.ppermute(array, "head", [(0, 1), (1, 0)])

    kv_shape = shape((half, 2 * keys.shape[1]), BF16)
    table_shape = shape((number, HEAD_SIZE), F32)
    rows_shape, state = shape((half, width), BF16), shape((half, width), F32)
    heads = width // HEAD_SIZE
    cut = heads - group
    some_shape = shape((half, cut * HEAD_SIZE), BF16)
    some_state = shape((half, cut * HEAD_SIZE), F32)
    last_shape = shape((half, group * HEAD_SIZE), BF16)
    near, onward, k_rot, v, q, p, cosine, sinus = call(
        functools.partial(keys_kernel, count),
        "rotate_keys",
        [hbm] * 5,
        [kv_shape, kv_shape]
        + [shape(keys.shape, BF16)] * 2
        + [shape(queries.shape, BF16), shape((1, number), jnp.int32), table_shape, table_shape],
        4 * MIB,
        4 * MIB,
        scratch=[pltpu.VMEM(keys.shape, BF16), pltpu.VMEM((1, HEAD_SIZE), F32), dma((5,))],
    )(*(in_hbm(array) for array in (keys, values, queries, position_row, frequency)))
    near_pairs = pairs(lambda r: r + 3 if r % 2 else r + 1)
    near_got = lax.ppermute(near, "ctx", near_pairs)
    early = call(pack_kernel, "pack_early", [vmem] * 5, shape((half, (group + 2) * HEAD_SIZE), BF16), MIB, MIB)(
        q, k_rot, v, cosine, sinus
    )
    early, q = lax.optimization_barrier((early, q))
    early_got = swapped(early)
    own, rot, acc, top, total = call(
        functools.partial(own_kernel, group),
        "own_tiles",
        [vmem] * 6,
        [some_shape, some_shape, some_state, some_state, some_state],
        256 * MIB,
        4 * MIB,
    )(q, k_rot, v, p, cosine, sinus)
    onward, rot = lax.optimization_barrier((onward, rot))
    next_got = lax.ppermute(onward, "ctx", pairs(lambda r: r + 2))
    first = call(
        functools.partial(first_kernel, count, group),
        "first_rows",
        [vmem] * 7,
        some_shape,
        256 * MIB,
        4 * MIB,
    )(own, rot, near_got, p, acc, top, total)
    first_got = swapped(first)
    q, first = lax.optimization_barrier((q, first))
    rot, *state_now, w = call(
        functools.partial(second_kernel, count, group),
        "second_rows",
        [vmem] * 7 + [hbm],
        [rows_shape, state, state, state, shape(out_weight.shape, BF16)],
        1024 * MIB,
        12 * MIB,
        scratch=[dma(())],
    )(q, k_rot, v, p, cosine, sinus, near_got, in_hbm(out_weight))
    early, rot = lax.optimization_barrier((early, rot))
    attend_early = call(
        functools.partial(early_kernel, count), "early_rows", [vmem] * 3, last_shape, 256 * MIB, 4 * MIB
    )
    last = attend_early(early, near_got, p)
    rot, next_got, last, early_got = lax.optimization_barrier((rot, next_got, last, early_got))
    last_got = lax.ppermute(next_got, "ctx", pairs(lambda r: r + 1 - 2 * (r % 2)))
    state_now = call(
        functools.partial(next_kernel, count, group),
        "next_tile",
        [vmem] * 6,
        [state, state, state],
        512 * MIB,
        4 * MIB,
        aliases={3: 0, 4: 1, 5: 2},
    )(rot, next_got, p, *state_now)
    parts = range(cut), range(cut, heads - 1), range(heads - 1, heads)
    rot, first_got = lax.optimization_barrier((rot, first_got))
    seconds, seconds_got = [], []
    for part in parts:
        second = call(
            functools.partial(third_kernel, count, group, part),
            "last_tile",
            [vmem] * 6,
            shape((half, len(part) * HEAD_SIZE), BF16),
            256 * MIB,
            4 * MIB,
        )(rot, last_got, p, *state_now)
        seconds_got.append(swapped(second))
        rot, second, first_got, early_got = lax.optimization_barrier((rot, second, first_got, early_got))
        seconds.append(second)
        if len(seconds) == 2:
            other_near = lax.ppermute(early_got[:, group * HEAD_SIZE :], "ctx", near_pairs)
    sum_shape = shape((half, columns), F32)
    first_sum, partial_sum = call(
        project_kernel, "project_own", [vmem] * 6, [sum_shape, sum_shape], 2048 * MIB, 8 * MIB
    )(first, last, *seconds, w)
    early_got, partial_sum, first_sum = lax.optimization_barrier((early_got, partial_sum, first_sum))
    got_last = attend_early(early_got, other_near, p)
    begun = call(
        first_out_kernel,
        "project_first",
        [vmem] * 4,
        shape((number, columns), BF16),
        1024 * MIB,
        8 * MIB,
        out_specs=hbm,
        scratch=[pltpu.VMEM((half, columns), BF16), dma((tiles,))],
    )(first_got, got_last, first_sum, w)
    begun, partial_sum = lax.optimization_barrier((begun, partial_sum))
    for part, got in zip(parts[:-1], seconds_got):
        partial_sum = call(
            functools.partial(add_kernel, part[0] * HEAD_SIZE),
            "project_second",
            [vmem] * 3,
            sum_shape,
            512 * MIB,
            4 * MIB,
        )(got, partial_sum, w)
    return call(
        functools.partial(last_kernel, parts[-1][0] * HEAD_SIZE),
        "project_last",
        [vmem] * 3 + [hbm],
        shape((number, columns), BF16),
        512 * MIB,
        4 * MIB,
        out_specs=hbm,
        scratch=[pltpu.VMEM((half, columns), BF16), dma((columns // LAST_TILE,))],
        aliases={3: 0},
    )(seconds_got[-1], partial_sum, w, begun)


def solution(mesh):
    in_specs = (P("ctx", "head"), P("ctx", "head"), P("ctx", "head"), P("ctx"), P(None, "head"))
    out_specs = P("ctx", "head")
    return jax.shard_map(shards, mesh=mesh, in_specs=in_specs, out_specs=out_specs, check_vma=False)
```

```python
import functools
import math

import jax
import jax.numpy as jnp
import numpy as np
from jax import lax
from jax.experimental import pallas as pl
from jax.experimental.pallas import tpu as pltpu
from jax.sharding import PartitionSpec as P

HEAD_SIZE = 128
LOWEST = -1e30
FAR = 1 << 16
MIB = 1 << 20
SCORE_SCALE = math.log2(math.e) / math.sqrt(HEAD_SIZE)
BF16, F32 = jnp.bfloat16, jnp.float32


def distance(rank, step, count):
    return jnp.where(rank >= step, step, count - step)


def waits_for_keys(rank):
    return (rank == 1) | (rank == 2)


def first_begin(rank, half):
    return pl.multiple_of(jnp.where(rank < 2, 0, half), half)


def half_positions(p_ref, rank, first):
    half = p_ref.shape[1] // 2
    early = (rank < 2) if first else (rank >= 2)
    return jnp.where(early, p_ref[:, :half], p_ref[:, half:])


def column(row, width):
    return jnp.broadcast_to(row, (width, row.shape[1])).T


def tile_biases(position_row, kinds):
    number = position_row.shape[1]
    position = column(position_row, number)
    query = lax.broadcasted_iota(jnp.int32, (number, number), 0)
    key = lax.broadcasted_iota(jnp.int32, (number, number), 1)
    ahead = key - query
    reach = ahead + position
    found = []
    for pieces, diagonal in kinds:
        allowed = reach >= pieces * number
        if diagonal:
            allowed = allowed & (ahead <= 0)
        found.append(jnp.where(allowed, 0.0, LOWEST).astype(F32))
    return found


def sine_cosine(angle):
    turns = jnp.floor(angle * (2.0 / math.pi) + 0.5)
    rest = ((angle - turns * 1.5703125) - turns * 4.837512969970703e-4) - turns * 7.549789954891888e-8
    square = rest * rest
    sine = ((-1.9515295891e-4 * square + 8.3321608736e-3) * square - 1.6666654611e-1) * square * rest + rest
    cosine = (
        ((2.443315711809948e-5 * square - 1.388731625493765e-3) * square + 4.166664568298827e-2) * square * square
        - 0.5 * square
        + 1.0
    )
    quarter = turns.astype(jnp.int32)
    swap = (quarter & 1) == 1
    out_sine = jnp.where(swap, cosine, sine)
    out_cosine = jnp.where(swap, sine, cosine)
    out_sine = jnp.where((quarter & 2) == 2, -out_sine, out_sine)
    out_cosine = jnp.where(((quarter + 1) & 2) == 2, -out_cosine, out_cosine)
    return out_sine, out_cosine


def turned(block, cosine, sinus):
    wide = block.astype(F32)
    return (wide * cosine + pltpu.roll(wide, HEAD_SIZE // 2, 1) * sinus).astype(BF16)


def scores_of(query, key, bias):
    raw = lax.dot_general(query, key, (((1,), (1,)), ((), ())), preferred_element_type=F32)
    return raw * SCORE_SCALE + bias


def weighted(weights, value):
    return jnp.dot(weights.astype(BF16), value, preferred_element_type=F32)


def spread(entries):
    return jnp.broadcast_to(entries, (entries.shape[0], HEAD_SIZE))


def with_ones(value):
    return jnp.concatenate([value, jnp.ones_like(value)], axis=1)


def head_slices(head, group, width):
    at = slice(head * HEAD_SIZE, (head + 1) * HEAD_SIZE)
    low = head // group * HEAD_SIZE
    return at, slice(low, low + HEAD_SIZE), slice(width + low, width + low + HEAD_SIZE)


def begin_state(query, keys, values, biases):
    scores = [scores_of(query, key, bias) for key, bias in zip(keys, biases)]
    top = jnp.max(functools.reduce(jnp.maximum, scores), axis=1, keepdims=True)
    weights = [jnp.exp2(score - top) for score in scores]
    both = functools.reduce(jnp.add, [weighted(w, value) for w, value in zip(weights, values)])
    return both[:, :HEAD_SIZE], spread(top), both[:, HEAD_SIZE:]


def added_tile(summed, top, total, query, key, value, bias):
    score = scores_of(query, key, bias)
    updated = jnp.maximum(top, spread(jnp.max(score, axis=1, keepdims=True)))
    weights = jnp.exp2(score - jnp.concatenate([updated] * (score.shape[1] // HEAD_SIZE), axis=1))
    factor = jnp.exp2(top - updated)
    both = weighted(weights, value)
    return summed * factor + both[:, :HEAD_SIZE], updated, total * factor + both[:, HEAD_SIZE:]


def finished(state):
    summed, _, total = state
    return (summed * (1.0 / total)).astype(BF16)


def keys_kernel(
    count, k_hbm, v_hbm, q_hbm, p_hbm, f_hbm, near_ref, next_ref, rot_ref, v_ref, q_ref, p_ref, cos_ref, sin_ref,
    k_ref, f_ref, sems,
):
    pairs = ((p_hbm, p_ref), (f_hbm, f_ref), (k_hbm, k_ref), (v_hbm, v_ref), (q_hbm, q_ref))
    copies = [pltpu.make_async_copy(source, target, sems.at[i]) for i, (source, target) in enumerate(pairs)]
    for copy in copies:
        copy.start()
    rank = lax.axis_index("ctx")
    half = k_ref.shape[0] // 2
    width = k_ref.shape[1]
    copies[0].wait()
    copies[1].wait()
    position = p_ref[...].astype(F32)
    early = column(position[:, :half], HEAD_SIZE)
    late = column(position[:, half:], HEAD_SIZE)
    lane = lax.broadcasted_iota(jnp.int32, (half, HEAD_SIZE), 1)
    front = lane < HEAD_SIZE // 2
    sine, cosine = sine_cosine(jnp.where(front, early, late) * f_ref[...])
    sine_other = pltpu.roll(sine, HEAD_SIZE // 2, 1)
    cosine_other = pltpu.roll(cosine, HEAD_SIZE // 2, 1)
    cos_ref[:half] = jnp.where(front, cosine, cosine_other)
    cos_ref[half:] = jnp.where(front, cosine_other, cosine)
    sin_ref[:half] = jnp.where(front, -sine, sine_other)
    sin_ref[half:] = jnp.where(front, -sine_other, sine)
    copies[2].wait()
    for head in range(width // HEAD_SIZE):
        at = slice(head * HEAD_SIZE, (head + 1) * HEAD_SIZE)
        rot_ref[:, at] = turned(k_ref[:, at], cos_ref[...], sin_ref[...])
    copies[3].wait()
    wrap = (rank % 2 == 1) & (rank + 3 >= count)
    rows = pl.ds(pl.multiple_of(jnp.where(wrap, half, 0), half), half)
    near_ref[:, :width] = rot_ref[rows, :]
    near_ref[:, width:] = v_ref[rows, :]
    rows = pl.ds(pl.multiple_of(jnp.where(rank + 2 >= count, half, 0), half), half)
    next_ref[:, :width] = rot_ref[rows, :]
    next_ref[:, width:] = v_ref[rows, :]
    copies[4].wait()


def pack_kernel(q_ref, k_ref, v_ref, cos_ref, sin_ref, out_ref):
    rank = lax.axis_index("ctx")
    half, width = out_ref.shape[0], k_ref.shape[1]
    rows = pl.ds(first_begin(rank, half), half)
    begin, late = out_ref.shape[1] - 2 * HEAD_SIZE, slice(width - HEAD_SIZE, width)
    out_ref[:, begin : begin + HEAD_SIZE] = k_ref[rows, late]
    out_ref[:, begin + HEAD_SIZE :] = v_ref[rows, late]
    low = q_ref.shape[1] - begin
    for head in range(begin // HEAD_SIZE):
        at = slice(head * HEAD_SIZE, (head + 1) * HEAD_SIZE)
        source = slice(low + head * HEAD_SIZE, low + (head + 1) * HEAD_SIZE)
        out_ref[:, at] = turned(q_ref[rows, source], cos_ref[rows, :], sin_ref[rows, :])


def own_kernel(group, q_ref, k_ref, v_ref, p_ref, cos_ref, sin_ref, out_ref, rot_ref, acc_ref, top_ref, sum_ref):
    rank = lax.axis_index("ctx")
    half = q_ref.shape[0] // 2
    rows = pl.ds(first_begin(rank, half), half)
    biases = tile_biases(half_positions(p_ref, rank, True), [(0, True)])
    for head in range(rot_ref.shape[1] // HEAD_SIZE):
        at, shared, _ = head_slices(head, group, 0)
        query = turned(q_ref[rows, at], cos_ref[rows, :], sin_ref[rows, :])
        rot_ref[:, at] = query
        if head % group == 0:
            key = k_ref[rows, shared]
            value = with_ones(v_ref[rows, shared])
        for low, high in ((0, half // 2), (half // 2, half)):
            part = slice(low, high)
            summed, top, total = begin_state(query[part], [key[:high]], [value[:high]], [biases[0][part, :high]])
            acc_ref[part, at] = summed
            top_ref[part, at] = top
            sum_ref[part, at] = total
            out_ref[part, at] = (summed * (1.0 / total)).astype(BF16)


def first_kernel(count, group, own_ref, rot_ref, kv_ref, p_ref, acc_ref, top_ref, sum_ref, out_ref):
    rank = lax.axis_index("ctx")
    width = kv_ref.shape[1] // 2
    depth = rot_ref.shape[1]
    step = jnp.where(rank % 2 == 1, 1, 3)
    used = waits_for_keys(rank)
    @pl.when(used)
    def _():
        biases = tile_biases(half_positions(p_ref, rank, True), [(distance(rank, step, count), False)])
        for head in range(depth // HEAD_SIZE):
            at, key_at, value_at = head_slices(head, group, width)
            state = acc_ref[:, at], top_ref[:, at], sum_ref[:, at]
            if head % group == 0:
                value = with_ones(kv_ref[:, value_at])
            out_ref[:, at] = finished(added_tile(*state, rot_ref[:, at], kv_ref[:, key_at], value, *biases))

    @pl.when(jnp.logical_not(used))
    def _():
        out_ref[...] = own_ref[...]


def early_kernel(count, early_ref, near_ref, p_ref, out_ref):
    rank = lax.axis_index("ctx")
    depth = out_ref.shape[1]
    width = near_ref.shape[1] // 2
    step = jnp.where(rank % 2 == 1, 1, 3)
    reach = jnp.where(waits_for_keys(rank), distance(rank, step, count), FAR)
    biases = tile_biases(half_positions(p_ref, rank, True), [(0, True), (reach, False)])
    keys = [early_ref[:, depth : depth + HEAD_SIZE], near_ref[:, width - HEAD_SIZE : width]]
    values = [with_ones(early_ref[:, depth + HEAD_SIZE :]), with_ones(near_ref[:, 2 * width - HEAD_SIZE :])]
    for head in range(depth // HEAD_SIZE):
        at = slice(head * HEAD_SIZE, (head + 1) * HEAD_SIZE)
        out_ref[:, at] = finished(begin_state(early_ref[:, at], keys, values, biases))


def second_kernel(
    count, group, q_ref, k_ref, v_ref, p_ref, cos_ref, sin_ref, kv_ref, w_hbm, rot_ref, acc_ref, top_ref, sum_ref, w_ref, sem
):
    copy = pltpu.make_async_copy(w_hbm, w_ref, sem)
    copy.start()
    rank = lax.axis_index("ctx")
    half = q_ref.shape[0] // 2
    width = k_ref.shape[1]
    rows = pl.ds(pl.multiple_of(half - first_begin(rank, half), half), half)
    step = jnp.where(rank % 2 == 1, 1, 3)
    reach = jnp.where(waits_for_keys(rank), FAR, distance(rank, step, count))
    biases = tile_biases(half_positions(p_ref, rank, False), [(0, True), (reach, False)])
    for head in range(q_ref.shape[1] // HEAD_SIZE):
        at, key_at, value_at = head_slices(head, group, width)
        query = turned(q_ref[rows, at], cos_ref[rows, :], sin_ref[rows, :])
        rot_ref[:, at] = query
        keys = [k_ref[rows, key_at], kv_ref[:, key_at]]
        if head % group == 0:
            values = [with_ones(v_ref[rows, key_at]), with_ones(kv_ref[:, value_at])]
        acc_ref[:, at], top_ref[:, at], sum_ref[:, at] = begin_state(query, keys, values, biases)
    copy.wait()


def next_kernel(count, group, rot_ref, kv_ref, p_ref, acc_ref, top_ref, sum_ref, *outs):
    rank = lax.axis_index("ctx")
    width = kv_ref.shape[1] // 2
    biases = tile_biases(half_positions(p_ref, rank, False), [(distance(rank, 2, count), False)])
    for head in range(rot_ref.shape[1] // HEAD_SIZE):
        at, key_at, value_at = head_slices(head, group, width)
        state = acc_ref[:, at], top_ref[:, at], sum_ref[:, at]
        if head % group == 0:
            value = with_ones(kv_ref[:, value_at])
        state = added_tile(*state, rot_ref[:, at], kv_ref[:, key_at], value, *biases)
        for out_ref, entries in zip(outs, state):
            out_ref[:, at] = entries


def third_kernel(count, group, heads, rot_ref, kv_ref, p_ref, acc_ref, top_ref, sum_ref, out_ref):
    rank = lax.axis_index("ctx")
    width = kv_ref.shape[1] // 2
    step = jnp.where(rank % 2 == 1, 3, 1)
    biases = tile_biases(half_positions(p_ref, rank, False), [(distance(rank, step, count), False)])
    for number, head in enumerate(heads):
        at, key_at, value_at = head_slices(head, group, width)
        state = acc_ref[:, at], top_ref[:, at], sum_ref[:, at]
        if number == 0 or head % group == 0:
            value = with_ones(kv_ref[:, value_at])
        state = added_tile(*state, rot_ref[:, at], kv_ref[:, key_at], value, *biases)
        out_ref[:, number * HEAD_SIZE : (number + 1) * HEAD_SIZE] = finished(state)


def dot(left, right):
    return jnp.dot(left, right, preferred_element_type=F32)


TILE = 512
LAST_TILE = 256


def other_rows(w_ref, begin, end):
    depth = w_ref.shape[0] // 2
    base = (1 - lax.axis_index("head")) * depth
    return pl.ds(pl.multiple_of(base + begin, HEAD_SIZE), end - begin)


def project_kernel(first_ref, last_ref, second0_ref, second1_ref, second2_ref, w_ref, sum_ref, part_ref):
    half, depth = first_ref.shape[0], w_ref.shape[0] // 2
    mine = pl.ds(pl.multiple_of(lax.axis_index("head") * depth, depth), depth)
    first = jnp.concatenate([first_ref[...], last_ref[...]], axis=1)
    second = jnp.concatenate([second0_ref[...], second1_ref[...], second2_ref[...]], axis=1)
    stacked = jnp.concatenate([first, second], axis=0)
    for tile in range(w_ref.shape[1] // TILE):
        at = slice(tile * TILE, (tile + 1) * TILE)
        both = dot(stacked, w_ref[mine, at])
        sum_ref[:, at] = both[:half]
        part_ref[:, at] = both[half:]


def first_out_kernel(got_ref, got_last_ref, sum_ref, w_ref, out_hbm, held_ref, sems):
    rank = lax.axis_index("ctx")
    half, depth = got_ref.shape[0], w_ref.shape[0] // 2
    rows = pl.ds(first_begin(rank, half), half)
    other = other_rows(w_ref, 0, depth)
    got = jnp.concatenate([got_ref[...], got_last_ref[...]], axis=1)
    copies = []
    for tile in range(w_ref.shape[1] // TILE):
        at = slice(tile * TILE, (tile + 1) * TILE)
        held_ref[:, at] = (sum_ref[:, at] + dot(got, w_ref[other, at])).astype(BF16)
        copies.append(pltpu.make_async_copy(held_ref.at[:, at], out_hbm.at[rows, at], sems.at[tile]))
        copies[-1].start()
    for copy in copies:
        copy.wait()


def add_kernel(begin, got_ref, part_ref, w_ref, out_ref):
    rows = other_rows(w_ref, begin, begin + got_ref.shape[1])
    for start in range(0, w_ref.shape[1], TILE):
        at = slice(start, start + TILE)
        out_ref[:, at] = part_ref[:, at] + dot(got_ref[...], w_ref[rows, at])


def last_kernel(begin, got_ref, part_ref, w_ref, begun_hbm, out_hbm, held_ref, sems):
    del begun_hbm
    rank = lax.axis_index("ctx")
    half, depth = got_ref.shape
    out_rows = pl.ds(pl.multiple_of(half - first_begin(rank, half), half), half)
    rows = other_rows(w_ref, begin, begin + depth)
    copies = []
    for tile in range(w_ref.shape[1] // LAST_TILE):
        at = slice(tile * LAST_TILE, (tile + 1) * LAST_TILE)
        added = dot(got_ref[...], w_ref[rows, at])
        held_ref[:, at] = (part_ref[:, at] + added).astype(BF16)
        copies.append(pltpu.make_async_copy(held_ref.at[:, at], out_hbm.at[out_rows, at], sems.at[tile]))
        copies[-1].start()
    for copy in copies:
        copy.wait()


def shards(queries, keys, values, positions, out_weight):
    number, width = queries.shape
    half = number // 2
    count = lax.axis_size("ctx")
    group = width // keys.shape[1]
    columns = out_weight.shape[1]
    tiles = columns // TILE
    in_hbm = lambda array: pltpu.with_memory_space_constraint(array, pltpu.HBM)
    position_row = positions.reshape(1, number)
    table = np.power(500000.0, -2.0 * np.arange(HEAD_SIZE // 2) / HEAD_SIZE).astype(np.float32)
    frequency = jnp.asarray(np.concatenate([table, table])[None, :])
    shape = jax.ShapeDtypeStruct
    vmem = pl.BlockSpec(memory_space=pltpu.VMEM)
    hbm = pl.BlockSpec(memory_space=pltpu.HBM)
    dma = pltpu.SemaphoreType.DMA

    def call(body, name, ins, outs, flops, nbytes, out_specs=None, scratch=(), aliases={}):
        return pl.pallas_call(
            body,
            name=name,
            in_specs=ins,
            out_shape=outs,
            out_specs=out_specs if out_specs is not None else jax.tree.map(lambda _: vmem, outs),
            scratch_shapes=scratch,
            input_output_aliases=aliases,
            compiler_params=pltpu.CompilerParams(vmem_limit_bytes=32 * MIB),
            cost_estimate=pl.CostEstimate(flops=flops, bytes_accessed=nbytes, transcendentals=0),
        )

    def pairs(target_of):
        found = [(source, target_of(source) % count) for source in range(count)]
        assert sorted(target for _, target in found) == list(range(count))
        return found

    def swapped(array):
        return lax.ppermute(array, "head", [(0, 1), (1, 0)])

    kv_shape = shape((half, 2 * keys.shape[1]), BF16)
    table_shape = shape((number, HEAD_SIZE), F32)
    rows_shape, state = shape((half, width), BF16), shape((half, width), F32)
    heads = width // HEAD_SIZE
    moved = group - 1
    cut = heads - moved
    some_shape = shape((half, cut * HEAD_SIZE), BF16)
    some_state = shape((half, cut * HEAD_SIZE), F32)
    last_shape = shape((half, moved * HEAD_SIZE), BF16)
    near, onward, k_rot, v, q, p, cosine, sinus = call(
        functools.partial(keys_kernel, count),
        "rotate_keys",
        [hbm] * 5,
        [kv_shape, kv_shape]
        + [shape(keys.shape, BF16)] * 2
        + [shape(queries.shape, BF16), shape((1, number), jnp.int32), table_shape, table_shape],
        4 * MIB,
        4 * MIB,
        scratch=[pltpu.VMEM(keys.shape, BF16), pltpu.VMEM((1, HEAD_SIZE), F32), dma((5,))],
    )(*(in_hbm(array) for array in (keys, values, queries, position_row, frequency)))
    near_pairs = pairs(lambda r: r + 3 if r % 2 else r + 1)
    near_got = lax.ppermute(near, "ctx", near_pairs)
    early = call(pack_kernel, "pack_early", [vmem] * 5, shape((half, (moved + 2) * HEAD_SIZE), BF16), MIB, MIB)(
        q, k_rot, v, cosine, sinus
    )
    early, q = lax.optimization_barrier((early, q))
    early_got = swapped(early)
    own, rot, acc, top, total = call(
        functools.partial(own_kernel, group),
        "own_tiles",
        [vmem] * 6,
        [some_shape, some_shape, some_state, some_state, some_state],
        256 * MIB,
        4 * MIB,
    )(q, k_rot, v, p, cosine, sinus)
    onward, rot = lax.optimization_barrier((onward, rot))
    next_got = lax.ppermute(onward, "ctx", pairs(lambda r: r + 2))
    first = call(
        functools.partial(first_kernel, count, group),
        "first_rows",
        [vmem] * 7,
        some_shape,
        256 * MIB,
        4 * MIB,
    )(own, rot, near_got, p, acc, top, total)
    first_got = swapped(first)
    q, first = lax.optimization_barrier((q, first))
    rot, *state_now, w = call(
        functools.partial(second_kernel, count, group),
        "second_rows",
        [vmem] * 7 + [hbm],
        [rows_shape, state, state, state, shape(out_weight.shape, BF16)],
        1024 * MIB,
        12 * MIB,
        scratch=[dma(())],
    )(q, k_rot, v, p, cosine, sinus, near_got, in_hbm(out_weight))
    rot, early_got = lax.optimization_barrier((rot, early_got))
    other_near = lax.ppermute(early_got[:, moved * HEAD_SIZE :], "ctx", near_pairs)
    rot, next_got = lax.optimization_barrier((rot, next_got))
    last_got = lax.ppermute(next_got, "ctx", pairs(lambda r: r + 1 - 2 * (r % 2)))
    state_now = call(
        functools.partial(next_kernel, count, group),
        "next_tile",
        [vmem] * 6,
        [state, state, state],
        512 * MIB,
        4 * MIB,
        aliases={3: 0, 4: 1, 5: 2},
    )(rot, next_got, p, *state_now)
    parts = range(heads // 2), range(heads // 2, heads - 1), range(heads - 1, heads)
    seconds, seconds_got = [], []
    for part in parts:
        second = call(
            functools.partial(third_kernel, count, group, part),
            "last_tile",
            [vmem] * 6,
            shape((half, len(part) * HEAD_SIZE), BF16),
            256 * MIB,
            4 * MIB,
        )(rot, last_got, p, *state_now)
        seconds_got.append(swapped(second))
        if len(seconds) == 0:
            rot, second, first_got = lax.optimization_barrier((rot, second, first_got))
        else:
            rot, second, other_near, early = lax.optimization_barrier((rot, second, other_near, early))
        seconds.append(second)
    attend_early = call(
        functools.partial(early_kernel, count), "early_rows", [vmem] * 3, last_shape, 256 * MIB, 4 * MIB
    )
    last = attend_early(early, near_got, p)
    sum_shape = shape((half, columns), F32)
    first_sum, partial_sum = call(
        project_kernel, "project_own", [vmem] * 6, [sum_shape, sum_shape], 2048 * MIB, 8 * MIB
    )(first, last, *seconds, w)
    early_got, partial_sum, first_sum = lax.optimization_barrier((early_got, partial_sum, first_sum))
    got_last = attend_early(early_got, other_near, p)
    begun = call(
        first_out_kernel,
        "project_first",
        [vmem] * 4,
        shape((number, columns), BF16),
        1024 * MIB,
        8 * MIB,
        out_specs=hbm,
        scratch=[pltpu.VMEM((half, columns), BF16), dma((tiles,))],
    )(first_got, got_last, first_sum, w)
    begun, partial_sum = lax.optimization_barrier((begun, partial_sum))
    for part, got in zip(parts[:-1], seconds_got):
        partial_sum = call(
            functools.partial(add_kernel, part[0] * HEAD_SIZE),
            "project_second",
            [vmem] * 3,
            sum_shape,
            512 * MIB,
            4 * MIB,
        )(got, partial_sum, w)
    return call(
        functools.partial(last_kernel, parts[-1][0] * HEAD_SIZE),
        "project_last",
        [vmem] * 3 + [hbm],
        shape((number, columns), BF16),
        512 * MIB,
        4 * MIB,
        out_specs=hbm,
        scratch=[pltpu.VMEM((half, columns), BF16), dma((columns // LAST_TILE,))],
        aliases={3: 0},
    )(seconds_got[-1], partial_sum, w, begun)


def solution(mesh):
    in_specs = (P("ctx", "head"), P("ctx", "head"), P("ctx", "head"), P("ctx"), P(None, "head"))
    out_specs = P("ctx", "head")
    return jax.shard_map(shards, mesh=mesh, in_specs=in_specs, out_specs=out_specs, check_vma=False)
```

```python
import functools
import math

import jax
import jax.numpy as jnp
import numpy as np
from jax import lax
from jax.experimental import pallas as pl
from jax.experimental.pallas import tpu as pltpu
from jax.sharding import PartitionSpec as P

HEAD_SIZE = 128
LOWEST = -1e30
FAR = 1 << 16
MIB = 1 << 20
SCORE_SCALE = math.log2(math.e) / math.sqrt(HEAD_SIZE)
BF16, F32 = jnp.bfloat16, jnp.float32


def distance(rank, step, count):
    return jnp.where(rank >= step, step, count - step)


def waits_for_keys(rank):
    return (rank == 1) | (rank == 2)


def first_begin(rank, half):
    return pl.multiple_of(jnp.where(rank < 2, 0, half), half)


def half_positions(p_ref, rank, first):
    half = p_ref.shape[1] // 2
    early = (rank < 2) if first else (rank >= 2)
    return jnp.where(early, p_ref[:, :half], p_ref[:, half:])


def column(row, width):
    return jnp.broadcast_to(row, (width, row.shape[1])).T


def tile_biases(position_row, kinds):
    number = position_row.shape[1]
    position = column(position_row, number)
    query = lax.broadcasted_iota(jnp.int32, (number, number), 0)
    key = lax.broadcasted_iota(jnp.int32, (number, number), 1)
    ahead = key - query
    reach = ahead + position
    found = []
    for pieces, diagonal in kinds:
        allowed = reach >= pieces * number
        if diagonal:
            allowed = allowed & (ahead <= 0)
        found.append(jnp.where(allowed, 0.0, LOWEST).astype(F32))
    return found


def sine_cosine(angle):
    turns = jnp.floor(angle * (2.0 / math.pi) + 0.5)
    rest = ((angle - turns * 1.5703125) - turns * 4.837512969970703e-4) - turns * 7.549789954891888e-8
    square = rest * rest
    sine = ((-1.9515295891e-4 * square + 8.3321608736e-3) * square - 1.6666654611e-1) * square * rest + rest
    cosine = (
        ((2.443315711809948e-5 * square - 1.388731625493765e-3) * square + 4.166664568298827e-2) * square * square
        - 0.5 * square
        + 1.0
    )
    quarter = turns.astype(jnp.int32)
    swap = (quarter & 1) == 1
    out_sine = jnp.where(swap, cosine, sine)
    out_cosine = jnp.where(swap, sine, cosine)
    out_sine = jnp.where((quarter & 2) == 2, -out_sine, out_sine)
    out_cosine = jnp.where(((quarter + 1) & 2) == 2, -out_cosine, out_cosine)
    return out_sine, out_cosine


def turned(block, cosine, sinus):
    wide = block.astype(F32)
    return (wide * cosine + pltpu.roll(wide, HEAD_SIZE // 2, 1) * sinus).astype(BF16)


def scores_of(query, key, bias):
    raw = lax.dot_general(query, key, (((1,), (1,)), ((), ())), preferred_element_type=F32)
    return raw * SCORE_SCALE + bias


def weighted(weights, value):
    return jnp.dot(weights.astype(BF16), value, preferred_element_type=F32)


def spread(entries):
    return jnp.broadcast_to(entries, (entries.shape[0], HEAD_SIZE))


def with_ones(value):
    return jnp.concatenate([value, jnp.ones_like(value)], axis=1)


def head_slices(head, group, width):
    at = slice(head * HEAD_SIZE, (head + 1) * HEAD_SIZE)
    low = head // group * HEAD_SIZE
    return at, slice(low, low + HEAD_SIZE), slice(width + low, width + low + HEAD_SIZE)


def begin_state(query, keys, values, biases):
    scores = [scores_of(query, key, bias) for key, bias in zip(keys, biases)]
    top = jnp.max(functools.reduce(jnp.maximum, scores), axis=1, keepdims=True)
    weights = [jnp.exp2(score - top) for score in scores]
    both = functools.reduce(jnp.add, [weighted(w, value) for w, value in zip(weights, values)])
    return both[:, :HEAD_SIZE], spread(top), both[:, HEAD_SIZE:]


def added_tile(summed, top, total, query, key, value, bias):
    score = scores_of(query, key, bias)
    updated = jnp.maximum(top, spread(jnp.max(score, axis=1, keepdims=True)))
    weights = jnp.exp2(score - jnp.concatenate([updated] * (score.shape[1] // HEAD_SIZE), axis=1))
    factor = jnp.exp2(top - updated)
    both = weighted(weights, value)
    return summed * factor + both[:, :HEAD_SIZE], updated, total * factor + both[:, HEAD_SIZE:]


def finished(state):
    summed, _, total = state
    return (summed * (1.0 / total)).astype(BF16)


def keys_kernel(
    count, k_hbm, v_hbm, q_hbm, p_hbm, f_hbm, near_ref, next_ref, rot_ref, v_ref, q_ref, p_ref, cos_ref, sin_ref,
    k_ref, f_ref, sems,
):
    pairs = ((p_hbm, p_ref), (f_hbm, f_ref), (k_hbm, k_ref), (v_hbm, v_ref), (q_hbm, q_ref))
    copies = [pltpu.make_async_copy(source, target, sems.at[i]) for i, (source, target) in enumerate(pairs)]
    for copy in copies:
        copy.start()
    rank = lax.axis_index("ctx")
    half = k_ref.shape[0] // 2
    width = k_ref.shape[1]
    copies[0].wait()
    copies[1].wait()
    position = p_ref[...].astype(F32)
    early = column(position[:, :half], HEAD_SIZE)
    late = column(position[:, half:], HEAD_SIZE)
    lane = lax.broadcasted_iota(jnp.int32, (half, HEAD_SIZE), 1)
    front = lane < HEAD_SIZE // 2
    sine, cosine = sine_cosine(jnp.where(front, early, late) * f_ref[...])
    sine_other = pltpu.roll(sine, HEAD_SIZE // 2, 1)
    cosine_other = pltpu.roll(cosine, HEAD_SIZE // 2, 1)
    cos_ref[:half] = jnp.where(front, cosine, cosine_other)
    cos_ref[half:] = jnp.where(front, cosine_other, cosine)
    sin_ref[:half] = jnp.where(front, -sine, sine_other)
    sin_ref[half:] = jnp.where(front, -sine_other, sine)
    copies[2].wait()
    for head in range(width // HEAD_SIZE):
        at = slice(head * HEAD_SIZE, (head + 1) * HEAD_SIZE)
        rot_ref[:, at] = turned(k_ref[:, at], cos_ref[...], sin_ref[...])
    copies[3].wait()
    wrap = (rank % 2 == 1) & (rank + 3 >= count)
    rows = pl.ds(pl.multiple_of(jnp.where(wrap, half, 0), half), half)
    near_ref[:, :width] = rot_ref[rows, :]
    near_ref[:, width:] = v_ref[rows, :]
    rows = pl.ds(pl.multiple_of(jnp.where(rank + 2 >= count, half, 0), half), half)
    next_ref[:, :width] = rot_ref[rows, :]
    next_ref[:, width:] = v_ref[rows, :]
    copies[4].wait()


def pack_kernel(q_ref, k_ref, v_ref, cos_ref, sin_ref, out_ref):
    rank = lax.axis_index("ctx")
    half, width = out_ref.shape[0], k_ref.shape[1]
    rows = pl.ds(first_begin(rank, half), half)
    begin, late = out_ref.shape[1] - 2 * HEAD_SIZE, slice(width - HEAD_SIZE, width)
    out_ref[:, begin : begin + HEAD_SIZE] = k_ref[rows, late]
    out_ref[:, begin + HEAD_SIZE :] = v_ref[rows, late]
    low = q_ref.shape[1] - begin
    for head in range(begin // HEAD_SIZE):
        at = slice(head * HEAD_SIZE, (head + 1) * HEAD_SIZE)
        source = slice(low + head * HEAD_SIZE, low + (head + 1) * HEAD_SIZE)
        out_ref[:, at] = turned(q_ref[rows, source], cos_ref[rows, :], sin_ref[rows, :])


def own_kernel(group, q_ref, k_ref, v_ref, p_ref, cos_ref, sin_ref, out_ref, rot_ref, acc_ref, top_ref, sum_ref):
    rank = lax.axis_index("ctx")
    half = q_ref.shape[0] // 2
    rows = pl.ds(first_begin(rank, half), half)
    biases = tile_biases(half_positions(p_ref, rank, True), [(0, True)])
    for head in range(rot_ref.shape[1] // HEAD_SIZE):
        at, shared, _ = head_slices(head, group, 0)
        query = turned(q_ref[rows, at], cos_ref[rows, :], sin_ref[rows, :])
        rot_ref[:, at] = query
        if head % group == 0:
            key = k_ref[rows, shared]
            value = with_ones(v_ref[rows, shared])
        for low, high in ((0, half // 2), (half // 2, half)):
            part = slice(low, high)
            summed, top, total = begin_state(query[part], [key[:high]], [value[:high]], [biases[0][part, :high]])
            acc_ref[part, at] = summed
            top_ref[part, at] = top
            sum_ref[part, at] = total
            out_ref[part, at] = (summed * (1.0 / total)).astype(BF16)


def first_kernel(count, group, own_ref, rot_ref, kv_ref, p_ref, acc_ref, top_ref, sum_ref, out_ref):
    rank = lax.axis_index("ctx")
    width = kv_ref.shape[1] // 2
    depth = rot_ref.shape[1]
    step = jnp.where(rank % 2 == 1, 1, 3)
    used = waits_for_keys(rank)
    @pl.when(used)
    def _():
        biases = tile_biases(half_positions(p_ref, rank, True), [(distance(rank, step, count), False)])
        for head in range(depth // HEAD_SIZE):
            at, key_at, value_at = head_slices(head, group, width)
            state = acc_ref[:, at], top_ref[:, at], sum_ref[:, at]
            if head % group == 0:
                value = with_ones(kv_ref[:, value_at])
            out_ref[:, at] = finished(added_tile(*state, rot_ref[:, at], kv_ref[:, key_at], value, *biases))

    @pl.when(jnp.logical_not(used))
    def _():
        out_ref[...] = own_ref[...]


def early_kernel(count, early_ref, near_ref, p_ref, out_ref):
    rank = lax.axis_index("ctx")
    depth = out_ref.shape[1]
    width = near_ref.shape[1] // 2
    step = jnp.where(rank % 2 == 1, 1, 3)
    reach = jnp.where(waits_for_keys(rank), distance(rank, step, count), FAR)
    biases = tile_biases(half_positions(p_ref, rank, True), [(0, True), (reach, False)])
    keys = [early_ref[:, depth : depth + HEAD_SIZE], near_ref[:, width - HEAD_SIZE : width]]
    values = [with_ones(early_ref[:, depth + HEAD_SIZE :]), with_ones(near_ref[:, 2 * width - HEAD_SIZE :])]
    for head in range(depth // HEAD_SIZE):
        at = slice(head * HEAD_SIZE, (head + 1) * HEAD_SIZE)
        out_ref[:, at] = finished(begin_state(early_ref[:, at], keys, values, biases))


def second_kernel(
    count, group, q_ref, k_ref, v_ref, p_ref, cos_ref, sin_ref, kv_ref, w_hbm, rot_ref, acc_ref, top_ref, sum_ref, w_ref, sem
):
    copy = pltpu.make_async_copy(w_hbm, w_ref, sem)
    copy.start()
    rank = lax.axis_index("ctx")
    half = q_ref.shape[0] // 2
    width = k_ref.shape[1]
    rows = pl.ds(pl.multiple_of(half - first_begin(rank, half), half), half)
    step = jnp.where(rank % 2 == 1, 1, 3)
    reach = jnp.where(waits_for_keys(rank), FAR, distance(rank, step, count))
    biases = tile_biases(half_positions(p_ref, rank, False), [(0, True), (reach, False)])
    for head in range(q_ref.shape[1] // HEAD_SIZE):
        at, key_at, value_at = head_slices(head, group, width)
        query = turned(q_ref[rows, at], cos_ref[rows, :], sin_ref[rows, :])
        rot_ref[:, at] = query
        keys = [k_ref[rows, key_at], kv_ref[:, key_at]]
        if head % group == 0:
            values = [with_ones(v_ref[rows, key_at]), with_ones(kv_ref[:, value_at])]
        acc_ref[:, at], top_ref[:, at], sum_ref[:, at] = begin_state(query, keys, values, biases)
    copy.wait()


def next_kernel(count, group, rot_ref, kv_ref, p_ref, acc_ref, top_ref, sum_ref, *outs):
    rank = lax.axis_index("ctx")
    width = kv_ref.shape[1] // 2
    biases = tile_biases(half_positions(p_ref, rank, False), [(distance(rank, 2, count), False)])
    for head in range(rot_ref.shape[1] // HEAD_SIZE):
        at, key_at, value_at = head_slices(head, group, width)
        state = acc_ref[:, at], top_ref[:, at], sum_ref[:, at]
        if head % group == 0:
            value = with_ones(kv_ref[:, value_at])
        state = added_tile(*state, rot_ref[:, at], kv_ref[:, key_at], value, *biases)
        for out_ref, entries in zip(outs, state):
            out_ref[:, at] = entries


def third_kernel(count, group, heads, rot_ref, kv_ref, p_ref, acc_ref, top_ref, sum_ref, out_ref):
    rank = lax.axis_index("ctx")
    width = kv_ref.shape[1] // 2
    step = jnp.where(rank % 2 == 1, 3, 1)
    biases = tile_biases(half_positions(p_ref, rank, False), [(distance(rank, step, count), False)])
    for number, head in enumerate(heads):
        at, key_at, value_at = head_slices(head, group, width)
        state = acc_ref[:, at], top_ref[:, at], sum_ref[:, at]
        if number == 0 or head % group == 0:
            value = with_ones(kv_ref[:, value_at])
        state = added_tile(*state, rot_ref[:, at], kv_ref[:, key_at], value, *biases)
        out_ref[:, number * HEAD_SIZE : (number + 1) * HEAD_SIZE] = finished(state)


def dot(left, right):
    return jnp.dot(left, right, preferred_element_type=F32)


TILE = 512
LAST_TILE = 256


def other_rows(w_ref, begin, end):
    depth = w_ref.shape[0] // 2
    base = (1 - lax.axis_index("head")) * depth
    return pl.ds(pl.multiple_of(base + begin, HEAD_SIZE), end - begin)


def project_kernel(first_ref, last_ref, second0_ref, second1_ref, second2_ref, w_ref, sum_ref, part_ref):
    half, depth = first_ref.shape[0], w_ref.shape[0] // 2
    mine = pl.ds(pl.multiple_of(lax.axis_index("head") * depth, depth), depth)
    first = jnp.concatenate([first_ref[...], last_ref[...]], axis=1)
    second = jnp.concatenate([second0_ref[...], second1_ref[...], second2_ref[...]], axis=1)
    stacked = jnp.concatenate([first, second], axis=0)
    for tile in range(w_ref.shape[1] // TILE):
        at = slice(tile * TILE, (tile + 1) * TILE)
        both = dot(stacked, w_ref[mine, at])
        sum_ref[:, at] = both[:half]
        part_ref[:, at] = both[half:]


def first_out_kernel(got_ref, got_last_ref, sum_ref, w_ref, out_hbm, held_ref, sems):
    rank = lax.axis_index("ctx")
    half, depth = got_ref.shape[0], w_ref.shape[0] // 2
    rows = pl.ds(first_begin(rank, half), half)
    other = other_rows(w_ref, 0, depth)
    got = jnp.concatenate([got_ref[...], got_last_ref[...]], axis=1)
    copies = []
    for tile in range(w_ref.shape[1] // TILE):
        at = slice(tile * TILE, (tile + 1) * TILE)
        held_ref[:, at] = (sum_ref[:, at] + dot(got, w_ref[other, at])).astype(BF16)
        copies.append(pltpu.make_async_copy(held_ref.at[:, at], out_hbm.at[rows, at], sems.at[tile]))
        copies[-1].start()
    for copy in copies:
        copy.wait()


def add_kernel(begin, got_ref, part_ref, w_ref, out_ref):
    rows = other_rows(w_ref, begin, begin + got_ref.shape[1])
    for start in range(0, w_ref.shape[1], TILE):
        at = slice(start, start + TILE)
        out_ref[:, at] = part_ref[:, at] + dot(got_ref[...], w_ref[rows, at])


def last_kernel(begin, got_ref, part_ref, w_ref, begun_hbm, out_hbm, held_ref, sems):
    del begun_hbm
    rank = lax.axis_index("ctx")
    half, depth = got_ref.shape
    out_rows = pl.ds(pl.multiple_of(half - first_begin(rank, half), half), half)
    rows = other_rows(w_ref, begin, begin + depth)
    copies = []
    for tile in range(w_ref.shape[1] // LAST_TILE):
        at = slice(tile * LAST_TILE, (tile + 1) * LAST_TILE)
        added = dot(got_ref[...], w_ref[rows, at])
        held_ref[:, at] = (part_ref[:, at] + added).astype(BF16)
        copies.append(pltpu.make_async_copy(held_ref.at[:, at], out_hbm.at[out_rows, at], sems.at[tile]))
        copies[-1].start()
    for copy in copies:
        copy.wait()


def shards(queries, keys, values, positions, out_weight):
    number, width = queries.shape
    half = number // 2
    count = lax.axis_size("ctx")
    group = width // keys.shape[1]
    columns = out_weight.shape[1]
    tiles = columns // TILE
    in_hbm = lambda array: pltpu.with_memory_space_constraint(array, pltpu.HBM)
    position_row = positions.reshape(1, number)
    table = np.power(500000.0, -2.0 * np.arange(HEAD_SIZE // 2) / HEAD_SIZE).astype(np.float32)
    frequency = jnp.asarray(np.concatenate([table, table])[None, :])
    shape = jax.ShapeDtypeStruct
    vmem = pl.BlockSpec(memory_space=pltpu.VMEM)
    hbm = pl.BlockSpec(memory_space=pltpu.HBM)
    dma = pltpu.SemaphoreType.DMA

    def call(body, name, ins, outs, flops, nbytes, out_specs=None, scratch=(), aliases={}):
        return pl.pallas_call(
            body,
            name=name,
            in_specs=ins,
            out_shape=outs,
            out_specs=out_specs if out_specs is not None else jax.tree.map(lambda _: vmem, outs),
            scratch_shapes=scratch,
            input_output_aliases=aliases,
            compiler_params=pltpu.CompilerParams(vmem_limit_bytes=32 * MIB),
            cost_estimate=pl.CostEstimate(flops=flops, bytes_accessed=nbytes, transcendentals=0),
        )

    def pairs(target_of):
        found = [(source, target_of(source) % count) for source in range(count)]
        assert sorted(target for _, target in found) == list(range(count))
        return found

    def swapped(array):
        return lax.ppermute(array, "head", [(0, 1), (1, 0)])

    kv_shape = shape((half, 2 * keys.shape[1]), BF16)
    table_shape = shape((number, HEAD_SIZE), F32)
    rows_shape, state = shape((half, width), BF16), shape((half, width), F32)
    heads = width // HEAD_SIZE
    moved = group - 1
    cut = heads - moved
    some_shape = shape((half, cut * HEAD_SIZE), BF16)
    some_state = shape((half, cut * HEAD_SIZE), F32)
    last_shape = shape((half, moved * HEAD_SIZE), BF16)
    near, onward, k_rot, v, q, p, cosine, sinus = call(
        functools.partial(keys_kernel, count),
        "rotate_keys",
        [hbm] * 5,
        [kv_shape, kv_shape]
        + [shape(keys.shape, BF16)] * 2
        + [shape(queries.shape, BF16), shape((1, number), jnp.int32), table_shape, table_shape],
        4 * MIB,
        4 * MIB,
        scratch=[pltpu.VMEM(keys.shape, BF16), pltpu.VMEM((1, HEAD_SIZE), F32), dma((5,))],
    )(*(in_hbm(array) for array in (keys, values, queries, position_row, frequency)))
    near_pairs = pairs(lambda r: r + 3 if r % 2 else r + 1)
    near_got = lax.ppermute(near, "ctx", near_pairs)
    early = call(pack_kernel, "pack_early", [vmem] * 5, shape((half, (moved + 2) * HEAD_SIZE), BF16), MIB, MIB)(
        q, k_rot, v, cosine, sinus
    )
    early, q = lax.optimization_barrier((early, q))
    early_got = swapped(early)
    own, rot, acc, top, total = call(
        functools.partial(own_kernel, group),
        "own_tiles",
        [vmem] * 6,
        [some_shape, some_shape, some_state, some_state, some_state],
        256 * MIB,
        4 * MIB,
    )(q, k_rot, v, p, cosine, sinus)
    onward, rot = lax.optimization_barrier((onward, rot))
    next_got = lax.ppermute(onward, "ctx", pairs(lambda r: r + 2))
    first = call(
        functools.partial(first_kernel, count, group),
        "first_rows",
        [vmem] * 7,
        some_shape,
        256 * MIB,
        4 * MIB,
    )(own, rot, near_got, p, acc, top, total)
    first_got = swapped(first)
    q, first = lax.optimization_barrier((q, first))
    rot, *state_now, w = call(
        functools.partial(second_kernel, count, group),
        "second_rows",
        [vmem] * 7 + [hbm],
        [rows_shape, state, state, state, shape(out_weight.shape, BF16)],
        1024 * MIB,
        12 * MIB,
        scratch=[dma(())],
    )(q, k_rot, v, p, cosine, sinus, near_got, in_hbm(out_weight))
    rot, next_got, early_got = lax.optimization_barrier((rot, next_got, early_got))
    last_got = lax.ppermute(next_got, "ctx", pairs(lambda r: r + 1 - 2 * (r % 2)))
    state_now = call(
        functools.partial(next_kernel, count, group),
        "next_tile",
        [vmem] * 6,
        [state, state, state],
        512 * MIB,
        4 * MIB,
        aliases={3: 0, 4: 1, 5: 2},
    )(rot, next_got, p, *state_now)
    parts = range(heads // 2), range(heads // 2, heads - 1), range(heads - 1, heads)
    seconds, seconds_got = [], []
    for part in parts:
        second = call(
            functools.partial(third_kernel, count, group, part),
            "last_tile",
            [vmem] * 6,
            shape((half, len(part) * HEAD_SIZE), BF16),
            256 * MIB,
            4 * MIB,
        )(rot, last_got, p, *state_now)
        if len(seconds) < 2:
            seconds_got.append(swapped(second))
        if len(seconds) == 0:
            rot, second, first_got, early_got = lax.optimization_barrier((rot, second, first_got, early_got))
            other_near = lax.ppermute(early_got[:, moved * HEAD_SIZE :], "ctx", near_pairs)
        rot, second, early = lax.optimization_barrier((rot, second, early))
        seconds.append(second)
    attend_early = call(
        functools.partial(early_kernel, count), "early_rows", [vmem] * 3, last_shape, 256 * MIB, 4 * MIB
    )
    last = attend_early(early, near_got, p)
    sum_shape = shape((half, columns), F32)
    first_sum, partial_sum = call(
        project_kernel, "project_own", [vmem] * 6, [sum_shape, sum_shape], 2048 * MIB, 8 * MIB
    )(first, last, *seconds, w)
    early_got, partial_sum, first_sum, second = lax.optimization_barrier((early_got, partial_sum, first_sum, seconds[-1]))
    seconds_got.append(swapped(second))
    got_last = attend_early(early_got, other_near, p)
    begun = call(
        first_out_kernel,
        "project_first",
        [vmem] * 4,
        shape((number, columns), BF16),
        1024 * MIB,
        8 * MIB,
        out_specs=hbm,
        scratch=[pltpu.VMEM((half, columns), BF16), dma((tiles,))],
    )(first_got, got_last, first_sum, w)
    begun, partial_sum = lax.optimization_barrier((begun, partial_sum))
    for part, got in zip(parts[:-1], seconds_got):
        partial_sum = call(
            functools.partial(add_kernel, part[0] * HEAD_SIZE),
            "project_second",
            [vmem] * 3,
            sum_shape,
            512 * MIB,
            4 * MIB,
        )(got, partial_sum, w)
    return call(
        functools.partial(last_kernel, parts[-1][0] * HEAD_SIZE),
        "project_last",
        [vmem] * 3 + [hbm],
        shape((number, columns), BF16),
        512 * MIB,
        4 * MIB,
        out_specs=hbm,
        scratch=[pltpu.VMEM((half, columns), BF16), dma((columns // LAST_TILE,))],
        aliases={3: 0},
    )(seconds_got[-1], partial_sum, w, begun)


def solution(mesh):
    in_specs = (P("ctx", "head"), P("ctx", "head"), P("ctx", "head"), P("ctx"), P(None, "head"))
    out_specs = P("ctx", "head")
    return jax.shard_map(shards, mesh=mesh, in_specs=in_specs, out_specs=out_specs, check_vma=False)
```

```python
import functools
import math

import jax
import jax.numpy as jnp
import numpy as np
from jax import lax
from jax.experimental import pallas as pl
from jax.experimental.pallas import tpu as pltpu
from jax.sharding import PartitionSpec as P

HEAD_SIZE = 128
LOWEST = -1e30
FAR = 1 << 16
MIB = 1 << 20
SCORE_SCALE = math.log2(math.e) / math.sqrt(HEAD_SIZE)
BF16, F32 = jnp.bfloat16, jnp.float32


def distance(rank, step, count):
    return jnp.where(rank >= step, step, count - step)


def waits_for_keys(rank):
    return (rank == 1) | (rank == 2)


def first_begin(rank, half):
    return pl.multiple_of(jnp.where(rank < 2, 0, half), half)


def half_positions(p_ref, rank, first):
    half = p_ref.shape[1] // 2
    early = (rank < 2) if first else (rank >= 2)
    return jnp.where(early, p_ref[:, :half], p_ref[:, half:])


def column(row, width):
    return jnp.broadcast_to(row, (width, row.shape[1])).T


def tile_biases(position_row, kinds):
    number = position_row.shape[1]
    position = column(position_row, number)
    query = lax.broadcasted_iota(jnp.int32, (number, number), 0)
    key = lax.broadcasted_iota(jnp.int32, (number, number), 1)
    ahead = key - query
    reach = ahead + position
    found = []
    for pieces, diagonal in kinds:
        allowed = reach >= pieces * number
        if diagonal:
            allowed = allowed & (ahead <= 0)
        found.append(jnp.where(allowed, 0.0, LOWEST).astype(F32))
    return found


def sine_cosine(angle):
    turns = jnp.floor(angle * (2.0 / math.pi) + 0.5)
    rest = ((angle - turns * 1.5703125) - turns * 4.837512969970703e-4) - turns * 7.549789954891888e-8
    square = rest * rest
    sine = ((-1.9515295891e-4 * square + 8.3321608736e-3) * square - 1.6666654611e-1) * square * rest + rest
    cosine = (
        ((2.443315711809948e-5 * square - 1.388731625493765e-3) * square + 4.166664568298827e-2) * square * square
        - 0.5 * square
        + 1.0
    )
    quarter = turns.astype(jnp.int32)
    swap = (quarter & 1) == 1
    out_sine = jnp.where(swap, cosine, sine)
    out_cosine = jnp.where(swap, sine, cosine)
    out_sine = jnp.where((quarter & 2) == 2, -out_sine, out_sine)
    out_cosine = jnp.where(((quarter + 1) & 2) == 2, -out_cosine, out_cosine)
    return out_sine, out_cosine


def turned(block, cosine, sinus):
    wide = block.astype(F32)
    return (wide * cosine + pltpu.roll(wide, HEAD_SIZE // 2, 1) * sinus).astype(BF16)


def scores_of(query, key, bias):
    raw = lax.dot_general(query, key, (((1,), (1,)), ((), ())), preferred_element_type=F32)
    return raw * SCORE_SCALE + bias


def weighted(weights, value):
    return jnp.dot(weights.astype(BF16), value, preferred_element_type=F32)


def spread(entries):
    return jnp.broadcast_to(entries, (entries.shape[0], HEAD_SIZE))


def with_ones(value):
    return jnp.concatenate([value, jnp.ones_like(value)], axis=1)


def head_slices(head, group, width):
    at = slice(head * HEAD_SIZE, (head + 1) * HEAD_SIZE)
    low = head // group * HEAD_SIZE
    return at, slice(low, low + HEAD_SIZE), slice(width + low, width + low + HEAD_SIZE)


def begin_state(query, keys, values, biases):
    scores = [scores_of(query, key, bias) for key, bias in zip(keys, biases)]
    top = jnp.max(functools.reduce(jnp.maximum, scores), axis=1, keepdims=True)
    weights = [jnp.exp2(score - top) for score in scores]
    both = functools.reduce(jnp.add, [weighted(w, value) for w, value in zip(weights, values)])
    return both[:, :HEAD_SIZE], spread(top), both[:, HEAD_SIZE:]


def added_tile(summed, top, total, query, key, value, bias):
    score = scores_of(query, key, bias)
    updated = jnp.maximum(top, spread(jnp.max(score, axis=1, keepdims=True)))
    weights = jnp.exp2(score - jnp.concatenate([updated] * (score.shape[1] // HEAD_SIZE), axis=1))
    factor = jnp.exp2(top - updated)
    both = weighted(weights, value)
    return summed * factor + both[:, :HEAD_SIZE], updated, total * factor + both[:, HEAD_SIZE:]


def finished(state):
    summed, _, total = state
    return (summed * (1.0 / total)).astype(BF16)


def keys_kernel(
    count, k_hbm, v_hbm, q_hbm, p_hbm, f_hbm, near_ref, next_ref, rot_ref, v_ref, q_ref, p_ref, cos_ref, sin_ref,
    k_ref, f_ref, sems,
):
    pairs = ((p_hbm, p_ref), (f_hbm, f_ref), (k_hbm, k_ref), (v_hbm, v_ref), (q_hbm, q_ref))
    copies = [pltpu.make_async_copy(source, target, sems.at[i]) for i, (source, target) in enumerate(pairs)]
    for copy in copies:
        copy.start()
    rank = lax.axis_index("ctx")
    half = k_ref.shape[0] // 2
    width = k_ref.shape[1]
    copies[0].wait()
    copies[1].wait()
    position = p_ref[...].astype(F32)
    early = column(position[:, :half], HEAD_SIZE)
    late = column(position[:, half:], HEAD_SIZE)
    lane = lax.broadcasted_iota(jnp.int32, (half, HEAD_SIZE), 1)
    front = lane < HEAD_SIZE // 2
    sine, cosine = sine_cosine(jnp.where(front, early, late) * f_ref[...])
    sine_other = pltpu.roll(sine, HEAD_SIZE // 2, 1)
    cosine_other = pltpu.roll(cosine, HEAD_SIZE // 2, 1)
    cos_ref[:half] = jnp.where(front, cosine, cosine_other)
    cos_ref[half:] = jnp.where(front, cosine_other, cosine)
    sin_ref[:half] = jnp.where(front, -sine, sine_other)
    sin_ref[half:] = jnp.where(front, -sine_other, sine)
    copies[2].wait()
    for head in range(width // HEAD_SIZE):
        at = slice(head * HEAD_SIZE, (head + 1) * HEAD_SIZE)
        rot_ref[:, at] = turned(k_ref[:, at], cos_ref[...], sin_ref[...])
    copies[3].wait()
    wrap = (rank % 2 == 1) & (rank + 3 >= count)
    rows = pl.ds(pl.multiple_of(jnp.where(wrap, half, 0), half), half)
    near_ref[:, :width] = rot_ref[rows, :]
    near_ref[:, width:] = v_ref[rows, :]
    rows = pl.ds(pl.multiple_of(jnp.where(rank + 2 >= count, half, 0), half), half)
    next_ref[:, :width] = rot_ref[rows, :]
    next_ref[:, width:] = v_ref[rows, :]
    copies[4].wait()


def pack_kernel(q_ref, k_ref, v_ref, cos_ref, sin_ref, out_ref):
    rank = lax.axis_index("ctx")
    half, width = out_ref.shape[0], k_ref.shape[1]
    rows = pl.ds(first_begin(rank, half), half)
    begin, late = out_ref.shape[1] - 2 * HEAD_SIZE, slice(width - HEAD_SIZE, width)
    out_ref[:, begin : begin + HEAD_SIZE] = k_ref[rows, late]
    out_ref[:, begin + HEAD_SIZE :] = v_ref[rows, late]
    low = q_ref.shape[1] - begin
    for head in range(begin // HEAD_SIZE):
        at = slice(head * HEAD_SIZE, (head + 1) * HEAD_SIZE)
        source = slice(low + head * HEAD_SIZE, low + (head + 1) * HEAD_SIZE)
        out_ref[:, at] = turned(q_ref[rows, source], cos_ref[rows, :], sin_ref[rows, :])


def own_kernel(group, q_ref, k_ref, v_ref, p_ref, cos_ref, sin_ref, out_ref, rot_ref, acc_ref, top_ref, sum_ref):
    rank = lax.axis_index("ctx")
    half = q_ref.shape[0] // 2
    rows = pl.ds(first_begin(rank, half), half)
    biases = tile_biases(half_positions(p_ref, rank, True), [(0, True)])
    for head in range(rot_ref.shape[1] // HEAD_SIZE):
        at, shared, _ = head_slices(head, group, 0)
        query = turned(q_ref[rows, at], cos_ref[rows, :], sin_ref[rows, :])
        rot_ref[:, at] = query
        if head % group == 0:
            key = k_ref[rows, shared]
            value = with_ones(v_ref[rows, shared])
        for low, high in ((0, half // 2), (half // 2, half)):
            part = slice(low, high)
            summed, top, total = begin_state(query[part], [key[:high]], [value[:high]], [biases[0][part, :high]])
            acc_ref[part, at] = summed
            top_ref[part, at] = top
            sum_ref[part, at] = total
            out_ref[part, at] = (summed * (1.0 / total)).astype(BF16)


def first_kernel(count, group, own_ref, rot_ref, kv_ref, p_ref, acc_ref, top_ref, sum_ref, out_ref):
    rank = lax.axis_index("ctx")
    width = kv_ref.shape[1] // 2
    depth = rot_ref.shape[1]
    step = jnp.where(rank % 2 == 1, 1, 3)
    used = waits_for_keys(rank)
    @pl.when(used)
    def _():
        biases = tile_biases(half_positions(p_ref, rank, True), [(distance(rank, step, count), False)])
        for head in range(depth // HEAD_SIZE):
            at, key_at, value_at = head_slices(head, group, width)
            state = acc_ref[:, at], top_ref[:, at], sum_ref[:, at]
            if head % group == 0:
                value = with_ones(kv_ref[:, value_at])
            out_ref[:, at] = finished(added_tile(*state, rot_ref[:, at], kv_ref[:, key_at], value, *biases))

    @pl.when(jnp.logical_not(used))
    def _():
        out_ref[...] = own_ref[...]


def early_kernel(count, early_ref, near_ref, p_ref, out_ref):
    rank = lax.axis_index("ctx")
    depth = out_ref.shape[1]
    width = near_ref.shape[1] // 2
    step = jnp.where(rank % 2 == 1, 1, 3)
    reach = jnp.where(waits_for_keys(rank), distance(rank, step, count), FAR)
    biases = tile_biases(half_positions(p_ref, rank, True), [(0, True), (reach, False)])
    keys = [early_ref[:, depth : depth + HEAD_SIZE], near_ref[:, width - HEAD_SIZE : width]]
    values = [with_ones(early_ref[:, depth + HEAD_SIZE :]), with_ones(near_ref[:, 2 * width - HEAD_SIZE :])]
    for head in range(depth // HEAD_SIZE):
        at = slice(head * HEAD_SIZE, (head + 1) * HEAD_SIZE)
        out_ref[:, at] = finished(begin_state(early_ref[:, at], keys, values, biases))


def second_kernel(
    count, group, q_ref, k_ref, v_ref, p_ref, cos_ref, sin_ref, kv_ref, w_hbm, rot_ref, acc_ref, top_ref, sum_ref, w_ref, sem
):
    copy = pltpu.make_async_copy(w_hbm, w_ref, sem)
    copy.start()
    rank = lax.axis_index("ctx")
    half = q_ref.shape[0] // 2
    width = k_ref.shape[1]
    rows = pl.ds(pl.multiple_of(half - first_begin(rank, half), half), half)
    step = jnp.where(rank % 2 == 1, 1, 3)
    reach = jnp.where(waits_for_keys(rank), FAR, distance(rank, step, count))
    biases = tile_biases(half_positions(p_ref, rank, False), [(0, True), (reach, False)])
    for head in range(q_ref.shape[1] // HEAD_SIZE):
        at, key_at, value_at = head_slices(head, group, width)
        query = turned(q_ref[rows, at], cos_ref[rows, :], sin_ref[rows, :])
        rot_ref[:, at] = query
        keys = [k_ref[rows, key_at], kv_ref[:, key_at]]
        if head % group == 0:
            values = [with_ones(v_ref[rows, key_at]), with_ones(kv_ref[:, value_at])]
        acc_ref[:, at], top_ref[:, at], sum_ref[:, at] = begin_state(query, keys, values, biases)
    copy.wait()


def next_kernel(count, group, rot_ref, kv_ref, p_ref, acc_ref, top_ref, sum_ref, *outs):
    rank = lax.axis_index("ctx")
    width = kv_ref.shape[1] // 2
    biases = tile_biases(half_positions(p_ref, rank, False), [(distance(rank, 2, count), False)])
    for head in range(rot_ref.shape[1] // HEAD_SIZE):
        at, key_at, value_at = head_slices(head, group, width)
        state = acc_ref[:, at], top_ref[:, at], sum_ref[:, at]
        if head % group == 0:
            value = with_ones(kv_ref[:, value_at])
        state = added_tile(*state, rot_ref[:, at], kv_ref[:, key_at], value, *biases)
        for out_ref, entries in zip(outs, state):
            out_ref[:, at] = entries


def third_kernel(count, group, heads, rot_ref, kv_ref, p_ref, acc_ref, top_ref, sum_ref, out_ref):
    rank = lax.axis_index("ctx")
    width = kv_ref.shape[1] // 2
    step = jnp.where(rank % 2 == 1, 3, 1)
    biases = tile_biases(half_positions(p_ref, rank, False), [(distance(rank, step, count), False)])
    for number, head in enumerate(heads):
        at, key_at, value_at = head_slices(head, group, width)
        state = acc_ref[:, at], top_ref[:, at], sum_ref[:, at]
        if number == 0 or head % group == 0:
            value = with_ones(kv_ref[:, value_at])
        state = added_tile(*state, rot_ref[:, at], kv_ref[:, key_at], value, *biases)
        out_ref[:, number * HEAD_SIZE : (number + 1) * HEAD_SIZE] = finished(state)


def dot(left, right):
    return jnp.dot(left, right, preferred_element_type=F32)


TILE = 512
LAST_TILE = 256


def other_rows(w_ref, begin, end):
    depth = w_ref.shape[0] // 2
    base = (1 - lax.axis_index("head")) * depth
    return pl.ds(pl.multiple_of(base + begin, HEAD_SIZE), end - begin)


def project_kernel(first_ref, last_ref, second0_ref, second1_ref, w_ref, sum_ref, part_ref):
    half, depth = first_ref.shape[0], w_ref.shape[0] // 2
    mine = pl.ds(pl.multiple_of(lax.axis_index("head") * depth, depth), depth)
    first = jnp.concatenate([first_ref[...], last_ref[...]], axis=1)
    second = jnp.concatenate([second0_ref[...], second1_ref[...]], axis=1)
    stacked = jnp.concatenate([first, second], axis=0)
    for tile in range(w_ref.shape[1] // TILE):
        at = slice(tile * TILE, (tile + 1) * TILE)
        both = dot(stacked, w_ref[mine, at])
        sum_ref[:, at] = both[:half]
        part_ref[:, at] = both[half:]


def first_out_kernel(got_ref, got_last_ref, sum_ref, w_ref, out_hbm, held_ref, sems):
    rank = lax.axis_index("ctx")
    half, depth = got_ref.shape[0], w_ref.shape[0] // 2
    rows = pl.ds(first_begin(rank, half), half)
    other = other_rows(w_ref, 0, depth)
    got = jnp.concatenate([got_ref[...], got_last_ref[...]], axis=1)
    copies = []
    for tile in range(w_ref.shape[1] // TILE):
        at = slice(tile * TILE, (tile + 1) * TILE)
        held_ref[:, at] = (sum_ref[:, at] + dot(got, w_ref[other, at])).astype(BF16)
        copies.append(pltpu.make_async_copy(held_ref.at[:, at], out_hbm.at[rows, at], sems.at[tile]))
        copies[-1].start()
    for copy in copies:
        copy.wait()


def add_kernel(begin, got_ref, part_ref, w_ref, out_ref):
    rows = other_rows(w_ref, begin, begin + got_ref.shape[1])
    for start in range(0, w_ref.shape[1], TILE):
        at = slice(start, start + TILE)
        out_ref[:, at] = part_ref[:, at] + dot(got_ref[...], w_ref[rows, at])


def last_kernel(begin, got_ref, part_ref, w_ref, begun_hbm, out_hbm, held_ref, sems):
    del begun_hbm
    rank = lax.axis_index("ctx")
    half, depth = got_ref.shape
    out_rows = pl.ds(pl.multiple_of(half - first_begin(rank, half), half), half)
    rows = other_rows(w_ref, begin, begin + depth)
    copies = []
    for tile in range(w_ref.shape[1] // LAST_TILE):
        at = slice(tile * LAST_TILE, (tile + 1) * LAST_TILE)
        added = dot(got_ref[...], w_ref[rows, at])
        held_ref[:, at] = (part_ref[:, at] + added).astype(BF16)
        copies.append(pltpu.make_async_copy(held_ref.at[:, at], out_hbm.at[out_rows, at], sems.at[tile]))
        copies[-1].start()
    for copy in copies:
        copy.wait()


def shards(queries, keys, values, positions, out_weight):
    number, width = queries.shape
    half = number // 2
    count = lax.axis_size("ctx")
    group = width // keys.shape[1]
    columns = out_weight.shape[1]
    tiles = columns // TILE
    in_hbm = lambda array: pltpu.with_memory_space_constraint(array, pltpu.HBM)
    position_row = positions.reshape(1, number)
    table = np.power(500000.0, -2.0 * np.arange(HEAD_SIZE // 2) / HEAD_SIZE).astype(np.float32)
    frequency = jnp.asarray(np.concatenate([table, table])[None, :])
    shape = jax.ShapeDtypeStruct
    vmem = pl.BlockSpec(memory_space=pltpu.VMEM)
    hbm = pl.BlockSpec(memory_space=pltpu.HBM)
    dma = pltpu.SemaphoreType.DMA

    def call(body, name, ins, outs, flops, nbytes, out_specs=None, scratch=(), aliases={}):
        return pl.pallas_call(
            body,
            name=name,
            in_specs=ins,
            out_shape=outs,
            out_specs=out_specs if out_specs is not None else jax.tree.map(lambda _: vmem, outs),
            scratch_shapes=scratch,
            input_output_aliases=aliases,
            compiler_params=pltpu.CompilerParams(vmem_limit_bytes=32 * MIB),
            cost_estimate=pl.CostEstimate(flops=flops, bytes_accessed=nbytes, transcendentals=0),
        )

    def pairs(target_of):
        found = [(source, target_of(source) % count) for source in range(count)]
        assert sorted(target for _, target in found) == list(range(count))
        return found

    def swapped(array):
        return lax.ppermute(array, "head", [(0, 1), (1, 0)])

    kv_shape = shape((half, 2 * keys.shape[1]), BF16)
    table_shape = shape((number, HEAD_SIZE), F32)
    rows_shape, state = shape((half, width), BF16), shape((half, width), F32)
    heads = width // HEAD_SIZE
    moved = group - 1
    cut = heads - moved
    some_shape = shape((half, cut * HEAD_SIZE), BF16)
    some_state = shape((half, cut * HEAD_SIZE), F32)
    last_shape = shape((half, moved * HEAD_SIZE), BF16)
    near, onward, k_rot, v, q, p, cosine, sinus = call(
        functools.partial(keys_kernel, count),
        "rotate_keys",
        [hbm] * 5,
        [kv_shape, kv_shape]
        + [shape(keys.shape, BF16)] * 2
        + [shape(queries.shape, BF16), shape((1, number), jnp.int32), table_shape, table_shape],
        4 * MIB,
        4 * MIB,
        scratch=[pltpu.VMEM(keys.shape, BF16), pltpu.VMEM((1, HEAD_SIZE), F32), dma((5,))],
    )(*(in_hbm(array) for array in (keys, values, queries, position_row, frequency)))
    near_pairs = pairs(lambda r: r + 3 if r % 2 else r + 1)
    near_got = lax.ppermute(near, "ctx", near_pairs)
    early = call(pack_kernel, "pack_early", [vmem] * 5, shape((half, (moved + 2) * HEAD_SIZE), BF16), MIB, MIB)(
        q, k_rot, v, cosine, sinus
    )
    early, q = lax.optimization_barrier((early, q))
    early_got = swapped(early)
    own, rot, acc, top, total = call(
        functools.partial(own_kernel, group),
        "own_tiles",
        [vmem] * 6,
        [some_shape, some_shape, some_state, some_state, some_state],
        256 * MIB,
        4 * MIB,
    )(q, k_rot, v, p, cosine, sinus)
    onward, rot = lax.optimization_barrier((onward, rot))
    next_got = lax.ppermute(onward, "ctx", pairs(lambda r: r + 2))
    first = call(
        functools.partial(first_kernel, count, group),
        "first_rows",
        [vmem] * 7,
        some_shape,
        256 * MIB,
        4 * MIB,
    )(own, rot, near_got, p, acc, top, total)
    first_got = swapped(first)
    q, first = lax.optimization_barrier((q, first))
    rot, *state_now, w = call(
        functools.partial(second_kernel, count, group),
        "second_rows",
        [vmem] * 7 + [hbm],
        [rows_shape, state, state, state, shape(out_weight.shape, BF16)],
        1024 * MIB,
        12 * MIB,
        scratch=[dma(())],
    )(q, k_rot, v, p, cosine, sinus, near_got, in_hbm(out_weight))
    rot, next_got, early_got = lax.optimization_barrier((rot, next_got, early_got))
    last_got = lax.ppermute(next_got, "ctx", pairs(lambda r: r + 1 - 2 * (r % 2)))
    state_now = call(
        functools.partial(next_kernel, count, group),
        "next_tile",
        [vmem] * 6,
        [state, state, state],
        512 * MIB,
        4 * MIB,
        aliases={3: 0, 4: 1, 5: 2},
    )(rot, next_got, p, *state_now)
    parts = range(heads // 2), range(heads // 2, heads)
    seconds, seconds_got = [], []
    for part in parts:
        second = call(
            functools.partial(third_kernel, count, group, part),
            "last_tile",
            [vmem] * 6,
            shape((half, len(part) * HEAD_SIZE), BF16),
            256 * MIB,
            4 * MIB,
        )(rot, last_got, p, *state_now)
        seconds_got.append(swapped(second))
        if len(seconds) == 0:
            rot, second, first_got, early_got = lax.optimization_barrier((rot, second, first_got, early_got))
            other_near = lax.ppermute(early_got[:, moved * HEAD_SIZE :], "ctx", near_pairs)
        rot, second, early = lax.optimization_barrier((rot, second, early))
        seconds.append(second)
    attend_early = call(
        functools.partial(early_kernel, count), "early_rows", [vmem] * 3, last_shape, 256 * MIB, 4 * MIB
    )
    last = attend_early(early, near_got, p)
    sum_shape = shape((half, columns), F32)
    first_sum, partial_sum = call(
        project_kernel, "project_own", [vmem] * 5, [sum_shape, sum_shape], 2048 * MIB, 8 * MIB
    )(first, last, *seconds, w)
    partial_sum, first_sum = lax.optimization_barrier((partial_sum, first_sum))
    partial_sum = call(
        functools.partial(add_kernel, 0), "project_second", [vmem] * 3, sum_shape, 512 * MIB, 4 * MIB
    )(seconds_got[0], partial_sum, w)
    first_sum, partial_sum, early_got = lax.optimization_barrier((first_sum, partial_sum, early_got))
    got_last = attend_early(early_got, other_near, p)
    begun = call(
        first_out_kernel,
        "project_first",
        [vmem] * 4,
        shape((number, columns), BF16),
        1024 * MIB,
        8 * MIB,
        out_specs=hbm,
        scratch=[pltpu.VMEM((half, columns), BF16), dma((tiles,))],
    )(first_got, got_last, first_sum, w)
    return call(
        functools.partial(last_kernel, parts[-1][0] * HEAD_SIZE),
        "project_last",
        [vmem] * 3 + [hbm],
        shape((number, columns), BF16),
        512 * MIB,
        4 * MIB,
        out_specs=hbm,
        scratch=[pltpu.VMEM((half, columns), BF16), dma((columns // LAST_TILE,))],
        aliases={3: 0},
    )(seconds_got[-1], partial_sum, w, begun)


def solution(mesh):
    in_specs = (P("ctx", "head"), P("ctx", "head"), P("ctx", "head"), P("ctx"), P(None, "head"))
    out_specs = P("ctx", "head")
    return jax.shard_map(shards, mesh=mesh, in_specs=in_specs, out_specs=out_specs, check_vma=False)
```

```python
import functools
import math

import jax
import jax.numpy as jnp
import numpy as np
from jax import lax
from jax.experimental import pallas as pl
from jax.experimental.pallas import tpu as pltpu
from jax.sharding import PartitionSpec as P

HEAD_SIZE = 128
LOWEST = -1e30
FAR = 1 << 16
MIB = 1 << 20
SCORE_SCALE = math.log2(math.e) / math.sqrt(HEAD_SIZE)
BF16, F32 = jnp.bfloat16, jnp.float32


def distance(rank, step, count):
    return jnp.where(rank >= step, step, count - step)


def waits_for_keys(rank):
    return (rank == 1) | (rank == 2)


def first_begin(rank, half):
    return pl.multiple_of(jnp.where(rank < 2, 0, half), half)


def half_positions(p_ref, rank, first):
    half = p_ref.shape[1] // 2
    early = (rank < 2) if first else (rank >= 2)
    return jnp.where(early, p_ref[:, :half], p_ref[:, half:])


def column(row, width):
    return jnp.broadcast_to(row, (width, row.shape[1])).T


def tile_biases(position_row, kinds):
    number = position_row.shape[1]
    position = column(position_row, number)
    query = lax.broadcasted_iota(jnp.int32, (number, number), 0)
    key = lax.broadcasted_iota(jnp.int32, (number, number), 1)
    ahead = key - query
    reach = ahead + position
    found = []
    for pieces, diagonal in kinds:
        allowed = reach >= pieces * number
        if diagonal:
            allowed = allowed & (ahead <= 0)
        found.append(jnp.where(allowed, 0.0, LOWEST).astype(F32))
    return found


def sine_cosine(angle):
    turns = jnp.floor(angle * (2.0 / math.pi) + 0.5)
    rest = ((angle - turns * 1.5703125) - turns * 4.837512969970703e-4) - turns * 7.549789954891888e-8
    square = rest * rest
    sine = ((-1.9515295891e-4 * square + 8.3321608736e-3) * square - 1.6666654611e-1) * square * rest + rest
    cosine = (
        ((2.443315711809948e-5 * square - 1.388731625493765e-3) * square + 4.166664568298827e-2) * square * square
        - 0.5 * square
        + 1.0
    )
    quarter = turns.astype(jnp.int32)
    swap = (quarter & 1) == 1
    out_sine = jnp.where(swap, cosine, sine)
    out_cosine = jnp.where(swap, sine, cosine)
    out_sine = jnp.where((quarter & 2) == 2, -out_sine, out_sine)
    out_cosine = jnp.where(((quarter + 1) & 2) == 2, -out_cosine, out_cosine)
    return out_sine, out_cosine


def turned(block, cosine, sinus):
    wide = block.astype(F32)
    return (wide * cosine + pltpu.roll(wide, HEAD_SIZE // 2, 1) * sinus).astype(BF16)


def scores_of(query, key, bias):
    raw = lax.dot_general(query, key, (((1,), (1,)), ((), ())), preferred_element_type=F32)
    return raw * SCORE_SCALE + bias


def weighted(weights, value):
    return jnp.dot(weights.astype(BF16), value, preferred_element_type=F32)


def spread(entries):
    return jnp.broadcast_to(entries, (entries.shape[0], HEAD_SIZE))


def with_ones(value):
    return jnp.concatenate([value, jnp.ones_like(value)], axis=1)


def head_slices(head, group, width):
    at = slice(head * HEAD_SIZE, (head + 1) * HEAD_SIZE)
    low = head // group * HEAD_SIZE
    return at, slice(low, low + HEAD_SIZE), slice(width + low, width + low + HEAD_SIZE)


def begin_state(query, keys, values, biases):
    scores = [scores_of(query, key, bias) for key, bias in zip(keys, biases)]
    top = jnp.max(functools.reduce(jnp.maximum, scores), axis=1, keepdims=True)
    weights = [jnp.exp2(score - top) for score in scores]
    both = functools.reduce(jnp.add, [weighted(w, value) for w, value in zip(weights, values)])
    return both[:, :HEAD_SIZE], spread(top), both[:, HEAD_SIZE:]


def added_tile(summed, top, total, query, key, value, bias):
    score = scores_of(query, key, bias)
    updated = jnp.maximum(top, spread(jnp.max(score, axis=1, keepdims=True)))
    weights = jnp.exp2(score - jnp.concatenate([updated] * (score.shape[1] // HEAD_SIZE), axis=1))
    factor = jnp.exp2(top - updated)
    both = weighted(weights, value)
    return summed * factor + both[:, :HEAD_SIZE], updated, total * factor + both[:, HEAD_SIZE:]


def finished(state):
    summed, _, total = state
    return (summed * (1.0 / total)).astype(BF16)


def keys_kernel(
    count, k_hbm, v_hbm, q_hbm, p_hbm, f_hbm, near_ref, next_ref, rot_ref, v_ref, q_ref, p_ref, cos_ref, sin_ref,
    k_ref, f_ref, sems,
):
    pairs = ((p_hbm, p_ref), (f_hbm, f_ref), (k_hbm, k_ref), (v_hbm, v_ref), (q_hbm, q_ref))
    copies = [pltpu.make_async_copy(source, target, sems.at[i]) for i, (source, target) in enumerate(pairs)]
    for copy in copies:
        copy.start()
    rank = lax.axis_index("ctx")
    half = k_ref.shape[0] // 2
    width = k_ref.shape[1]
    copies[0].wait()
    copies[1].wait()
    position = p_ref[...].astype(F32)
    early = column(position[:, :half], HEAD_SIZE)
    late = column(position[:, half:], HEAD_SIZE)
    lane = lax.broadcasted_iota(jnp.int32, (half, HEAD_SIZE), 1)
    front = lane < HEAD_SIZE // 2
    sine, cosine = sine_cosine(jnp.where(front, early, late) * f_ref[...])
    sine_other = pltpu.roll(sine, HEAD_SIZE // 2, 1)
    cosine_other = pltpu.roll(cosine, HEAD_SIZE // 2, 1)
    cos_ref[:half] = jnp.where(front, cosine, cosine_other)
    cos_ref[half:] = jnp.where(front, cosine_other, cosine)
    sin_ref[:half] = jnp.where(front, -sine, sine_other)
    sin_ref[half:] = jnp.where(front, -sine_other, sine)
    copies[2].wait()
    for head in range(width // HEAD_SIZE):
        at = slice(head * HEAD_SIZE, (head + 1) * HEAD_SIZE)
        rot_ref[:, at] = turned(k_ref[:, at], cos_ref[...], sin_ref[...])
    copies[3].wait()
    wrap = (rank % 2 == 1) & (rank + 3 >= count)
    rows = pl.ds(pl.multiple_of(jnp.where(wrap, half, 0), half), half)
    near_ref[:, :width] = rot_ref[rows, :]
    near_ref[:, width:] = v_ref[rows, :]
    rows = pl.ds(pl.multiple_of(jnp.where(rank + 2 >= count, half, 0), half), half)
    next_ref[:, :width] = rot_ref[rows, :]
    next_ref[:, width:] = v_ref[rows, :]
    copies[4].wait()


def pack_kernel(q_ref, k_ref, v_ref, cos_ref, sin_ref, out_ref):
    rank = lax.axis_index("ctx")
    half, width = out_ref.shape[0], k_ref.shape[1]
    rows = pl.ds(first_begin(rank, half), half)
    begin, late = out_ref.shape[1] - 2 * HEAD_SIZE, slice(width - HEAD_SIZE, width)
    out_ref[:, begin : begin + HEAD_SIZE] = k_ref[rows, late]
    out_ref[:, begin + HEAD_SIZE :] = v_ref[rows, late]
    low = q_ref.shape[1] - begin
    for head in range(begin // HEAD_SIZE):
        at = slice(head * HEAD_SIZE, (head + 1) * HEAD_SIZE)
        source = slice(low + head * HEAD_SIZE, low + (head + 1) * HEAD_SIZE)
        out_ref[:, at] = turned(q_ref[rows, source], cos_ref[rows, :], sin_ref[rows, :])


def own_kernel(group, q_ref, k_ref, v_ref, p_ref, cos_ref, sin_ref, out_ref, rot_ref, acc_ref, top_ref, sum_ref):
    rank = lax.axis_index("ctx")
    half = q_ref.shape[0] // 2
    rows = pl.ds(first_begin(rank, half), half)
    biases = tile_biases(half_positions(p_ref, rank, True), [(0, True)])
    for head in range(rot_ref.shape[1] // HEAD_SIZE):
        at, shared, _ = head_slices(head, group, 0)
        query = turned(q_ref[rows, at], cos_ref[rows, :], sin_ref[rows, :])
        rot_ref[:, at] = query
        if head % group == 0:
            key = k_ref[rows, shared]
            value = with_ones(v_ref[rows, shared])
        for low, high in ((0, half // 2), (half // 2, half)):
            part = slice(low, high)
            summed, top, total = begin_state(query[part], [key[:high]], [value[:high]], [biases[0][part, :high]])
            acc_ref[part, at] = summed
            top_ref[part, at] = top
            sum_ref[part, at] = total
            out_ref[part, at] = (summed * (1.0 / total)).astype(BF16)


def first_kernel(count, group, own_ref, rot_ref, kv_ref, p_ref, acc_ref, top_ref, sum_ref, out_ref):
    rank = lax.axis_index("ctx")
    width = kv_ref.shape[1] // 2
    depth = rot_ref.shape[1]
    step = jnp.where(rank % 2 == 1, 1, 3)
    used = waits_for_keys(rank)
    @pl.when(used)
    def _():
        biases = tile_biases(half_positions(p_ref, rank, True), [(distance(rank, step, count), False)])
        for head in range(depth // HEAD_SIZE):
            at, key_at, value_at = head_slices(head, group, width)
            state = acc_ref[:, at], top_ref[:, at], sum_ref[:, at]
            if head % group == 0:
                value = with_ones(kv_ref[:, value_at])
            out_ref[:, at] = finished(added_tile(*state, rot_ref[:, at], kv_ref[:, key_at], value, *biases))

    @pl.when(jnp.logical_not(used))
    def _():
        out_ref[...] = own_ref[...]


def early_kernel(count, early_ref, near_ref, p_ref, out_ref):
    rank = lax.axis_index("ctx")
    depth = out_ref.shape[1]
    width = near_ref.shape[1] // 2
    step = jnp.where(rank % 2 == 1, 1, 3)
    reach = jnp.where(waits_for_keys(rank), distance(rank, step, count), FAR)
    biases = tile_biases(half_positions(p_ref, rank, True), [(0, True), (reach, False)])
    keys = [early_ref[:, depth : depth + HEAD_SIZE], near_ref[:, width - HEAD_SIZE : width]]
    values = [with_ones(early_ref[:, depth + HEAD_SIZE :]), with_ones(near_ref[:, 2 * width - HEAD_SIZE :])]
    for head in range(depth // HEAD_SIZE):
        at = slice(head * HEAD_SIZE, (head + 1) * HEAD_SIZE)
        out_ref[:, at] = finished(begin_state(early_ref[:, at], keys, values, biases))


def second_kernel(
    count, group, q_ref, k_ref, v_ref, p_ref, cos_ref, sin_ref, kv_ref, w_hbm, rot_ref, acc_ref, top_ref, sum_ref, w_ref, sem
):
    copy = pltpu.make_async_copy(w_hbm, w_ref, sem)
    copy.start()
    rank = lax.axis_index("ctx")
    half = q_ref.shape[0] // 2
    width = k_ref.shape[1]
    rows = pl.ds(pl.multiple_of(half - first_begin(rank, half), half), half)
    step = jnp.where(rank % 2 == 1, 1, 3)
    reach = jnp.where(waits_for_keys(rank), FAR, distance(rank, step, count))
    biases = tile_biases(half_positions(p_ref, rank, False), [(0, True), (reach, False)])
    for head in range(q_ref.shape[1] // HEAD_SIZE):
        at, key_at, value_at = head_slices(head, group, width)
        query = turned(q_ref[rows, at], cos_ref[rows, :], sin_ref[rows, :])
        rot_ref[:, at] = query
        keys = [k_ref[rows, key_at], kv_ref[:, key_at]]
        if head % group == 0:
            values = [with_ones(v_ref[rows, key_at]), with_ones(kv_ref[:, value_at])]
        acc_ref[:, at], top_ref[:, at], sum_ref[:, at] = begin_state(query, keys, values, biases)
    copy.wait()


def next_kernel(count, group, rot_ref, kv_ref, p_ref, acc_ref, top_ref, sum_ref, *outs):
    rank = lax.axis_index("ctx")
    width = kv_ref.shape[1] // 2
    biases = tile_biases(half_positions(p_ref, rank, False), [(distance(rank, 2, count), False)])
    for head in range(rot_ref.shape[1] // HEAD_SIZE):
        at, key_at, value_at = head_slices(head, group, width)
        state = acc_ref[:, at], top_ref[:, at], sum_ref[:, at]
        if head % group == 0:
            value = with_ones(kv_ref[:, value_at])
        state = added_tile(*state, rot_ref[:, at], kv_ref[:, key_at], value, *biases)
        for out_ref, entries in zip(outs, state):
            out_ref[:, at] = entries


def third_kernel(count, group, heads, rot_ref, kv_ref, p_ref, acc_ref, top_ref, sum_ref, out_ref):
    rank = lax.axis_index("ctx")
    width = kv_ref.shape[1] // 2
    step = jnp.where(rank % 2 == 1, 3, 1)
    biases = tile_biases(half_positions(p_ref, rank, False), [(distance(rank, step, count), False)])
    for number, head in enumerate(heads):
        at, key_at, value_at = head_slices(head, group, width)
        state = acc_ref[:, at], top_ref[:, at], sum_ref[:, at]
        if number == 0 or head % group == 0:
            value = with_ones(kv_ref[:, value_at])
        state = added_tile(*state, rot_ref[:, at], kv_ref[:, key_at], value, *biases)
        out_ref[:, number * HEAD_SIZE : (number + 1) * HEAD_SIZE] = finished(state)


def dot(left, right):
    return jnp.dot(left, right, preferred_element_type=F32)


TILE = 512
LAST_TILE = 256


def other_rows(w_ref, begin, end):
    depth = w_ref.shape[0] // 2
    base = (1 - lax.axis_index("head")) * depth
    return pl.ds(pl.multiple_of(base + begin, HEAD_SIZE), end - begin)


def project_kernel(first_ref, last_ref, second0_ref, second1_ref, w_ref, sum_ref, part_ref):
    half, depth = first_ref.shape[0], w_ref.shape[0] // 2
    mine = pl.ds(pl.multiple_of(lax.axis_index("head") * depth, depth), depth)
    first = jnp.concatenate([first_ref[...], last_ref[...]], axis=1)
    second = jnp.concatenate([second0_ref[...], second1_ref[...]], axis=1)
    stacked = jnp.concatenate([first, second], axis=0)
    for tile in range(w_ref.shape[1] // TILE):
        at = slice(tile * TILE, (tile + 1) * TILE)
        both = dot(stacked, w_ref[mine, at])
        sum_ref[:, at] = both[:half]
        part_ref[:, at] = both[half:]


def first_out_kernel(got_ref, got_last_ref, sum_ref, w_ref, out_hbm, held_ref, sems):
    rank = lax.axis_index("ctx")
    half, depth = got_ref.shape[0], w_ref.shape[0] // 2
    rows = pl.ds(first_begin(rank, half), half)
    other = other_rows(w_ref, 0, depth)
    got = jnp.concatenate([got_ref[...], got_last_ref[...]], axis=1)
    copies = []
    for tile in range(w_ref.shape[1] // TILE):
        at = slice(tile * TILE, (tile + 1) * TILE)
        held_ref[:, at] = (sum_ref[:, at] + dot(got, w_ref[other, at])).astype(BF16)
        copies.append(pltpu.make_async_copy(held_ref.at[:, at], out_hbm.at[rows, at], sems.at[tile]))
        copies[-1].start()
    for copy in copies:
        copy.wait()


def add_kernel(begin, got_ref, part_ref, w_ref, out_ref):
    rows = other_rows(w_ref, begin, begin + got_ref.shape[1])
    for start in range(0, w_ref.shape[1], TILE):
        at = slice(start, start + TILE)
        out_ref[:, at] = part_ref[:, at] + dot(got_ref[...], w_ref[rows, at])


def last_kernel(begin, got_ref, part_ref, w_ref, begun_hbm, out_hbm, held_ref, sems):
    del begun_hbm
    rank = lax.axis_index("ctx")
    half, depth = got_ref.shape
    out_rows = pl.ds(pl.multiple_of(half - first_begin(rank, half), half), half)
    rows = other_rows(w_ref, begin, begin + depth)
    copies = []
    for tile in range(w_ref.shape[1] // LAST_TILE):
        at = slice(tile * LAST_TILE, (tile + 1) * LAST_TILE)
        added = dot(got_ref[...], w_ref[rows, at])
        held_ref[:, at] = (part_ref[:, at] + added).astype(BF16)
        copies.append(pltpu.make_async_copy(held_ref.at[:, at], out_hbm.at[out_rows, at], sems.at[tile]))
        copies[-1].start()
    for copy in copies:
        copy.wait()


def shards(queries, keys, values, positions, out_weight):
    number, width = queries.shape
    half = number // 2
    count = lax.axis_size("ctx")
    group = width // keys.shape[1]
    columns = out_weight.shape[1]
    tiles = columns // TILE
    in_hbm = lambda array: pltpu.with_memory_space_constraint(array, pltpu.HBM)
    position_row = positions.reshape(1, number)
    table = np.power(500000.0, -2.0 * np.arange(HEAD_SIZE // 2) / HEAD_SIZE).astype(np.float32)
    frequency = jnp.asarray(np.concatenate([table, table])[None, :])
    shape = jax.ShapeDtypeStruct
    vmem = pl.BlockSpec(memory_space=pltpu.VMEM)
    hbm = pl.BlockSpec(memory_space=pltpu.HBM)
    dma = pltpu.SemaphoreType.DMA

    def call(body, name, ins, outs, flops, nbytes, out_specs=None, scratch=(), aliases={}):
        return pl.pallas_call(
            body,
            name=name,
            in_specs=ins,
            out_shape=outs,
            out_specs=out_specs if out_specs is not None else jax.tree.map(lambda _: vmem, outs),
            scratch_shapes=scratch,
            input_output_aliases=aliases,
            compiler_params=pltpu.CompilerParams(vmem_limit_bytes=32 * MIB),
            cost_estimate=pl.CostEstimate(flops=flops, bytes_accessed=nbytes, transcendentals=0),
        )

    def pairs(target_of):
        found = [(source, target_of(source) % count) for source in range(count)]
        assert sorted(target for _, target in found) == list(range(count))
        return found

    def swapped(array):
        return lax.ppermute(array, "head", [(0, 1), (1, 0)])

    kv_shape = shape((half, 2 * keys.shape[1]), BF16)
    table_shape = shape((number, HEAD_SIZE), F32)
    rows_shape, state = shape((half, width), BF16), shape((half, width), F32)
    heads = width // HEAD_SIZE
    moved = group - 1
    cut = heads - moved
    some_shape = shape((half, cut * HEAD_SIZE), BF16)
    some_state = shape((half, cut * HEAD_SIZE), F32)
    last_shape = shape((half, moved * HEAD_SIZE), BF16)
    near, onward, k_rot, v, q, p, cosine, sinus = call(
        functools.partial(keys_kernel, count),
        "rotate_keys",
        [hbm] * 5,
        [kv_shape, kv_shape]
        + [shape(keys.shape, BF16)] * 2
        + [shape(queries.shape, BF16), shape((1, number), jnp.int32), table_shape, table_shape],
        4 * MIB,
        4 * MIB,
        scratch=[pltpu.VMEM(keys.shape, BF16), pltpu.VMEM((1, HEAD_SIZE), F32), dma((5,))],
    )(*(in_hbm(array) for array in (keys, values, queries, position_row, frequency)))
    near_got = lax.ppermute(near, "ctx", pairs(lambda r: r + 3 if r % 2 else r + 1))
    early = call(pack_kernel, "pack_early", [vmem] * 5, shape((half, (moved + 2) * HEAD_SIZE), BF16), MIB, MIB)(
        q, k_rot, v, cosine, sinus
    )
    early, q = lax.optimization_barrier((early, q))
    early_got = swapped(early)
    own, rot, acc, top, total = call(
        functools.partial(own_kernel, group),
        "own_tiles",
        [vmem] * 6,
        [some_shape, some_shape, some_state, some_state, some_state],
        256 * MIB,
        4 * MIB,
    )(q, k_rot, v, p, cosine, sinus)
    onward, rot = lax.optimization_barrier((onward, rot))
    next_got = lax.ppermute(onward, "ctx", pairs(lambda r: r + 2))
    first = call(
        functools.partial(first_kernel, count, group),
        "first_rows",
        [vmem] * 7,
        some_shape,
        256 * MIB,
        4 * MIB,
    )(own, rot, near_got, p, acc, top, total)
    first_got = swapped(first)
    q, first = lax.optimization_barrier((q, first))
    rot, *state_now, w = call(
        functools.partial(second_kernel, count, group),
        "second_rows",
        [vmem] * 7 + [hbm],
        [rows_shape, state, state, state, shape(out_weight.shape, BF16)],
        1024 * MIB,
        12 * MIB,
        scratch=[dma(())],
    )(q, k_rot, v, p, cosine, sinus, near_got, in_hbm(out_weight))
    rot, next_got, early_got = lax.optimization_barrier((rot, next_got, early_got))
    last_got = lax.ppermute(next_got, "ctx", pairs(lambda r: r + 1 - 2 * (r % 2)))
    state_now = call(
        functools.partial(next_kernel, count, group),
        "next_tile",
        [vmem] * 6,
        [state, state, state],
        512 * MIB,
        4 * MIB,
        aliases={3: 0, 4: 1, 5: 2},
    )(rot, next_got, p, *state_now)
    parts = range(heads // 2), range(heads // 2, heads)
    seconds, seconds_got = [], []
    for part in parts:
        second = call(
            functools.partial(third_kernel, count, group, part),
            "last_tile",
            [vmem] * 6,
            shape((half, len(part) * HEAD_SIZE), BF16),
            256 * MIB,
            4 * MIB,
        )(rot, last_got, p, *state_now)
        seconds_got.append(swapped(second))
        if len(seconds) == 0:
            rot, second, first_got, own_near = lax.optimization_barrier((rot, second, first_got, near_got))
            low, high = keys.shape[1] - HEAD_SIZE, 2 * keys.shape[1] - HEAD_SIZE
            own_near = jnp.concatenate([own_near[:, low : low + HEAD_SIZE], own_near[:, high:]], axis=1)
            swaps = [(2 * block + side, 2 * block + 1 - side) for block in (1, 2) for side in (0, 1)]
            other_near = lax.ppermute(own_near, ("ctx", "head"), swaps)
        rot, second, early = lax.optimization_barrier((rot, second, early))
        seconds.append(second)
    attend_early = call(
        functools.partial(early_kernel, count), "early_rows", [vmem] * 3, last_shape, 256 * MIB, 4 * MIB
    )
    last = attend_early(early, near_got, p)
    sum_shape = shape((half, columns), F32)
    first_sum, partial_sum = call(
        project_kernel, "project_own", [vmem] * 5, [sum_shape, sum_shape], 2048 * MIB, 8 * MIB
    )(first, last, *seconds, w)
    partial_sum, first_sum = lax.optimization_barrier((partial_sum, first_sum))
    partial_sum = call(
        functools.partial(add_kernel, 0), "project_second", [vmem] * 3, sum_shape, 512 * MIB, 4 * MIB
    )(seconds_got[0], partial_sum, w)
    first_sum, partial_sum, early_got = lax.optimization_barrier((first_sum, partial_sum, early_got))
    got_last = attend_early(early_got, other_near, p)
    begun = call(
        first_out_kernel,
        "project_first",
        [vmem] * 4,
        shape((number, columns), BF16),
        1024 * MIB,
        8 * MIB,
        out_specs=hbm,
        scratch=[pltpu.VMEM((half, columns), BF16), dma((tiles,))],
    )(first_got, got_last, first_sum, w)
    return call(
        functools.partial(last_kernel, parts[-1][0] * HEAD_SIZE),
        "project_last",
        [vmem] * 3 + [hbm],
        shape((number, columns), BF16),
        512 * MIB,
        4 * MIB,
        out_specs=hbm,
        scratch=[pltpu.VMEM((half, columns), BF16), dma((columns // LAST_TILE,))],
        aliases={3: 0},
    )(seconds_got[-1], partial_sum, w, begun)


def solution(mesh):
    in_specs = (P("ctx", "head"), P("ctx", "head"), P("ctx", "head"), P("ctx"), P(None, "head"))
    out_specs = P("ctx", "head")
    return jax.shard_map(shards, mesh=mesh, in_specs=in_specs, out_specs=out_specs, check_vma=False)
```

```python
import functools
import math

import jax
import jax.numpy as jnp
import numpy as np
from jax import lax
from jax.experimental import pallas as pl
from jax.experimental.pallas import tpu as pltpu
from jax.sharding import PartitionSpec as P

HEAD_SIZE = 128
LOWEST = -1e30
FAR = 1 << 16
MIB = 1 << 20
SCORE_SCALE = math.log2(math.e) / math.sqrt(HEAD_SIZE)
BF16, F32 = jnp.bfloat16, jnp.float32


def distance(rank, step, count):
    return jnp.where(rank >= step, step, count - step)


def waits_for_keys(rank):
    return (rank == 1) | (rank == 2)


def first_begin(rank, half):
    return pl.multiple_of(jnp.where(rank < 2, 0, half), half)


def half_positions(p_ref, rank, first):
    half = p_ref.shape[1] // 2
    early = (rank < 2) if first else (rank >= 2)
    return jnp.where(early, p_ref[:, :half], p_ref[:, half:])


def column(row, width):
    return jnp.broadcast_to(row, (width, row.shape[1])).T


def tile_biases(position_row, kinds):
    number = position_row.shape[1]
    position = column(position_row, number)
    query = lax.broadcasted_iota(jnp.int32, (number, number), 0)
    key = lax.broadcasted_iota(jnp.int32, (number, number), 1)
    ahead = key - query
    reach = ahead + position
    found = []
    for pieces, diagonal in kinds:
        allowed = reach >= pieces * number
        if diagonal:
            allowed = allowed & (ahead <= 0)
        found.append(jnp.where(allowed, 0.0, LOWEST).astype(F32))
    return found


def sine_cosine(angle):
    turns = jnp.floor(angle * (2.0 / math.pi) + 0.5)
    rest = ((angle - turns * 1.5703125) - turns * 4.837512969970703e-4) - turns * 7.549789954891888e-8
    square = rest * rest
    sine = ((-1.9515295891e-4 * square + 8.3321608736e-3) * square - 1.6666654611e-1) * square * rest + rest
    cosine = (
        ((2.443315711809948e-5 * square - 1.388731625493765e-3) * square + 4.166664568298827e-2) * square * square
        - 0.5 * square
        + 1.0
    )
    quarter = turns.astype(jnp.int32)
    swap = (quarter & 1) == 1
    out_sine = jnp.where(swap, cosine, sine)
    out_cosine = jnp.where(swap, sine, cosine)
    out_sine = jnp.where((quarter & 2) == 2, -out_sine, out_sine)
    out_cosine = jnp.where(((quarter + 1) & 2) == 2, -out_cosine, out_cosine)
    return out_sine, out_cosine


def turned(block, cosine, sinus):
    wide = block.astype(F32)
    return (wide * cosine + pltpu.roll(wide, HEAD_SIZE // 2, 1) * sinus).astype(BF16)


def scores_of(query, key, bias):
    raw = lax.dot_general(query, key, (((1,), (1,)), ((), ())), preferred_element_type=F32)
    return raw * SCORE_SCALE + bias


def weighted(weights, value):
    return jnp.dot(weights.astype(BF16), value, preferred_element_type=F32)


def spread(entries):
    return jnp.broadcast_to(entries, (entries.shape[0], HEAD_SIZE))


def with_ones(value):
    return jnp.concatenate([value, jnp.ones_like(value)], axis=1)


def head_slices(head, group, width):
    at = slice(head * HEAD_SIZE, (head + 1) * HEAD_SIZE)
    low = head // group * HEAD_SIZE
    return at, slice(low, low + HEAD_SIZE), slice(width + low, width + low + HEAD_SIZE)


def begin_state(query, keys, values, biases):
    scores = [scores_of(query, key, bias) for key, bias in zip(keys, biases)]
    top = jnp.max(functools.reduce(jnp.maximum, scores), axis=1, keepdims=True)
    weights = [jnp.exp2(score - top) for score in scores]
    both = functools.reduce(jnp.add, [weighted(w, value) for w, value in zip(weights, values)])
    return both[:, :HEAD_SIZE], spread(top), both[:, HEAD_SIZE:]


def added_tile(summed, top, total, query, key, value, bias):
    score = scores_of(query, key, bias)
    updated = jnp.maximum(top, spread(jnp.max(score, axis=1, keepdims=True)))
    weights = jnp.exp2(score - jnp.concatenate([updated] * (score.shape[1] // HEAD_SIZE), axis=1))
    factor = jnp.exp2(top - updated)
    both = weighted(weights, value)
    return summed * factor + both[:, :HEAD_SIZE], updated, total * factor + both[:, HEAD_SIZE:]


def finished(state):
    summed, _, total = state
    return (summed * (1.0 / total)).astype(BF16)


def keys_kernel(
    count, k_hbm, v_hbm, q_hbm, p_hbm, f_hbm, near_ref, next_ref, rot_ref, v_ref, q_ref, p_ref, cos_ref, sin_ref,
    k_ref, f_ref, sems,
):
    pairs = ((p_hbm, p_ref), (f_hbm, f_ref), (k_hbm, k_ref), (v_hbm, v_ref), (q_hbm, q_ref))
    copies = [pltpu.make_async_copy(source, target, sems.at[i]) for i, (source, target) in enumerate(pairs)]
    for copy in copies:
        copy.start()
    rank = lax.axis_index("ctx")
    half = k_ref.shape[0] // 2
    width = k_ref.shape[1]
    copies[0].wait()
    copies[1].wait()
    position = p_ref[...].astype(F32)
    early = column(position[:, :half], HEAD_SIZE)
    late = column(position[:, half:], HEAD_SIZE)
    lane = lax.broadcasted_iota(jnp.int32, (half, HEAD_SIZE), 1)
    front = lane < HEAD_SIZE // 2
    sine, cosine = sine_cosine(jnp.where(front, early, late) * f_ref[...])
    sine_other = pltpu.roll(sine, HEAD_SIZE // 2, 1)
    cosine_other = pltpu.roll(cosine, HEAD_SIZE // 2, 1)
    cos_ref[:half] = jnp.where(front, cosine, cosine_other)
    cos_ref[half:] = jnp.where(front, cosine_other, cosine)
    sin_ref[:half] = jnp.where(front, -sine, sine_other)
    sin_ref[half:] = jnp.where(front, -sine_other, sine)
    copies[2].wait()
    for head in range(width // HEAD_SIZE):
        at = slice(head * HEAD_SIZE, (head + 1) * HEAD_SIZE)
        rot_ref[:, at] = turned(k_ref[:, at], cos_ref[...], sin_ref[...])
    copies[3].wait()
    wrap = (rank % 2 == 1) & (rank + 3 >= count)
    rows = pl.ds(pl.multiple_of(jnp.where(wrap, half, 0), half), half)
    near_ref[:, :width] = rot_ref[rows, :]
    near_ref[:, width:] = v_ref[rows, :]
    rows = pl.ds(pl.multiple_of(jnp.where(rank + 2 >= count, half, 0), half), half)
    next_ref[:, :width] = rot_ref[rows, :]
    next_ref[:, width:] = v_ref[rows, :]
    copies[4].wait()


def pack_kernel(q_ref, k_ref, v_ref, cos_ref, sin_ref, out_ref):
    rank = lax.axis_index("ctx")
    half, width = out_ref.shape[0], k_ref.shape[1]
    rows = pl.ds(first_begin(rank, half), half)
    begin, late = out_ref.shape[1] - 2 * HEAD_SIZE, slice(width - HEAD_SIZE, width)
    out_ref[:, begin : begin + HEAD_SIZE] = k_ref[rows, late]
    out_ref[:, begin + HEAD_SIZE :] = v_ref[rows, late]
    low = q_ref.shape[1] - begin
    for head in range(begin // HEAD_SIZE):
        at = slice(head * HEAD_SIZE, (head + 1) * HEAD_SIZE)
        source = slice(low + head * HEAD_SIZE, low + (head + 1) * HEAD_SIZE)
        out_ref[:, at] = turned(q_ref[rows, source], cos_ref[rows, :], sin_ref[rows, :])


def own_kernel(group, q_ref, k_ref, v_ref, p_ref, cos_ref, sin_ref, out_ref, rot_ref, acc_ref, top_ref, sum_ref):
    rank = lax.axis_index("ctx")
    half = q_ref.shape[0] // 2
    rows = pl.ds(first_begin(rank, half), half)
    biases = tile_biases(half_positions(p_ref, rank, True), [(0, True)])
    for head in range(rot_ref.shape[1] // HEAD_SIZE):
        at, shared, _ = head_slices(head, group, 0)
        query = turned(q_ref[rows, at], cos_ref[rows, :], sin_ref[rows, :])
        rot_ref[:, at] = query
        if head % group == 0:
            key = k_ref[rows, shared]
            value = with_ones(v_ref[rows, shared])
        for low, high in ((0, half // 2), (half // 2, half)):
            part = slice(low, high)
            summed, top, total = begin_state(query[part], [key[:high]], [value[:high]], [biases[0][part, :high]])
            acc_ref[part, at] = summed
            top_ref[part, at] = top
            sum_ref[part, at] = total
            out_ref[part, at] = (summed * (1.0 / total)).astype(BF16)


def first_kernel(count, group, own_ref, rot_ref, kv_ref, p_ref, acc_ref, top_ref, sum_ref, out_ref):
    rank = lax.axis_index("ctx")
    width = kv_ref.shape[1] // 2
    depth = rot_ref.shape[1]
    step = jnp.where(rank % 2 == 1, 1, 3)
    used = waits_for_keys(rank)
    @pl.when(used)
    def _():
        biases = tile_biases(half_positions(p_ref, rank, True), [(distance(rank, step, count), False)])
        for head in range(depth // HEAD_SIZE):
            at, key_at, value_at = head_slices(head, group, width)
            state = acc_ref[:, at], top_ref[:, at], sum_ref[:, at]
            if head % group == 0:
                value = with_ones(kv_ref[:, value_at])
            out_ref[:, at] = finished(added_tile(*state, rot_ref[:, at], kv_ref[:, key_at], value, *biases))

    @pl.when(jnp.logical_not(used))
    def _():
        out_ref[...] = own_ref[...]


def early_kernel(count, early_ref, near_ref, p_ref, out_ref):
    rank = lax.axis_index("ctx")
    depth = out_ref.shape[1]
    width = near_ref.shape[1] // 2
    step = jnp.where(rank % 2 == 1, 1, 3)
    reach = jnp.where(waits_for_keys(rank), distance(rank, step, count), FAR)
    biases = tile_biases(half_positions(p_ref, rank, True), [(0, True), (reach, False)])
    keys = [early_ref[:, depth : depth + HEAD_SIZE], near_ref[:, width - HEAD_SIZE : width]]
    values = [with_ones(early_ref[:, depth + HEAD_SIZE :]), with_ones(near_ref[:, 2 * width - HEAD_SIZE :])]
    for head in range(depth // HEAD_SIZE):
        at = slice(head * HEAD_SIZE, (head + 1) * HEAD_SIZE)
        out_ref[:, at] = finished(begin_state(early_ref[:, at], keys, values, biases))


def second_kernel(
    count, group, q_ref, k_ref, v_ref, p_ref, cos_ref, sin_ref, kv_ref, w_hbm, rot_ref, acc_ref, top_ref, sum_ref, w_ref, sem
):
    copy = pltpu.make_async_copy(w_hbm, w_ref, sem)
    copy.start()
    rank = lax.axis_index("ctx")
    half = q_ref.shape[0] // 2
    width = k_ref.shape[1]
    rows = pl.ds(pl.multiple_of(half - first_begin(rank, half), half), half)
    step = jnp.where(rank % 2 == 1, 1, 3)
    reach = jnp.where(waits_for_keys(rank), FAR, distance(rank, step, count))
    biases = tile_biases(half_positions(p_ref, rank, False), [(0, True), (reach, False)])
    for head in range(q_ref.shape[1] // HEAD_SIZE):
        at, key_at, value_at = head_slices(head, group, width)
        query = turned(q_ref[rows, at], cos_ref[rows, :], sin_ref[rows, :])
        rot_ref[:, at] = query
        keys = [k_ref[rows, key_at], kv_ref[:, key_at]]
        if head % group == 0:
            values = [with_ones(v_ref[rows, key_at]), with_ones(kv_ref[:, value_at])]
        acc_ref[:, at], top_ref[:, at], sum_ref[:, at] = begin_state(query, keys, values, biases)
    copy.wait()


def next_kernel(count, group, heads, rot_ref, kv_ref, p_ref, acc_ref, top_ref, sum_ref, *outs):
    rank = lax.axis_index("ctx")
    width = kv_ref.shape[1] // 2
    biases = tile_biases(half_positions(p_ref, rank, False), [(distance(rank, 2, count), False)])
    for number, head in enumerate(heads):
        at, key_at, value_at = head_slices(head, group, width)
        state = acc_ref[:, at], top_ref[:, at], sum_ref[:, at]
        if number == 0 or head % group == 0:
            value = with_ones(kv_ref[:, value_at])
        state = added_tile(*state, rot_ref[:, at], kv_ref[:, key_at], value, *biases)
        for out_ref, entries in zip(outs, state):
            out_ref[:, number * HEAD_SIZE : (number + 1) * HEAD_SIZE] = entries


def third_kernel(count, group, heads, base, rot_ref, kv_ref, p_ref, acc_ref, top_ref, sum_ref, out_ref):
    rank = lax.axis_index("ctx")
    width = kv_ref.shape[1] // 2
    step = jnp.where(rank % 2 == 1, 3, 1)
    biases = tile_biases(half_positions(p_ref, rank, False), [(distance(rank, step, count), False)])
    for number, head in enumerate(heads):
        at, key_at, value_at = head_slices(head, group, width)
        held = slice((head - base) * HEAD_SIZE, (head - base + 1) * HEAD_SIZE)
        state = acc_ref[:, held], top_ref[:, held], sum_ref[:, held]
        if number == 0 or head % group == 0:
            value = with_ones(kv_ref[:, value_at])
        state = added_tile(*state, rot_ref[:, at], kv_ref[:, key_at], value, *biases)
        out_ref[:, number * HEAD_SIZE : (number + 1) * HEAD_SIZE] = finished(state)


def dot(left, right):
    return jnp.dot(left, right, preferred_element_type=F32)


TILE = 512
LAST_TILE = 256


def other_rows(w_ref, begin, end):
    depth = w_ref.shape[0] // 2
    base = (1 - lax.axis_index("head")) * depth
    return pl.ds(pl.multiple_of(base + begin, HEAD_SIZE), end - begin)


def project_kernel(first_ref, last_ref, second0_ref, second1_ref, second2_ref, w_ref, sum_ref, part_ref):
    half, depth = first_ref.shape[0], w_ref.shape[0] // 2
    mine = pl.ds(pl.multiple_of(lax.axis_index("head") * depth, depth), depth)
    first = jnp.concatenate([first_ref[...], last_ref[...]], axis=1)
    second = jnp.concatenate([second0_ref[...], second1_ref[...], second2_ref[...]], axis=1)
    stacked = jnp.concatenate([first, second], axis=0)
    for tile in range(w_ref.shape[1] // TILE):
        at = slice(tile * TILE, (tile + 1) * TILE)
        both = dot(stacked, w_ref[mine, at])
        sum_ref[:, at] = both[:half]
        part_ref[:, at] = both[half:]


def first_out_kernel(got_ref, got_last_ref, sum_ref, w_ref, out_hbm, held_ref, sems):
    rank = lax.axis_index("ctx")
    half, depth = got_ref.shape[0], w_ref.shape[0] // 2
    rows = pl.ds(first_begin(rank, half), half)
    other = other_rows(w_ref, 0, depth)
    got = jnp.concatenate([got_ref[...], got_last_ref[...]], axis=1)
    copies = []
    for tile in range(w_ref.shape[1] // TILE):
        at = slice(tile * TILE, (tile + 1) * TILE)
        held_ref[:, at] = (sum_ref[:, at] + dot(got, w_ref[other, at])).astype(BF16)
        copies.append(pltpu.make_async_copy(held_ref.at[:, at], out_hbm.at[rows, at], sems.at[tile]))
        copies[-1].start()
    for copy in copies:
        copy.wait()


def add_kernel(begin, got_ref, part_ref, w_ref, out_ref):
    rows = other_rows(w_ref, begin, begin + got_ref.shape[1])
    for start in range(0, w_ref.shape[1], TILE):
        at = slice(start, start + TILE)
        out_ref[:, at] = part_ref[:, at] + dot(got_ref[...], w_ref[rows, at])


def last_kernel(begin, got_ref, part_ref, w_ref, begun_hbm, out_hbm, held_ref, sems):
    del begun_hbm
    rank = lax.axis_index("ctx")
    half, depth = got_ref.shape
    out_rows = pl.ds(pl.multiple_of(half - first_begin(rank, half), half), half)
    rows = other_rows(w_ref, begin, begin + depth)
    copies = []
    for tile in range(w_ref.shape[1] // LAST_TILE):
        at = slice(tile * LAST_TILE, (tile + 1) * LAST_TILE)
        added = dot(got_ref[...], w_ref[rows, at])
        held_ref[:, at] = (part_ref[:, at] + added).astype(BF16)
        copies.append(pltpu.make_async_copy(held_ref.at[:, at], out_hbm.at[out_rows, at], sems.at[tile]))
        copies[-1].start()
    for copy in copies:
        copy.wait()


def shards(queries, keys, values, positions, out_weight):
    number, width = queries.shape
    half = number // 2
    count = lax.axis_size("ctx")
    group = width // keys.shape[1]
    columns = out_weight.shape[1]
    tiles = columns // TILE
    in_hbm = lambda array: pltpu.with_memory_space_constraint(array, pltpu.HBM)
    position_row = positions.reshape(1, number)
    table = np.power(500000.0, -2.0 * np.arange(HEAD_SIZE // 2) / HEAD_SIZE).astype(np.float32)
    frequency = jnp.asarray(np.concatenate([table, table])[None, :])
    shape = jax.ShapeDtypeStruct
    vmem = pl.BlockSpec(memory_space=pltpu.VMEM)
    hbm = pl.BlockSpec(memory_space=pltpu.HBM)
    dma = pltpu.SemaphoreType.DMA

    def call(body, name, ins, outs, flops, nbytes, out_specs=None, scratch=(), aliases={}):
        return pl.pallas_call(
            body,
            name=name,
            in_specs=ins,
            out_shape=outs,
            out_specs=out_specs if out_specs is not None else jax.tree.map(lambda _: vmem, outs),
            scratch_shapes=scratch,
            input_output_aliases=aliases,
            compiler_params=pltpu.CompilerParams(vmem_limit_bytes=32 * MIB),
            cost_estimate=pl.CostEstimate(flops=flops, bytes_accessed=nbytes, transcendentals=0),
        )

    def pairs(target_of):
        found = [(source, target_of(source) % count) for source in range(count)]
        assert sorted(target for _, target in found) == list(range(count))
        return found

    def swapped(array):
        return lax.ppermute(array, "head", [(0, 1), (1, 0)])

    kv_shape = shape((half, 2 * keys.shape[1]), BF16)
    table_shape = shape((number, HEAD_SIZE), F32)
    rows_shape, state = shape((half, width), BF16), shape((half, width), F32)
    heads = width // HEAD_SIZE
    moved = group - 1
    cut = heads - moved
    some_shape = shape((half, cut * HEAD_SIZE), BF16)
    some_state = shape((half, cut * HEAD_SIZE), F32)
    last_shape = shape((half, moved * HEAD_SIZE), BF16)
    near, onward, k_rot, v, q, p, cosine, sinus = call(
        functools.partial(keys_kernel, count),
        "rotate_keys",
        [hbm] * 5,
        [kv_shape, kv_shape]
        + [shape(keys.shape, BF16)] * 2
        + [shape(queries.shape, BF16), shape((1, number), jnp.int32), table_shape, table_shape],
        4 * MIB,
        4 * MIB,
        scratch=[pltpu.VMEM(keys.shape, BF16), pltpu.VMEM((1, HEAD_SIZE), F32), dma((5,))],
    )(*(in_hbm(array) for array in (keys, values, queries, position_row, frequency)))
    near_pairs = pairs(lambda r: r + 3 if r % 2 else r + 1)
    near_got = lax.ppermute(near, "ctx", near_pairs)
    early = call(pack_kernel, "pack_early", [vmem] * 5, shape((half, (moved + 2) * HEAD_SIZE), BF16), MIB, MIB)(
        q, k_rot, v, cosine, sinus
    )
    early, q = lax.optimization_barrier((early, q))
    early_got = swapped(early)
    own, rot, acc, top, total = call(
        functools.partial(own_kernel, group),
        "own_tiles",
        [vmem] * 6,
        [some_shape, some_shape, some_state, some_state, some_state],
        256 * MIB,
        4 * MIB,
    )(q, k_rot, v, p, cosine, sinus)
    onward, rot = lax.optimization_barrier((onward, rot))
    next_got = lax.ppermute(onward, "ctx", pairs(lambda r: r + 2))
    first = call(
        functools.partial(first_kernel, count, group),
        "first_rows",
        [vmem] * 7,
        some_shape,
        256 * MIB,
        4 * MIB,
    )(own, rot, near_got, p, acc, top, total)
    first_got = swapped(first)
    q, first = lax.optimization_barrier((q, first))
    rot, *state_now, w = call(
        functools.partial(second_kernel, count, group),
        "second_rows",
        [vmem] * 7 + [hbm],
        [rows_shape, state, state, state, shape(out_weight.shape, BF16)],
        1024 * MIB,
        12 * MIB,
        scratch=[dma(())],
    )(q, k_rot, v, p, cosine, sinus, near_got, in_hbm(out_weight))
    rot, early_got = lax.optimization_barrier((rot, early_got))
    other_near = lax.ppermute(early_got[:, moved * HEAD_SIZE :], "ctx", near_pairs)
    rot, next_got = lax.optimization_barrier((rot, next_got))
    last_got = lax.ppermute(next_got, "ctx", pairs(lambda r: r + 1 - 2 * (r % 2)))
    def with_next_tile(part, rot):
        held = shape((half, len(part) * HEAD_SIZE), F32)
        return call(
            functools.partial(next_kernel, count, group, part), "next_tile", [vmem] * 6, [held] * 3, 512 * MIB, 4 * MIB
        )(rot, next_got, p, *state_now)

    parts = range(heads // 2), range(heads // 2, heads - 1), range(heads - 1, heads)
    seconds, seconds_got = [], []
    for part in parts:
        if len(seconds) < 2:
            base = part[0]
            held_state = with_next_tile(range(base, base + heads // 2), rot)
        second = call(
            functools.partial(third_kernel, count, group, part, base),
            "last_tile",
            [vmem] * 6,
            shape((half, len(part) * HEAD_SIZE), BF16),
            256 * MIB,
            4 * MIB,
        )(rot, last_got, p, *held_state)
        seconds_got.append(swapped(second))
        if len(seconds) == 0:
            rot, second, first_got = lax.optimization_barrier((rot, second, first_got))
        else:
            rot, second, other_near, early = lax.optimization_barrier((rot, second, other_near, early))
        seconds.append(second)
    attend_early = call(
        functools.partial(early_kernel, count), "early_rows", [vmem] * 3, last_shape, 256 * MIB, 4 * MIB
    )
    last = attend_early(early, near_got, p)
    sum_shape = shape((half, columns), F32)
    first_sum, partial_sum = call(
        project_kernel, "project_own", [vmem] * 6, [sum_shape, sum_shape], 2048 * MIB, 8 * MIB
    )(first, last, *seconds, w)
    early_got, partial_sum, first_sum = lax.optimization_barrier((early_got, partial_sum, first_sum))
    got_last = attend_early(early_got, other_near, p)
    begun = call(
        first_out_kernel,
        "project_first",
        [vmem] * 4,
        shape((number, columns), BF16),
        1024 * MIB,
        8 * MIB,
        out_specs=hbm,
        scratch=[pltpu.VMEM((half, columns), BF16), dma((tiles,))],
    )(first_got, got_last, first_sum, w)
    begun, partial_sum = lax.optimization_barrier((begun, partial_sum))
    for part, got in zip(parts[:-1], seconds_got):
        partial_sum = call(
            functools.partial(add_kernel, part[0] * HEAD_SIZE),
            "project_second",
            [vmem] * 3,
            sum_shape,
            512 * MIB,
            4 * MIB,
        )(got, partial_sum, w)
    return call(
        functools.partial(last_kernel, parts[-1][0] * HEAD_SIZE),
        "project_last",
        [vmem] * 3 + [hbm],
        shape((number, columns), BF16),
        512 * MIB,
        4 * MIB,
        out_specs=hbm,
        scratch=[pltpu.VMEM((half, columns), BF16), dma((columns // LAST_TILE,))],
        aliases={3: 0},
    )(seconds_got[-1], partial_sum, w, begun)


def solution(mesh):
    in_specs = (P("ctx", "head"), P("ctx", "head"), P("ctx", "head"), P("ctx"), P(None, "head"))
    out_specs = P("ctx", "head")
    return jax.shard_map(shards, mesh=mesh, in_specs=in_specs, out_specs=out_specs, check_vma=False)
```

```python
import functools
import math

import jax
import jax.numpy as jnp
import numpy as np
from jax import lax
from jax.experimental import pallas as pl
from jax.experimental.pallas import tpu as pltpu
from jax.sharding import PartitionSpec as P

HEAD_SIZE = 128
LOWEST = -1e30
FAR = 1 << 16
MIB = 1 << 20
SCORE_SCALE = math.log2(math.e) / math.sqrt(HEAD_SIZE)
BF16, F32 = jnp.bfloat16, jnp.float32


def distance(rank, step, count):
    return jnp.where(rank >= step, step, count - step)


def waits_for_keys(rank):
    return (rank == 1) | (rank == 2)


def first_begin(rank, half):
    return pl.multiple_of(jnp.where(rank < 2, 0, half), half)


def half_positions(p_ref, rank, first):
    half = p_ref.shape[1] // 2
    early = (rank < 2) if first else (rank >= 2)
    return jnp.where(early, p_ref[:, :half], p_ref[:, half:])


def column(row, width):
    return jnp.broadcast_to(row, (width, row.shape[1])).T


def tile_biases(position_row, kinds):
    number = position_row.shape[1]
    position = column(position_row, number)
    query = lax.broadcasted_iota(jnp.int32, (number, number), 0)
    key = lax.broadcasted_iota(jnp.int32, (number, number), 1)
    ahead = key - query
    reach = ahead + position
    found = []
    for pieces, diagonal in kinds:
        allowed = reach >= pieces * number
        if diagonal:
            allowed = allowed & (ahead <= 0)
        found.append(jnp.where(allowed, 0.0, LOWEST).astype(F32))
    return found


def sine_cosine(angle):
    turns = jnp.floor(angle * (2.0 / math.pi) + 0.5)
    rest = ((angle - turns * 1.5703125) - turns * 4.837512969970703e-4) - turns * 7.549789954891888e-8
    square = rest * rest
    sine = ((-1.9515295891e-4 * square + 8.3321608736e-3) * square - 1.6666654611e-1) * square * rest + rest
    cosine = (
        ((2.443315711809948e-5 * square - 1.388731625493765e-3) * square + 4.166664568298827e-2) * square * square
        - 0.5 * square
        + 1.0
    )
    quarter = turns.astype(jnp.int32)
    swap = (quarter & 1) == 1
    out_sine = jnp.where(swap, cosine, sine)
    out_cosine = jnp.where(swap, sine, cosine)
    out_sine = jnp.where((quarter & 2) == 2, -out_sine, out_sine)
    out_cosine = jnp.where(((quarter + 1) & 2) == 2, -out_cosine, out_cosine)
    return out_sine, out_cosine


def turned(block, cosine, sinus):
    wide = block.astype(F32)
    return (wide * cosine + pltpu.roll(wide, HEAD_SIZE // 2, 1) * sinus).astype(BF16)


def scores_of(query, key, bias):
    raw = lax.dot_general(query, key, (((1,), (1,)), ((), ())), preferred_element_type=F32)
    return raw * SCORE_SCALE + bias


def weighted(weights, value):
    return jnp.dot(weights.astype(BF16), value, preferred_element_type=F32)


def spread(entries):
    return jnp.broadcast_to(entries, (entries.shape[0], HEAD_SIZE))


def with_ones(value):
    return jnp.concatenate([value, jnp.ones_like(value)], axis=1)


def head_slices(head, group, width):
    at = slice(head * HEAD_SIZE, (head + 1) * HEAD_SIZE)
    low = head // group * HEAD_SIZE
    return at, slice(low, low + HEAD_SIZE), slice(width + low, width + low + HEAD_SIZE)


def begin_state(query, keys, values, biases):
    scores = [scores_of(query, key, bias) for key, bias in zip(keys, biases)]
    top = jnp.max(functools.reduce(jnp.maximum, scores), axis=1, keepdims=True)
    weights = [jnp.exp2(score - top) for score in scores]
    both = functools.reduce(jnp.add, [weighted(w, value) for w, value in zip(weights, values)])
    return both[:, :HEAD_SIZE], spread(top), both[:, HEAD_SIZE:]


def added_tile(summed, top, total, query, key, value, bias):
    score = scores_of(query, key, bias)
    updated = jnp.maximum(top, spread(jnp.max(score, axis=1, keepdims=True)))
    weights = jnp.exp2(score - jnp.concatenate([updated] * (score.shape[1] // HEAD_SIZE), axis=1))
    factor = jnp.exp2(top - updated)
    both = weighted(weights, value)
    return summed * factor + both[:, :HEAD_SIZE], updated, total * factor + both[:, HEAD_SIZE:]


def finished(state):
    summed, _, total = state
    return (summed * (1.0 / total)).astype(BF16)


def keys_kernel(
    count, k_hbm, v_hbm, q_hbm, p_hbm, f_hbm, near_ref, next_ref, rot_ref, v_ref, q_ref, p_ref, cos_ref, sin_ref,
    k_ref, f_ref, sems,
):
    pairs = ((p_hbm, p_ref), (f_hbm, f_ref), (k_hbm, k_ref), (v_hbm, v_ref), (q_hbm, q_ref))
    copies = [pltpu.make_async_copy(source, target, sems.at[i]) for i, (source, target) in enumerate(pairs)]
    for copy in copies:
        copy.start()
    rank = lax.axis_index("ctx")
    half = k_ref.shape[0] // 2
    width = k_ref.shape[1]
    copies[0].wait()
    copies[1].wait()
    position = p_ref[...].astype(F32)
    early = column(position[:, :half], HEAD_SIZE)
    late = column(position[:, half:], HEAD_SIZE)
    lane = lax.broadcasted_iota(jnp.int32, (half, HEAD_SIZE), 1)
    front = lane < HEAD_SIZE // 2
    sine, cosine = sine_cosine(jnp.where(front, early, late) * f_ref[...])
    sine_other = pltpu.roll(sine, HEAD_SIZE // 2, 1)
    cosine_other = pltpu.roll(cosine, HEAD_SIZE // 2, 1)
    cos_ref[:half] = jnp.where(front, cosine, cosine_other)
    cos_ref[half:] = jnp.where(front, cosine_other, cosine)
    sin_ref[:half] = jnp.where(front, -sine, sine_other)
    sin_ref[half:] = jnp.where(front, -sine_other, sine)
    copies[2].wait()
    for head in range(width // HEAD_SIZE):
        at = slice(head * HEAD_SIZE, (head + 1) * HEAD_SIZE)
        rot_ref[:, at] = turned(k_ref[:, at], cos_ref[...], sin_ref[...])
    copies[3].wait()
    wrap = (rank % 2 == 1) & (rank + 3 >= count)
    rows = pl.ds(pl.multiple_of(jnp.where(wrap, half, 0), half), half)
    near_ref[:, :width] = rot_ref[rows, :]
    near_ref[:, width:] = v_ref[rows, :]
    rows = pl.ds(pl.multiple_of(jnp.where(rank + 2 >= count, half, 0), half), half)
    next_ref[:, :width] = rot_ref[rows, :]
    next_ref[:, width:] = v_ref[rows, :]
    copies[4].wait()


def pack_kernel(q_ref, k_ref, v_ref, cos_ref, sin_ref, out_ref):
    rank = lax.axis_index("ctx")
    half, width = out_ref.shape[0], k_ref.shape[1]
    rows = pl.ds(first_begin(rank, half), half)
    begin, late = out_ref.shape[1] - 2 * HEAD_SIZE, slice(width - HEAD_SIZE, width)
    out_ref[:, begin : begin + HEAD_SIZE] = k_ref[rows, late]
    out_ref[:, begin + HEAD_SIZE :] = v_ref[rows, late]
    low = q_ref.shape[1] - begin
    for head in range(begin // HEAD_SIZE):
        at = slice(head * HEAD_SIZE, (head + 1) * HEAD_SIZE)
        source = slice(low + head * HEAD_SIZE, low + (head + 1) * HEAD_SIZE)
        out_ref[:, at] = turned(q_ref[rows, source], cos_ref[rows, :], sin_ref[rows, :])


def own_kernel(group, q_ref, k_ref, v_ref, p_ref, cos_ref, sin_ref, out_ref, rot_ref, acc_ref, top_ref, sum_ref):
    rank = lax.axis_index("ctx")
    half = q_ref.shape[0] // 2
    rows = pl.ds(first_begin(rank, half), half)
    biases = tile_biases(half_positions(p_ref, rank, True), [(0, True)])
    for head in range(rot_ref.shape[1] // HEAD_SIZE):
        at, shared, _ = head_slices(head, group, 0)
        query = turned(q_ref[rows, at], cos_ref[rows, :], sin_ref[rows, :])
        rot_ref[:, at] = query
        if head % group == 0:
            key = k_ref[rows, shared]
            value = with_ones(v_ref[rows, shared])
        for low, high in ((0, half // 2), (half // 2, half)):
            part = slice(low, high)
            summed, top, total = begin_state(query[part], [key[:high]], [value[:high]], [biases[0][part, :high]])
            acc_ref[part, at] = summed
            top_ref[part, at] = top
            sum_ref[part, at] = total
            out_ref[part, at] = (summed * (1.0 / total)).astype(BF16)


def first_kernel(count, group, own_ref, rot_ref, kv_ref, p_ref, acc_ref, top_ref, sum_ref, out_ref):
    rank = lax.axis_index("ctx")
    width = kv_ref.shape[1] // 2
    depth = rot_ref.shape[1]
    step = jnp.where(rank % 2 == 1, 1, 3)
    used = waits_for_keys(rank)
    @pl.when(used)
    def _():
        biases = tile_biases(half_positions(p_ref, rank, True), [(distance(rank, step, count), False)])
        for head in range(depth // HEAD_SIZE):
            at, key_at, value_at = head_slices(head, group, width)
            state = acc_ref[:, at], top_ref[:, at], sum_ref[:, at]
            if head % group == 0:
                value = with_ones(kv_ref[:, value_at])
            out_ref[:, at] = finished(added_tile(*state, rot_ref[:, at], kv_ref[:, key_at], value, *biases))

    @pl.when(jnp.logical_not(used))
    def _():
        out_ref[...] = own_ref[...]


def early_kernel(count, early_ref, near_ref, p_ref, out_ref):
    rank = lax.axis_index("ctx")
    depth = out_ref.shape[1]
    width = near_ref.shape[1] // 2
    step = jnp.where(rank % 2 == 1, 1, 3)
    reach = jnp.where(waits_for_keys(rank), distance(rank, step, count), FAR)
    biases = tile_biases(half_positions(p_ref, rank, True), [(0, True), (reach, False)])
    keys = [early_ref[:, depth : depth + HEAD_SIZE], near_ref[:, width - HEAD_SIZE : width]]
    values = [with_ones(early_ref[:, depth + HEAD_SIZE :]), with_ones(near_ref[:, 2 * width - HEAD_SIZE :])]
    for head in range(depth // HEAD_SIZE):
        at = slice(head * HEAD_SIZE, (head + 1) * HEAD_SIZE)
        out_ref[:, at] = finished(begin_state(early_ref[:, at], keys, values, biases))


def second_kernel(
    count, group, q_ref, k_ref, v_ref, p_ref, cos_ref, sin_ref, kv_ref, w_hbm, rot_ref, acc_ref, top_ref, sum_ref, w_ref, sem
):
    copy = pltpu.make_async_copy(w_hbm, w_ref, sem)
    copy.start()
    rank = lax.axis_index("ctx")
    half = q_ref.shape[0] // 2
    width = k_ref.shape[1]
    rows = pl.ds(pl.multiple_of(half - first_begin(rank, half), half), half)
    step = jnp.where(rank % 2 == 1, 1, 3)
    reach = jnp.where(waits_for_keys(rank), FAR, distance(rank, step, count))
    biases = tile_biases(half_positions(p_ref, rank, False), [(0, True), (reach, False)])
    for head in range(q_ref.shape[1] // HEAD_SIZE):
        at, key_at, value_at = head_slices(head, group, width)
        query = turned(q_ref[rows, at], cos_ref[rows, :], sin_ref[rows, :])
        rot_ref[:, at] = query
        keys = [k_ref[rows, key_at], kv_ref[:, key_at]]
        if head % group == 0:
            values = [with_ones(v_ref[rows, key_at]), with_ones(kv_ref[:, value_at])]
        acc_ref[:, at], top_ref[:, at], sum_ref[:, at] = begin_state(query, keys, values, biases)
    copy.wait()


def next_kernel(count, group, heads, rot_ref, kv_ref, p_ref, acc_ref, top_ref, sum_ref, *outs):
    rank = lax.axis_index("ctx")
    width = kv_ref.shape[1] // 2
    biases = tile_biases(half_positions(p_ref, rank, False), [(distance(rank, 2, count), False)])
    for number, head in enumerate(heads):
        at, key_at, value_at = head_slices(head, group, width)
        state = acc_ref[:, at], top_ref[:, at], sum_ref[:, at]
        if number == 0 or head % group == 0:
            value = with_ones(kv_ref[:, value_at])
        state = added_tile(*state, rot_ref[:, at], kv_ref[:, key_at], value, *biases)
        for out_ref, entries in zip(outs, state):
            out_ref[:, number * HEAD_SIZE : (number + 1) * HEAD_SIZE] = entries


def third_kernel(count, group, heads, base, rot_ref, kv_ref, p_ref, acc_ref, top_ref, sum_ref, out_ref):
    rank = lax.axis_index("ctx")
    width = kv_ref.shape[1] // 2
    step = jnp.where(rank % 2 == 1, 3, 1)
    biases = tile_biases(half_positions(p_ref, rank, False), [(distance(rank, step, count), False)])
    for number, head in enumerate(heads):
        at, key_at, value_at = head_slices(head, group, width)
        held = slice((head - base) * HEAD_SIZE, (head - base + 1) * HEAD_SIZE)
        state = acc_ref[:, held], top_ref[:, held], sum_ref[:, held]
        if number == 0 or head % group == 0:
            value = with_ones(kv_ref[:, value_at])
        state = added_tile(*state, rot_ref[:, at], kv_ref[:, key_at], value, *biases)
        out_ref[:, number * HEAD_SIZE : (number + 1) * HEAD_SIZE] = finished(state)


def dot(left, right):
    return jnp.dot(left, right, preferred_element_type=F32)


TILE = 512
LAST_TILE = 256


def other_rows(w_ref, begin, end):
    depth = w_ref.shape[0] // 2
    base = (1 - lax.axis_index("head")) * depth
    return pl.ds(pl.multiple_of(base + begin, HEAD_SIZE), end - begin)


def project_kernel(first_ref, last_ref, second0_ref, second1_ref, second2_ref, w_ref, sum_ref, part_ref):
    half, depth = first_ref.shape[0], w_ref.shape[0] // 2
    mine = pl.ds(pl.multiple_of(lax.axis_index("head") * depth, depth), depth)
    first = jnp.concatenate([first_ref[...], last_ref[...]], axis=1)
    second = jnp.concatenate([second0_ref[...], second1_ref[...], second2_ref[...]], axis=1)
    stacked = jnp.concatenate([first, second], axis=0)
    for tile in range(w_ref.shape[1] // TILE):
        at = slice(tile * TILE, (tile + 1) * TILE)
        both = dot(stacked, w_ref[mine, at])
        sum_ref[:, at] = both[:half]
        part_ref[:, at] = both[half:]


def first_out_kernel(got_ref, got_last_ref, sum_ref, w_ref, out_hbm, held_ref, sems):
    rank = lax.axis_index("ctx")
    half, depth = got_ref.shape[0], w_ref.shape[0] // 2
    rows = pl.ds(first_begin(rank, half), half)
    other = other_rows(w_ref, 0, depth)
    got = jnp.concatenate([got_ref[...], got_last_ref[...]], axis=1)
    copies = []
    for tile in range(w_ref.shape[1] // TILE):
        at = slice(tile * TILE, (tile + 1) * TILE)
        held_ref[:, at] = (sum_ref[:, at] + dot(got, w_ref[other, at])).astype(BF16)
        copies.append(pltpu.make_async_copy(held_ref.at[:, at], out_hbm.at[rows, at], sems.at[tile]))
        copies[-1].start()
    for copy in copies:
        copy.wait()


def add_kernel(begin, got_ref, part_ref, w_ref, out_ref):
    rows = other_rows(w_ref, begin, begin + got_ref.shape[1])
    for start in range(0, w_ref.shape[1], TILE):
        at = slice(start, start + TILE)
        out_ref[:, at] = part_ref[:, at] + dot(got_ref[...], w_ref[rows, at])


def last_kernel(begin, got_ref, part_ref, w_ref, begun_hbm, out_hbm, held_ref, sems):
    del begun_hbm
    rank = lax.axis_index("ctx")
    half, depth = got_ref.shape
    out_rows = pl.ds(pl.multiple_of(half - first_begin(rank, half), half), half)
    rows = other_rows(w_ref, begin, begin + depth)
    copies = []
    for tile in range(w_ref.shape[1] // LAST_TILE):
        at = slice(tile * LAST_TILE, (tile + 1) * LAST_TILE)
        added = dot(got_ref[...], w_ref[rows, at])
        held_ref[:, at] = (part_ref[:, at] + added).astype(BF16)
        copies.append(pltpu.make_async_copy(held_ref.at[:, at], out_hbm.at[out_rows, at], sems.at[tile]))
        copies[-1].start()
    for copy in copies:
        copy.wait()


def shards(queries, keys, values, positions, out_weight):
    number, width = queries.shape
    half = number // 2
    count = lax.axis_size("ctx")
    group = width // keys.shape[1]
    columns = out_weight.shape[1]
    tiles = columns // TILE
    in_hbm = lambda array: pltpu.with_memory_space_constraint(array, pltpu.HBM)
    position_row = positions.reshape(1, number)
    table = np.power(500000.0, -2.0 * np.arange(HEAD_SIZE // 2) / HEAD_SIZE).astype(np.float32)
    frequency = jnp.asarray(np.concatenate([table, table])[None, :])
    shape = jax.ShapeDtypeStruct
    vmem = pl.BlockSpec(memory_space=pltpu.VMEM)
    hbm = pl.BlockSpec(memory_space=pltpu.HBM)
    dma = pltpu.SemaphoreType.DMA

    def call(body, name, ins, outs, flops, nbytes, out_specs=None, scratch=(), aliases={}):
        return pl.pallas_call(
            body,
            name=name,
            in_specs=ins,
            out_shape=outs,
            out_specs=out_specs if out_specs is not None else jax.tree.map(lambda _: vmem, outs),
            scratch_shapes=scratch,
            input_output_aliases=aliases,
            compiler_params=pltpu.CompilerParams(vmem_limit_bytes=32 * MIB),
            cost_estimate=pl.CostEstimate(flops=flops, bytes_accessed=nbytes, transcendentals=0),
        )

    def pairs(target_of):
        found = [(source, target_of(source) % count) for source in range(count)]
        assert sorted(target for _, target in found) == list(range(count))
        return found

    def swapped(array):
        return lax.ppermute(array, "head", [(0, 1), (1, 0)])

    kv_shape = shape((half, 2 * keys.shape[1]), BF16)
    table_shape = shape((number, HEAD_SIZE), F32)
    rows_shape, state = shape((half, width), BF16), shape((half, width), F32)
    heads = width // HEAD_SIZE
    moved = group - 1
    cut = heads - moved
    some_shape = shape((half, cut * HEAD_SIZE), BF16)
    some_state = shape((half, cut * HEAD_SIZE), F32)
    last_shape = shape((half, moved * HEAD_SIZE), BF16)
    near, onward, k_rot, v, q, p, cosine, sinus = call(
        functools.partial(keys_kernel, count),
        "rotate_keys",
        [hbm] * 5,
        [kv_shape, kv_shape]
        + [shape(keys.shape, BF16)] * 2
        + [shape(queries.shape, BF16), shape((1, number), jnp.int32), table_shape, table_shape],
        4 * MIB,
        4 * MIB,
        scratch=[pltpu.VMEM(keys.shape, BF16), pltpu.VMEM((1, HEAD_SIZE), F32), dma((5,))],
    )(*(in_hbm(array) for array in (keys, values, queries, position_row, frequency)))
    near_pairs = pairs(lambda r: r + 3 if r % 2 else r + 1)
    near_got = lax.ppermute(near, "ctx", near_pairs)
    early = call(pack_kernel, "pack_early", [vmem] * 5, shape((half, (moved + 2) * HEAD_SIZE), BF16), MIB, MIB)(
        q, k_rot, v, cosine, sinus
    )
    early, q = lax.optimization_barrier((early, q))
    early_got = swapped(early)
    own, rot, acc, top, total = call(
        functools.partial(own_kernel, group),
        "own_tiles",
        [vmem] * 6,
        [some_shape, some_shape, some_state, some_state, some_state],
        256 * MIB,
        4 * MIB,
    )(q, k_rot, v, p, cosine, sinus)
    onward, rot = lax.optimization_barrier((onward, rot))
    next_got = lax.ppermute(onward, "ctx", pairs(lambda r: r + 2))
    first = call(
        functools.partial(first_kernel, count, group),
        "first_rows",
        [vmem] * 7,
        some_shape,
        256 * MIB,
        4 * MIB,
    )(own, rot, near_got, p, acc, top, total)
    first_got = swapped(first)
    q, first = lax.optimization_barrier((q, first))
    rot, *state_now, w = call(
        functools.partial(second_kernel, count, group),
        "second_rows",
        [vmem] * 7 + [hbm],
        [rows_shape, state, state, state, shape(out_weight.shape, BF16)],
        1024 * MIB,
        12 * MIB,
        scratch=[dma(())],
    )(q, k_rot, v, p, cosine, sinus, near_got, in_hbm(out_weight))
    rot, early_got = lax.optimization_barrier((rot, early_got))
    other_near = lax.ppermute(early_got[:, moved * HEAD_SIZE :], "ctx", near_pairs)
    rot, next_got = lax.optimization_barrier((rot, next_got))
    last_got = lax.ppermute(next_got, "ctx", pairs(lambda r: r + 1 - 2 * (r % 2)))
    def with_next_tile(part, rot):
        held = shape((half, len(part) * HEAD_SIZE), F32)
        return call(
            functools.partial(next_kernel, count, group, part), "next_tile", [vmem] * 6, [held] * 3, 512 * MIB, 4 * MIB
        )(rot, next_got, p, *state_now)

    begin = heads // 2 - 1
    parts = range(begin), range(begin, heads - 1), range(heads - 1, heads)
    seconds, seconds_got = [], []
    for part in parts:
        if len(seconds) < 2:
            base = part[0]
            held_state = with_next_tile(range(base, begin if base == 0 else heads), rot)
        second = call(
            functools.partial(third_kernel, count, group, part, base),
            "last_tile",
            [vmem] * 6,
            shape((half, len(part) * HEAD_SIZE), BF16),
            256 * MIB,
            4 * MIB,
        )(rot, last_got, p, *held_state)
        seconds_got.append(swapped(second))
        if len(seconds) == 0:
            rot, second, first_got = lax.optimization_barrier((rot, second, first_got))
        else:
            rot, second, other_near, early = lax.optimization_barrier((rot, second, other_near, early))
        seconds.append(second)
    attend_early = call(
        functools.partial(early_kernel, count), "early_rows", [vmem] * 3, last_shape, 256 * MIB, 4 * MIB
    )
    last = attend_early(early, near_got, p)
    sum_shape = shape((half, columns), F32)
    first_sum, partial_sum = call(
        project_kernel, "project_own", [vmem] * 6, [sum_shape, sum_shape], 2048 * MIB, 8 * MIB
    )(first, last, *seconds, w)
    early_got, partial_sum, first_sum = lax.optimization_barrier((early_got, partial_sum, first_sum))
    got_last = attend_early(early_got, other_near, p)
    begun = call(
        first_out_kernel,
        "project_first",
        [vmem] * 4,
        shape((number, columns), BF16),
        1024 * MIB,
        8 * MIB,
        out_specs=hbm,
        scratch=[pltpu.VMEM((half, columns), BF16), dma((tiles,))],
    )(first_got, got_last, first_sum, w)
    begun, partial_sum = lax.optimization_barrier((begun, partial_sum))
    for part, got in zip(parts[:-1], seconds_got):
        partial_sum = call(
            functools.partial(add_kernel, part[0] * HEAD_SIZE),
            "project_second",
            [vmem] * 3,
            sum_shape,
            512 * MIB,
            4 * MIB,
        )(got, partial_sum, w)
    return call(
        functools.partial(last_kernel, parts[-1][0] * HEAD_SIZE),
        "project_last",
        [vmem] * 3 + [hbm],
        shape((number, columns), BF16),
        512 * MIB,
        4 * MIB,
        out_specs=hbm,
        scratch=[pltpu.VMEM((half, columns), BF16), dma((columns // LAST_TILE,))],
        aliases={3: 0},
    )(seconds_got[-1], partial_sum, w, begun)


def solution(mesh):
    in_specs = (P("ctx", "head"), P("ctx", "head"), P("ctx", "head"), P("ctx"), P(None, "head"))
    out_specs = P("ctx", "head")
    return jax.shard_map(shards, mesh=mesh, in_specs=in_specs, out_specs=out_specs, check_vma=False)
```
